32 devices in a mesh: seq: 4 (over y, x), head: 8 (over z, core).
Axes of the slice: x: 2, y: 2, z: 4, core: 2. Of those that a mesh axis runs over, the one named last changes fastest.
Arguments:
- queries: bfloat16 [6144, 4096], P(('seq', 'head')), may hold values from -48 to 48
- keys: bfloat16 [6144, 2048], P(('seq', 'head')), may hold values from -4 to 4
- values: bfloat16 [6144, 2048], P(('seq', 'head')), may hold values from -6 to 6
- grad_out: bfloat16 [6144, 4096], P(('seq', 'head')), may hold values from -6 to 6
- doc_lengths: int32 [16], replicated, may hold values from 1 to 1536, 6144 in all
Outputs:
- grad_queries: bfloat16 [6144, 4096], P(('seq', 'head'))
- grad_keys: bfloat16 [6144, 2048], P(('seq', 'head'))
- grad_values: bfloat16 [6144, 2048], P(('seq', 'head'))
The draws below stay inside these ranges and needn't reach their ends.
Inputs may be any that keep to these rules, and one draw needn't show every extreme that they name: `doc_lengths`: the lengths sum to 6144.
All inputs are finite; a program needn't handle non-finite values.
Results may differ from the reference program's by a relative error of at most 0.012.
Values may be sent and summed in bfloat16 or wider, within the bound.
No kernel may reach another device: no remote copies, remote signals or barrier semaphores. Data moves between devices by JAX's collectives and lax.ppermute only.
A program may use at most 128 MiB of HBM per device.

```python
import math
import jax
import jax.numpy as jnp
import numpy as np
from jax import lax

HEADS = 32
KV_HEADS = 16
HD = 128
WINDOW = 1024
QBLK = 512
DOCS = 16
TOKENS = 6144
DOC_MOST = 1536


def query_key_pair(key):
    key_query, key_keys = jax.random.split(jax.random.fold_in(key, 11), 2)
    q_shape = (TOKENS, HEADS, HD)
    k_shape = (TOKENS, KV_HEADS, HD)
    query_out = jax.random.truncated_normal(key_query, -4.0, 4.0, q_shape, jnp.float32)
    keys_out = jax.random.truncated_normal(key_keys, -4.0, 4.0, k_shape, jnp.float32)
    return (query_out.reshape(TOKENS, HEADS * HD), keys_out.reshape(TOKENS, KV_HEADS * HD))


def draw_queries(key, part):
    return query_key_pair(key)[0].astype(jnp.bfloat16)


def draw_keys(key, part):
    return query_key_pair(key)[1].astype(jnp.bfloat16)


def block_levels(stream_key, dims, cuts, smallest, high):
    def one(dim, blocks):
        heights = jax.random.uniform(jax.random.fold_in(jax.random.fold_in(stream_key, 6), dim), (blocks,), jnp.float32, smallest / len(cuts), high / len(cuts))
        return jnp.repeat(jnp.exp(heights), dims[dim] // blocks).reshape((-1,) + (1,) * (len(dims) - dim - 1))

    gain = one(*cuts[0])
    for cut in cuts[1:]:
        gain = gain * one(*cut)
    return gain


def split_up(count, total, reach, lean):
    weights = [(1 << 20) // math.isqrt(rank ** lean) + 1 for rank in range(2, count + 1)]
    rest, given = total - reach - (count - 1), [1] * (count - 1)
    while rest > 0:
        candidates = [i for i in range(count - 1) if given[i] < reach]
        pool, budget = sum([weights[i] for i in candidates]), rest
        for i in candidates:
            addition = min(reach - given[i], max(1, budget * weights[i] // pool), rest)
            given[i] = given[i] + addition
            rest = rest - addition
    return np.array([reach] + given)


def ragged(rng, amount, total, limit, slope):
    if amount == 2:
        one = jax.random.randint(rng, (), max(1, total - limit), min(limit, total - 1) + 1)
        return jnp.stack([one, total - one])
    sizes = jnp.asarray(split_up(amount, total, limit, slope), jnp.int32)
    twos = (amount - 1) // 2
    source_of, sink = sizes[1:1 + 2 * twos:2], sizes[2:2 + 2 * twos:2]
    slack = jnp.minimum(source_of - 1, limit - sink)
    passed = jax.random.randint(jax.random.fold_in(rng, 1), (twos,), 0, 1 << 20) % (slack + 1)
    sizes = sizes.at[1:1 + 2 * twos:2].set(source_of - passed).at[2:2 + 2 * twos:2].set(sink + passed)
    return sizes[jax.random.permutation(jax.random.fold_in(rng, 2), amount)]


def bell_draw(rng, shape, scale, reach, shards=(), kind=jnp.bfloat16):
    gain = block_levels(rng, shape, shards, -0.22, 0.18) if shards else 1.0
    drawn = jax.random.normal(rng, shape, jnp.float32) * scale * gain
    return jnp.minimum(jnp.maximum(drawn, -reach), reach).astype(kind)


def setup_inputs(seed: int = 0) -> dict:
    splits = jax.random.split(jax.random.key(seed), 6)
    queries = draw_queries(jax.random.fold_in(splits[5], 71), 0)
    keys = draw_keys(jax.random.fold_in(splits[5], 71), 0)
    values = bell_draw(splits[2], (TOKENS, KV_HEADS * HD), 1.0, 6.0, ((0, 32),))
    grad_out = bell_draw(splits[3], (TOKENS, HEADS * HD), 1.0, 6.0, ((0, 32),))
    doc_lengths = ragged(splits[4], DOCS, TOKENS, DOC_MOST, 1).astype(jnp.int32)
    return dict(queries=queries, keys=keys, values=values, grad_out=grad_out, doc_lengths=doc_lengths)


def doc_index(doc_lengths, positions):
    doc_ends = jnp.cumsum(doc_lengths).astype(jnp.int32)
    return jnp.sum((positions[:, None] >= doc_ends[None, :]).astype(jnp.int32), axis=1)


def tile_grads(q_rows, out_rows, key_rows, value_rows, allowed):
    scaling = HD ** -0.5
    row_count = q_rows.shape[0]
    kv_count = key_rows.shape[1]
    per_group = q_rows.shape[1] // kv_count
    q_four = q_rows.reshape(row_count, kv_count, per_group, HD).astype(jnp.float32)
    out_four = out_rows.reshape(row_count, kv_count, per_group, HD).astype(jnp.float32)
    key_float = key_rows.astype(jnp.float32)
    value_float = value_rows.astype(jnp.float32)
    scores = jnp.einsum("qagd,kad->agqk", q_four, key_float) * scaling
    scores = jnp.where(allowed[None, None], scores, -jnp.inf)
    row_max = jnp.max(scores, axis=3, keepdims=True)
    exponent = jnp.exp(scores - row_max)
    weights = exponent / jnp.sum(exponent, axis=3, keepdims=True)
    weights_b = weights.astype(jnp.bfloat16)
    grad_values = jnp.einsum("agqk,qagd->kad", weights_b.astype(jnp.float32), out_four)
    grad_weights = jnp.einsum("qagd,kad->agqk", out_four, value_float)
    row_dot = jnp.sum(weights * grad_weights, axis=3, keepdims=True)
    grad_scores = (weights * (grad_weights - row_dot) * scaling).astype(jnp.bfloat16)
    grad_query = jnp.einsum("agqk,kad->qagd", grad_scores.astype(jnp.float32), key_float)
    grad_keys = jnp.einsum("agqk,qagd->kad", grad_scores.astype(jnp.float32), q_four)
    return grad_query.reshape(row_count, kv_count * per_group, HD), grad_keys, grad_values


def reference(queries, keys, values, grad_out, doc_lengths):
    q_all = queries.reshape(TOKENS, HEADS, HD)
    out_all = grad_out.reshape(TOKENS, HEADS, HD)
    pad_rows = jnp.zeros((WINDOW, KV_HEADS, HD), jnp.bfloat16)
    key_ext = jnp.concatenate([pad_rows, keys.reshape(TOKENS, KV_HEADS, HD)], axis=0)
    value_ext = jnp.concatenate([pad_rows, values.reshape(TOKENS, KV_HEADS, HD)], axis=0)
    q_docs = doc_index(doc_lengths, jnp.arange(TOKENS, dtype=jnp.int32))
    k_docs = doc_index(doc_lengths, jnp.arange(TOKENS + WINDOW, dtype=jnp.int32) - WINDOW)
    span = QBLK + WINDOW
    q_iota = jnp.arange(QBLK, dtype=jnp.int32)
    k_iota = jnp.arange(span, dtype=jnp.int32)

    def advance(totals, block):
        key_total, value_total = totals
        first_row = (block * QBLK).astype(jnp.int32)
        q_rows = lax.dynamic_slice_in_dim(q_all, first_row, QBLK, 0)
        out_rows = lax.dynamic_slice_in_dim(out_all, first_row, QBLK, 0)
        key_rows = lax.dynamic_slice_in_dim(key_ext, first_row, span, 0)
        value_rows = lax.dynamic_slice_in_dim(value_ext, first_row, span, 0)
        q_pos = first_row + q_iota
        k_pos = first_row - WINDOW + k_iota
        q_doc = lax.dynamic_slice_in_dim(q_docs, first_row, QBLK, 0)
        k_doc = lax.dynamic_slice_in_dim(k_docs, first_row, span, 0)
        allowed = (q_doc[:, None] == k_doc[None, :]) & (k_pos[None, :] <= q_pos[:, None])
        allowed = allowed & (q_pos[:, None] - k_pos[None, :] < WINDOW) & (k_pos[None, :] >= 0)
        grad_query, grad_keys, grad_values = tile_grads(q_rows, out_rows, key_rows, value_rows, allowed)
        key_total = lax.dynamic_update_slice_in_dim(key_total, lax.dynamic_slice_in_dim(key_total, first_row, span, 0) + grad_keys, first_row, 0)
        value_total = lax.dynamic_update_slice_in_dim(value_total, lax.dynamic_slice_in_dim(value_total, first_row, span, 0) + grad_values, first_row, 0)
        return (key_total, value_total), grad_query

    zeros_ext = jnp.zeros((TOKENS + WINDOW, KV_HEADS, HD), jnp.float32)
    totals, grad_query = lax.scan(advance, (zeros_ext, zeros_ext), jnp.arange(TOKENS // QBLK, dtype=jnp.int32))
    grad_queries = grad_query.reshape(TOKENS, HEADS * HD).astype(jnp.bfloat16)
    grad_keys = totals[0][WINDOW:].reshape(TOKENS, KV_HEADS * HD).astype(jnp.bfloat16)
    grad_values = totals[1][WINDOW:].reshape(TOKENS, KV_HEADS * HD).astype(jnp.bfloat16)
    return grad_queries, grad_keys, grad_values
```

```python
import functools
import math

import jax
import jax.numpy as jnp
from jax import lax
from jax.experimental import pallas as pl
from jax.experimental.pallas import tpu as pltpu
from jax.sharding import PartitionSpec as P

HD = 128
WINDOW = 1024
TQ = 256
TK = 256
SCALING = HD ** (-0.5)
EXP2_SCALE = SCALING * math.log2(math.e)
MASKED = -1e30


def passed_along(shard, axis, by):
    count = lax.axis_size(axis)
    pairs = [(i, i + by) for i in range(count) if 0 <= i + by < count]
    return lax.ppermute(shard, axis, pairs)


def dot_nt(a, b):
    return lax.dot_general(a, b, (((1,), (1,)), ((), ())), preferred_element_type=jnp.float32)


def dot_nn(a, b):
    return lax.dot_general(a, b, (((1,), (0,)), ((), ())), preferred_element_type=jnp.float32)


def attend_kernel(
    per_group, first_tile, low_ref, qd_ref, halo_k, halo_v, own_k, own_v,
    dq_ref, own_ref, rim_ref,
    k_ext, v_ext, k_t, dk_ext, dv_ext, s_buf, dp_buf,
):
    group = qd_ref.shape[0]
    reach = WINDOW // TK
    k_ext[:WINDOW, :] = halo_k[...]
    k_ext[WINDOW:, :] = own_k[...]
    v_ext[:WINDOW, :] = halo_v[...]
    v_ext[WINDOW:, :] = own_v[...]
    dk_ext[...] = jnp.zeros_like(dk_ext)
    dv_ext[...] = jnp.zeros_like(dv_ext)

    def turn(t, carry):
        rows = pl.ds(pl.multiple_of(t * TK, TK), TK)
        k_t[t] = jnp.transpose(k_ext[rows, :].astype(jnp.float32)).astype(jnp.bfloat16)
        return carry

    lax.fori_loop(0, (group + WINDOW) // TK, turn, 0)
    wide = per_group * TQ
    key_iota = lax.broadcasted_iota(jnp.int32, (TK, wide), 0)

    def q_block(b, carry):
        q_rows = pl.ds(pl.multiple_of(b * TQ, TQ), TQ)
        start = first_tile[b]
        stop = b * (TQ // TK) + (TQ // TK - 1) + reach + 1
        q = jnp.concatenate(
            [qd_ref[q_rows, i * HD : (i + 1) * HD] for i in range(per_group)], axis=0
        )
        d_out = jnp.concatenate(
            [qd_ref[q_rows, i * HD : (i + 1) * HD] for i in range(per_group, 2 * per_group)],
            axis=0,
        )
        low = low_ref[:, q_rows]
        low = jnp.concatenate([low] * per_group, axis=1)
        high = b * TQ + WINDOW + lax.broadcasted_iota(jnp.int32, (1, TQ), 1)
        high = jnp.concatenate([high] * per_group, axis=1)

        def score(t, top):
            rows = pl.ds(pl.multiple_of(t * TK, TK), TK)
            slot = pl.ds(pl.multiple_of((t - start) * TK, TK), TK)
            s = dot_nt(k_ext[rows, :], q)
            j = key_iota + t * TK
            s = jnp.where((j >= low) & (j <= high), s, MASKED)
            s_buf[slot, :] = s
            return jnp.maximum(top, jnp.max(s, axis=0, keepdims=True))

        top = lax.fori_loop(start, stop, score, jnp.full((1, wide), MASKED, jnp.float32))

        def weigh(t, sums):
            total, dotted = sums
            rows = pl.ds(pl.multiple_of(t * TK, TK), TK)
            slot = pl.ds(pl.multiple_of((t - start) * TK, TK), TK)
            p = jnp.exp2((s_buf[slot, :] - top) * EXP2_SCALE)
            dp = dot_nt(v_ext[rows, :], d_out)
            s_buf[slot, :] = p
            dp_buf[slot, :] = dp
            return (
                total + jnp.sum(p, axis=0, keepdims=True),
                dotted + jnp.sum(p * dp, axis=0, keepdims=True),
            )

        zero = jnp.zeros((1, wide), jnp.float32)
        total, dotted = lax.fori_loop(start, stop, weigh, (zero, zero))
        inverse = 1.0 / total
        row_dot = dotted * inverse
        inverse_scaled = inverse * SCALING

        def grads(t, dq_t):
            rows = pl.ds(pl.multiple_of(t * TK, TK), TK)
            slot = pl.ds(pl.multiple_of((t - start) * TK, TK), TK)
            p = s_buf[slot, :]
            ds = ((p * inverse_scaled) * (dp_buf[slot, :] - row_dot)).astype(jnp.bfloat16)
            weights = (p * inverse).astype(jnp.bfloat16)
            dv_ext[rows, :] += dot_nn(weights, d_out)
            dk_ext[rows, :] += dot_nn(ds, q)
            return dq_t + dot_nn(k_t[t], ds)

        dq_t = lax.fori_loop(start, stop, grads, jnp.zeros((HD, wide), jnp.float32))
        dq = jnp.transpose(dq_t).astype(jnp.bfloat16)
        for i in range(per_group):
            dq_ref[q_rows, i * HD : (i + 1) * HD] = dq[i * TQ : (i + 1) * TQ, :]
        return carry

    lax.fori_loop(0, group // TQ, q_block, 0)
    rim_ref[:, :HD] = dk_ext[:WINDOW, :].astype(jnp.bfloat16)
    rim_ref[:, HD:] = dv_ext[:WINDOW, :].astype(jnp.bfloat16)
    own_ref[:, :HD] = dk_ext[WINDOW:, :]
    own_ref[:, HD:] = dv_ext[WINDOW:, :]


def attend(qd, halo, own, chunk, kv_local, low, first_tile):
    group = qd.shape[0]
    per_group = qd.shape[1] // (2 * HD)
    ext = group + WINDOW
    wide = per_group * TQ
    span = WINDOW + TQ

    def vmem(shape, lane_block=0):
        return pl.BlockSpec(shape, lambda i: (0, lane_block))

    area = group * (WINDOW + TQ) * per_group
    return pl.pallas_call(
        functools.partial(attend_kernel, per_group),
        grid=(1,),
        out_shape=(
            jax.ShapeDtypeStruct((group, per_group * HD), jnp.bfloat16),
            jax.ShapeDtypeStruct((group, 2 * HD), jnp.float32),
            jax.ShapeDtypeStruct((WINDOW, 2 * HD), jnp.bfloat16),
        ),
        in_specs=[
            pl.BlockSpec(memory_space=pltpu.SMEM),
            vmem((1, group)),
            vmem((group, 2 * per_group * HD)),
            vmem((WINDOW, HD), chunk),
            vmem((WINDOW, HD), kv_local + chunk),
            vmem((group, HD), chunk),
            vmem((group, HD), kv_local + chunk),
        ],
        out_specs=(
            vmem((group, per_group * HD)),
            vmem((group, 2 * HD)),
            vmem((WINDOW, 2 * HD)),
        ),
        scratch_shapes=[
            pltpu.VMEM((ext, HD), jnp.bfloat16),
            pltpu.VMEM((ext, HD), jnp.bfloat16),
            pltpu.VMEM((ext // TK, HD, TK), jnp.bfloat16),
            pltpu.VMEM((ext, HD), jnp.float32),
            pltpu.VMEM((ext, HD), jnp.float32),
            pltpu.VMEM((span, wide), jnp.float32),
            pltpu.VMEM((span, wide), jnp.float32),
        ],
        compiler_params=pltpu.CompilerParams(vmem_limit_bytes=40 * 1024 * 1024),
        cost_estimate=pl.CostEstimate(
            flops=area * HD * 2 * 5, bytes_accessed=group * HD * 24, transcendentals=area
        ),
        name="attend",
    )(first_tile, low, qd, halo, halo, own, own)


def to_heads(parts):
    rows = parts[0].shape[0]
    sent = jnp.concatenate([jnp.transpose(p, (1, 0, 2)) for p in parts], axis=2)
    came = lax.all_to_all(sent, "head", split_axis=0, concat_axis=0, tiled=True)
    return came.reshape(-1, sent.shape[2])


def to_tokens(rows, ways):
    sent = rows.reshape(ways, rows.shape[0] // ways, rows.shape[1])
    return lax.all_to_all(sent, "head", split_axis=0, concat_axis=0, tiled=True)


def local(queries, keys, values, grad_out, doc_lengths):
    ways = lax.axis_size("head")
    tokens = queries.shape[0]
    group = tokens * ways
    kv_local = keys.shape[1] // (ways * HD)
    per_group = queries.shape[1] // keys.shape[1]
    group_first = lax.axis_index("seq") * group

    kv = to_heads([keys.reshape(tokens, ways, -1), values.reshape(tokens, ways, -1)])
    halo = passed_along(kv[group - WINDOW :], "seq", 1)
    q_cut = queries.reshape(tokens, ways, kv_local, per_group * HD)
    o_cut = grad_out.reshape(tokens, ways, kv_local, per_group * HD)
    qds = [to_heads([q_cut[:, :, c], o_cut[:, :, c]]) for c in range(kv_local)]

    position = group_first + jnp.arange(group, dtype=jnp.int32)
    ends = jnp.cumsum(doc_lengths)
    doc_start = jnp.sum(
        jnp.where(position[:, None] >= ends[None, :], doc_lengths[None, :], 0), axis=1
    )
    low = jnp.maximum(doc_start, position - (WINDOW - 1)) - (group_first - WINDOW)
    low = low.astype(jnp.int32)
    first_tile = low[::TQ] // TK

    grads = []
    for c in range(kv_local):
        dq, own, rim = attend(qds[c], halo, kv, c, kv_local, low.reshape(1, group), first_tile)
        returned = passed_along(rim, "seq", -1).astype(jnp.float32)
        dkv = jnp.concatenate(
            [own[: group - WINDOW], own[group - WINDOW :] + returned], axis=0
        ).astype(jnp.bfloat16)
        grads.append(to_tokens(jnp.concatenate([dq, dkv], axis=1), ways))

    def gathered(first, last):
        cut = jnp.stack([g[:, :, first:last] for g in grads], axis=2)
        return jnp.transpose(cut, (1, 0, 2, 3)).reshape(tokens, -1)

    q_end = per_group * HD
    return (
        gathered(0, q_end),
        gathered(q_end, q_end + HD),
        gathered(q_end + HD, q_end + 2 * HD),
    )


def solution(mesh):
    rows = P(("seq", "head"), None)
    return jax.shard_map(
        local,
        mesh=mesh,
        in_specs=(rows, rows, rows, rows, P()),
        out_specs=(rows, rows, rows),
        check_vma=False,
    )
```

```python
import functools
import math

import jax
import jax.numpy as jnp
from jax import lax
from jax.experimental import pallas as pl
from jax.experimental.pallas import tpu as pltpu
from jax.sharding import PartitionSpec as P

HD = 128
WINDOW = 1024
TQ = 256
TK = 256
SCALING = HD ** (-0.5)
EXP2_SCALE = SCALING * math.log2(math.e)
MASKED = -1e30


def passed_along(shard, axis, by):
    count = lax.axis_size(axis)
    pairs = [(i, i + by) for i in range(count) if 0 <= i + by < count]
    return lax.ppermute(shard, axis, pairs)


def dot_nt(a, b):
    return lax.dot_general(a, b, (((1,), (1,)), ((), ())), preferred_element_type=jnp.float32)


def dot_nn(a, b):
    return lax.dot_general(a, b, (((1,), (0,)), ((), ())), preferred_element_type=jnp.float32)


def attend_kernel(
    per_group, first_tile, low_ref, qd_ref, halo_k, halo_v, own_k, own_v,
    dq_ref, own_ref, rim_ref,
    k_ext, v_ext, k_t, dk_ext, dv_ext, s_buf, dp_buf,
):
    group = qd_ref.shape[0]
    reach = WINDOW // TK
    k_ext[:WINDOW, :] = halo_k[...]
    k_ext[WINDOW:, :] = own_k[...]
    v_ext[:WINDOW, :] = halo_v[...]
    v_ext[WINDOW:, :] = own_v[...]
    dk_ext[...] = jnp.zeros_like(dk_ext)
    dv_ext[...] = jnp.zeros_like(dv_ext)

    def turn(t, carry):
        rows = pl.ds(pl.multiple_of(t * TK, TK), TK)
        k_t[t] = jnp.transpose(k_ext[rows, :].astype(jnp.float32)).astype(jnp.bfloat16)
        return carry

    lax.fori_loop(0, (group + WINDOW) // TK, turn, 0)
    wide = per_group * TQ
    key_iota = lax.broadcasted_iota(jnp.int32, (TK, wide), 0)

    def q_block(b, carry):
        q_rows = pl.ds(pl.multiple_of(b * TQ, TQ), TQ)
        start = first_tile[b]
        stop = b * (TQ // TK) + (TQ // TK - 1) + reach + 1
        q = jnp.concatenate(
            [qd_ref[q_rows, i * HD : (i + 1) * HD] for i in range(per_group)], axis=0
        )
        d_out = jnp.concatenate(
            [qd_ref[q_rows, i * HD : (i + 1) * HD] for i in range(per_group, 2 * per_group)],
            axis=0,
        )
        low = low_ref[:, q_rows]
        low = jnp.concatenate([low] * per_group, axis=1)
        high = b * TQ + WINDOW + lax.broadcasted_iota(jnp.int32, (1, TQ), 1)
        high = jnp.concatenate([high] * per_group, axis=1)

        def score(t, top):
            rows = pl.ds(pl.multiple_of(t * TK, TK), TK)
            slot = pl.ds(pl.multiple_of((t - start) * TK, TK), TK)
            s = dot_nt(k_ext[rows, :], q)
            j = key_iota + t * TK
            s = jnp.where((j >= low) & (j <= high), s, MASKED)
            s_buf[slot, :] = s
            return jnp.maximum(top, jnp.max(s, axis=0, keepdims=True))

        top = lax.fori_loop(start, stop, score, jnp.full((1, wide), MASKED, jnp.float32))

        def weigh(t, sums):
            total, dotted = sums
            rows = pl.ds(pl.multiple_of(t * TK, TK), TK)
            slot = pl.ds(pl.multiple_of((t - start) * TK, TK), TK)
            p = jnp.exp2((s_buf[slot, :] - top) * EXP2_SCALE)
            dp = dot_nt(v_ext[rows, :], d_out)
            s_buf[slot, :] = p
            dp_buf[slot, :] = dp
            return (
                total + jnp.sum(p, axis=0, keepdims=True),
                dotted + jnp.sum(p * dp, axis=0, keepdims=True),
            )

        zero = jnp.zeros((1, wide), jnp.float32)
        total, dotted = lax.fori_loop(start, stop, weigh, (zero, zero))
        inverse = 1.0 / total
        row_dot = dotted * inverse
        inverse_scaled = inverse * SCALING

        def grads(t, dq_t):
            rows = pl.ds(pl.multiple_of(t * TK, TK), TK)
            slot = pl.ds(pl.multiple_of((t - start) * TK, TK), TK)
            p = s_buf[slot, :]
            ds = ((p * inverse_scaled) * (dp_buf[slot, :] - row_dot)).astype(jnp.bfloat16)
            weights = (p * inverse).astype(jnp.bfloat16)
            dv_ext[rows, :] += dot_nn(weights, d_out)
            dk_ext[rows, :] += dot_nn(ds, q)
            return dq_t + dot_nn(k_t[t], ds)

        dq_t = lax.fori_loop(start, stop, grads, jnp.zeros((HD, wide), jnp.float32))
        dq = jnp.transpose(dq_t).astype(jnp.bfloat16)
        for i in range(per_group):
            dq_ref[q_rows, i * HD : (i + 1) * HD] = dq[i * TQ : (i + 1) * TQ, :]
        return carry

    lax.fori_loop(0, group // TQ, q_block, 0)
    rim_ref[:, :HD] = dk_ext[:WINDOW, :].astype(jnp.bfloat16)
    rim_ref[:, HD:] = dv_ext[:WINDOW, :].astype(jnp.bfloat16)
    own_ref[:, :HD] = dk_ext[WINDOW:, :]
    own_ref[:, HD:] = dv_ext[WINDOW:, :]


def attend(qd, halo, own, chunk, kv_local, low, first_tile):
    group = qd.shape[0]
    per_group = qd.shape[1] // (2 * HD)
    ext = group + WINDOW
    wide = per_group * TQ
    span = WINDOW + TQ

    def vmem(shape, lane_block=0):
        return pl.BlockSpec(shape, lambda i: (0, lane_block))

    area = group * (WINDOW + TQ) * per_group
    return pl.pallas_call(
        functools.partial(attend_kernel, per_group),
        grid=(1,),
        out_shape=(
            jax.ShapeDtypeStruct((group, per_group * HD), jnp.bfloat16),
            jax.ShapeDtypeStruct((group, 2 * HD), jnp.float32),
            jax.ShapeDtypeStruct((WINDOW, 2 * HD), jnp.bfloat16),
        ),
        in_specs=[
            pl.BlockSpec(memory_space=pltpu.SMEM),
            vmem((1, group)),
            vmem((group, 2 * per_group * HD)),
            vmem((WINDOW, HD), chunk),
            vmem((WINDOW, HD), kv_local + chunk),
            vmem((group, HD), chunk),
            vmem((group, HD), kv_local + chunk),
        ],
        out_specs=(
            vmem((group, per_group * HD)),
            vmem((group, 2 * HD)),
            vmem((WINDOW, 2 * HD)),
        ),
        scratch_shapes=[
            pltpu.VMEM((ext, HD), jnp.bfloat16),
            pltpu.VMEM((ext, HD), jnp.bfloat16),
            pltpu.VMEM((ext // TK, HD, TK), jnp.bfloat16),
            pltpu.VMEM((ext, HD), jnp.float32),
            pltpu.VMEM((ext, HD), jnp.float32),
            pltpu.VMEM((span, wide), jnp.float32),
            pltpu.VMEM((span, wide), jnp.float32),
        ],
        compiler_params=pltpu.CompilerParams(vmem_limit_bytes=40 * 1024 * 1024),
        cost_estimate=pl.CostEstimate(
            flops=area * HD * 2 * 5, bytes_accessed=group * HD * 24, transcendentals=area
        ),
        name="attend",
    )(first_tile, low, qd, halo, halo, own, own)


def copied(copies, args, out_shapes):
    anywhere = pl.BlockSpec(memory_space=pl.ANY)
    count = copies(None)

    def kernel(*refs):
        sems = refs[-1]
        started = [
            pltpu.make_async_copy(source, target, sems.at[n])
            for n, (source, target) in enumerate(copies(refs[:-1]))
        ]
        for copy in started:
            copy.start()
        for copy in started:
            copy.wait()

    return pl.pallas_call(
        kernel,
        out_shape=tuple(jax.ShapeDtypeStruct(shape, jnp.bfloat16) for shape in out_shapes),
        in_specs=[anywhere] * len(args),
        out_specs=(anywhere,) * len(out_shapes),
        scratch_shapes=[pltpu.SemaphoreType.DMA((count,))],
        name="copied",
    )(*args)


def packed_kv(keys, values, ways):
    tokens, lanes = keys.shape[0], keys.shape[1] // ways

    def copies(refs):
        if refs is None:
            return 2 * ways
        k_ref, v_ref, out = refs
        return [
            (ref.at[:, pl.ds(j * lanes, lanes)], out.at[j, :, pl.ds(n * lanes, lanes)])
            for j in range(ways)
            for n, ref in enumerate((k_ref, v_ref))
        ]

    return copied(copies, (keys, values), [(ways, tokens, 2 * lanes)])[0]


def packed_qd(queries, grad_out, ways, chunks):
    tokens, lanes = queries.shape[0], queries.shape[1] // (ways * chunks)

    def copies(refs):
        if refs is None:
            return 2 * ways * chunks
        ins, outs = refs[:2], refs[2:]
        return [
            (
                ref.at[:, pl.ds((j * chunks + c) * lanes, lanes)],
                outs[c].at[j, :, pl.ds(n * lanes, lanes)],
            )
            for c in range(chunks)
            for j in range(ways)
            for n, ref in enumerate(ins)
        ]

    return copied(copies, (queries, grad_out), [(ways, tokens, 2 * lanes)] * chunks)


def unpacked(grads, q_lanes):
    ways, tokens, chunks = grads[0].shape[0], grads[0].shape[1], len(grads)

    def copies(refs):
        if refs is None:
            return 3 * ways * chunks
        ins, outs = refs[:chunks], refs[chunks:]
        return [
            (
                ins[c].at[j, :, pl.ds(first, lanes)],
                out.at[:, pl.ds((j * chunks + c) * lanes, lanes)],
            )
            for c in range(chunks)
            for j in range(ways)
            for out, first, lanes in zip(outs, (0, q_lanes, q_lanes + HD), (q_lanes, HD, HD))
        ]

    heads = ways * chunks
    return copied(
        copies,
        grads,
        [(tokens, heads * q_lanes), (tokens, heads * HD), (tokens, heads * HD)],
    )


def after(array, earlier):
    anywhere = pl.BlockSpec(memory_space=pl.ANY)

    def kernel(array_ref, earlier_ref, out_ref):
        pass

    return pl.pallas_call(
        kernel,
        out_shape=jax.ShapeDtypeStruct(array.shape, array.dtype),
        in_specs=[anywhere, anywhere],
        out_specs=anywhere,
        input_output_aliases={0: 0},
        name="after",
    )(array, earlier)


def exchanged(sent):
    return lax.all_to_all(sent, "head", split_axis=0, concat_axis=0, tiled=True)


def local(queries, keys, values, grad_out, doc_lengths):
    ways = lax.axis_size("head")
    tokens = queries.shape[0]
    group = tokens * ways
    kv_local = keys.shape[1] // (ways * HD)
    per_group = queries.shape[1] // keys.shape[1]
    q_lanes = per_group * HD
    group_first = lax.axis_index("seq") * group

    kv = exchanged(packed_kv(keys, values, ways)).reshape(group, 2 * kv_local * HD)
    halo = passed_along(kv[group - WINDOW :], "seq", 1)
    qds = []
    last = kv
    for sent in packed_qd(queries, grad_out, ways, kv_local):
        last = exchanged(after(sent, last)).reshape(group, 2 * q_lanes)
        qds.append(last)

    position = group_first + jnp.arange(group, dtype=jnp.int32)
    ends = jnp.cumsum(doc_lengths)
    doc_start = jnp.sum(
        jnp.where(position[:, None] >= ends[None, :], doc_lengths[None, :], 0), axis=1
    )
    low = jnp.maximum(doc_start, position - (WINDOW - 1)) - (group_first - WINDOW)
    low = low.astype(jnp.int32)
    first_tile = low[::TQ] // TK

    grads = []
    for c in range(kv_local):
        dq, own, rim = attend(qds[c], halo, kv, c, kv_local, low.reshape(1, group), first_tile)
        returned = passed_along(rim, "seq", -1).astype(jnp.float32)
        dkv = jnp.concatenate(
            [own[: group - WINDOW], own[group - WINDOW :] + returned], axis=0
        ).astype(jnp.bfloat16)
        together = jnp.concatenate([dq, dkv], axis=1)
        grads.append(exchanged(together.reshape(ways, tokens, q_lanes + 2 * HD)))
    return unpacked(grads, q_lanes)


def solution(mesh):
    rows = P(("seq", "head"), None)
    return jax.shard_map(
        local,
        mesh=mesh,
        in_specs=(rows, rows, rows, rows, P()),
        out_specs=(rows, rows, rows),
        check_vma=False,
    )
```

```python
import functools
import math

import jax
import jax.numpy as jnp
from jax import lax
from jax.experimental import pallas as pl
from jax.experimental.pallas import tpu as pltpu
from jax.sharding import PartitionSpec as P

HD = 128
WINDOW = 1024
TQ = 256
TK = 256
SCALING = HD ** (-0.5)
EXP2_SCALE = SCALING * math.log2(math.e)
MASKED = -1e30


def passed_along(shard, axis, by):
    count = lax.axis_size(axis)
    pairs = [(i, i + by) for i in range(count) if 0 <= i + by < count]
    return lax.ppermute(shard, axis, pairs)


def dot_nt(a, b):
    return lax.dot_general(a, b, (((1,), (1,)), ((), ())), preferred_element_type=jnp.float32)


def dot_nn(a, b):
    return lax.dot_general(a, b, (((1,), (0,)), ((), ())), preferred_element_type=jnp.float32)


def attend_kernel(
    per_group, first_tile, low_ref, qd_ref, halo_k, halo_v, own_k, own_v,
    dq_ref, own_ref, rim_ref,
    k_ext, v_ext, k_t, dk_ext, dv_ext, s_buf, dp_buf,
):
    group = qd_ref.shape[0]
    reach = WINDOW // TK
    k_ext[:WINDOW, :] = halo_k[...]
    k_ext[WINDOW:, :] = own_k[...]
    v_ext[:WINDOW, :] = halo_v[...]
    v_ext[WINDOW:, :] = own_v[...]
    dk_ext[...] = jnp.zeros_like(dk_ext)
    dv_ext[...] = jnp.zeros_like(dv_ext)

    def turn(t, carry):
        rows = pl.ds(pl.multiple_of(t * TK, TK), TK)
        k_t[t] = jnp.transpose(k_ext[rows, :].astype(jnp.float32)).astype(jnp.bfloat16)
        return carry

    lax.fori_loop(0, (group + WINDOW) // TK, turn, 0)
    wide = per_group * TQ
    key_iota = lax.broadcasted_iota(jnp.int32, (TK, wide), 0)

    def q_block(b, carry):
        q_rows = pl.ds(pl.multiple_of(b * TQ, TQ), TQ)
        start = first_tile[b]
        stop = b * (TQ // TK) + (TQ // TK - 1) + reach + 1
        q = jnp.concatenate(
            [qd_ref[q_rows, i * HD : (i + 1) * HD] for i in range(per_group)], axis=0
        )
        d_out = jnp.concatenate(
            [qd_ref[q_rows, i * HD : (i + 1) * HD] for i in range(per_group, 2 * per_group)],
            axis=0,
        )
        low = low_ref[:, q_rows]
        low = jnp.concatenate([low] * per_group, axis=1)
        high = b * TQ + WINDOW + lax.broadcasted_iota(jnp.int32, (1, TQ), 1)
        high = jnp.concatenate([high] * per_group, axis=1)

        def score(t, top):
            rows = pl.ds(pl.multiple_of(t * TK, TK), TK)
            slot = pl.ds(pl.multiple_of((t - start) * TK, TK), TK)
            s = dot_nt(k_ext[rows, :], q)
            j = key_iota + t * TK
            s = jnp.where((j >= low) & (j <= high), s, MASKED)
            s_buf[slot, :] = s
            return jnp.maximum(top, jnp.max(s, axis=0, keepdims=True))

        top = lax.fori_loop(start, stop, score, jnp.full((1, wide), MASKED, jnp.float32))

        def weigh(t, sums):
            total, dotted = sums
            rows = pl.ds(pl.multiple_of(t * TK, TK), TK)
            slot = pl.ds(pl.multiple_of((t - start) * TK, TK), TK)
            p = jnp.exp2((s_buf[slot, :] - top) * EXP2_SCALE)
            dp = dot_nt(v_ext[rows, :], d_out)
            s_buf[slot, :] = p
            dp_buf[slot, :] = dp
            return (
                total + jnp.sum(p, axis=0, keepdims=True),
                dotted + jnp.sum(p * dp, axis=0, keepdims=True),
            )

        zero = jnp.zeros((1, wide), jnp.float32)
        total, dotted = lax.fori_loop(start, stop, weigh, (zero, zero))
        inverse = 1.0 / total
        row_dot = dotted * inverse
        inverse_scaled = inverse * SCALING

        def grads(t, dq_t):
            rows = pl.ds(pl.multiple_of(t * TK, TK), TK)
            slot = pl.ds(pl.multiple_of((t - start) * TK, TK), TK)
            p = s_buf[slot, :]
            ds = ((p * inverse_scaled) * (dp_buf[slot, :] - row_dot)).astype(jnp.bfloat16)
            weights = (p * inverse).astype(jnp.bfloat16)
            dv_ext[rows, :] += dot_nn(weights, d_out)
            dk_ext[rows, :] += dot_nn(ds, q)
            return dq_t + dot_nn(k_t[t], ds)

        dq_t = lax.fori_loop(start, stop, grads, jnp.zeros((HD, wide), jnp.float32))
        dq = jnp.transpose(dq_t).astype(jnp.bfloat16)
        for i in range(per_group):
            dq_ref[q_rows, i * HD : (i + 1) * HD] = dq[i * TQ : (i + 1) * TQ, :]
        return carry

    lax.fori_loop(0, group // TQ, q_block, 0)
    rim_ref[:, :HD] = dk_ext[:WINDOW, :].astype(jnp.bfloat16)
    rim_ref[:, HD:] = dv_ext[:WINDOW, :].astype(jnp.bfloat16)
    own_ref[:, :HD] = dk_ext[WINDOW:, :]
    own_ref[:, HD:] = dv_ext[WINDOW:, :]


def attend(qd, halo, own, chunk, kv_local, low, first_tile):
    group = qd.shape[0]
    per_group = qd.shape[1] // (2 * HD)
    ext = group + WINDOW
    wide = per_group * TQ
    span = WINDOW + TQ

    def vmem(shape, lane_block=0):
        return pl.BlockSpec(shape, lambda i: (0, lane_block))

    area = group * (WINDOW + TQ) * per_group
    return pl.pallas_call(
        functools.partial(attend_kernel, per_group),
        grid=(1,),
        out_shape=(
            jax.ShapeDtypeStruct((group, per_group * HD), jnp.bfloat16),
            jax.ShapeDtypeStruct((group, 2 * HD), jnp.float32),
            jax.ShapeDtypeStruct((WINDOW, 2 * HD), jnp.bfloat16),
        ),
        in_specs=[
            pl.BlockSpec(memory_space=pltpu.SMEM),
            vmem((1, group)),
            vmem((group, 2 * per_group * HD)),
            vmem((WINDOW, HD), chunk),
            vmem((WINDOW, HD), kv_local + chunk),
            vmem((group, HD), chunk),
            vmem((group, HD), kv_local + chunk),
        ],
        out_specs=(
            vmem((group, per_group * HD)),
            vmem((group, 2 * HD)),
            vmem((WINDOW, 2 * HD)),
        ),
        scratch_shapes=[
            pltpu.VMEM((ext, HD), jnp.bfloat16),
            pltpu.VMEM((ext, HD), jnp.bfloat16),
            pltpu.VMEM((ext // TK, HD, TK), jnp.bfloat16),
            pltpu.VMEM((ext, HD), jnp.float32),
            pltpu.VMEM((ext, HD), jnp.float32),
            pltpu.VMEM((span, wide), jnp.float32),
            pltpu.VMEM((span, wide), jnp.float32),
        ],
        compiler_params=pltpu.CompilerParams(vmem_limit_bytes=40 * 1024 * 1024),
        cost_estimate=pl.CostEstimate(
            flops=area * HD * 2 * 5, bytes_accessed=group * HD * 24, transcendentals=area
        ),
        name="attend",
    )(first_tile, low, qd, halo, halo, own, own)


def row_block(tokens):
    return tokens // 4 if tokens % 64 == 0 else tokens


def packed(arrays, ways, chunks):
    tokens = arrays[0].shape[0]
    rows = row_block(tokens)
    lanes = [a.shape[1] // (ways * chunks) for a in arrays]
    total = sum(lanes)

    def kernel(*refs):
        ins, outs = refs[: len(arrays)], refs[len(arrays) :]
        for c, out in enumerate(outs):
            for j in range(ways):
                first = 0
                for ref, width in zip(ins, lanes):
                    at = (j * chunks + c) * width
                    out[j, :, first : first + width] = ref[:, at : at + width]
                    first += width

    return pl.pallas_call(
        kernel,
        grid=(tokens // rows,),
        out_shape=(jax.ShapeDtypeStruct((ways, tokens, total), jnp.bfloat16),) * chunks,
        in_specs=[pl.BlockSpec((rows, a.shape[1]), lambda r: (r, 0)) for a in arrays],
        out_specs=(pl.BlockSpec((ways, rows, total), lambda r: (0, r, 0)),) * chunks,
        compiler_params=pltpu.CompilerParams(vmem_limit_bytes=40 * 1024 * 1024),
        cost_estimate=pl.CostEstimate(
            flops=0, bytes_accessed=4 * ways * tokens * total * chunks, transcendentals=0
        ),
        name="packed",
    )(*arrays)


def unpacked(grads, q_lanes):
    ways, tokens, total = grads[0].shape
    chunks = len(grads)
    rows = row_block(tokens)
    lanes = (q_lanes, HD, HD)

    def kernel(*refs):
        ins, outs = refs[:chunks], refs[chunks:]
        for c, ref in enumerate(ins):
            for j in range(ways):
                first = 0
                for out, width in zip(outs, lanes):
                    at = (j * chunks + c) * width
                    out[:, at : at + width] = ref[j, :, first : first + width]
                    first += width

    widths = [ways * chunks * width for width in lanes]
    return pl.pallas_call(
        kernel,
        grid=(tokens // rows,),
        out_shape=tuple(jax.ShapeDtypeStruct((tokens, w), jnp.bfloat16) for w in widths),
        in_specs=[pl.BlockSpec((ways, rows, total), lambda r: (0, r, 0))] * chunks,
        out_specs=tuple(pl.BlockSpec((rows, w), lambda r: (r, 0)) for w in widths),
        compiler_params=pltpu.CompilerParams(vmem_limit_bytes=40 * 1024 * 1024),
        cost_estimate=pl.CostEstimate(
            flops=0, bytes_accessed=4 * ways * tokens * total * chunks, transcendentals=0
        ),
        name="unpacked",
    )(*grads)


def after(array, *earlier):
    anywhere = pl.BlockSpec(memory_space=pl.ANY)

    def kernel(*refs):
        pass

    return pl.pallas_call(
        kernel,
        out_shape=jax.ShapeDtypeStruct(array.shape, array.dtype),
        in_specs=[anywhere] * (1 + len(earlier)),
        out_specs=anywhere,
        input_output_aliases={0: 0},
        name="after",
    )(array, *earlier)


def exchanged(sent):
    return lax.all_to_all(sent, "head", split_axis=0, concat_axis=0, tiled=True)


def local(queries, keys, values, grad_out, doc_lengths):
    ways = lax.axis_size("head")
    tokens = queries.shape[0]
    group = tokens * ways
    kv_local = keys.shape[1] // (ways * HD)
    per_group = queries.shape[1] // keys.shape[1]
    q_lanes = per_group * HD
    group_first = lax.axis_index("seq") * group

    kv = exchanged(packed((keys, values), ways, 1)[0]).reshape(group, 2 * kv_local * HD)
    halo = passed_along(kv[group - WINDOW :], "seq", 1)
    qds = []
    for c, sent in enumerate(packed((queries, grad_out), ways, kv_local)):
        earlier = (qds[-1], halo) if c else (kv,)
        qds.append(exchanged(after(sent, *earlier)).reshape(group, 2 * q_lanes))

    position = group_first + jnp.arange(group, dtype=jnp.int32)
    ends = jnp.cumsum(doc_lengths)
    doc_start = jnp.sum(
        jnp.where(position[:, None] >= ends[None, :], doc_lengths[None, :], 0), axis=1
    )
    low = jnp.maximum(doc_start, position - (WINDOW - 1)) - (group_first - WINDOW)
    low = low.astype(jnp.int32)
    first_tile = low[::TQ] // TK

    grads = []
    for c in range(kv_local):
        dq, own, rim = attend(qds[c], halo, kv, c, kv_local, low.reshape(1, group), first_tile)
        returned = passed_along(rim, "seq", -1).astype(jnp.float32)
        dkv = jnp.concatenate(
            [own[: group - WINDOW], own[group - WINDOW :] + returned], axis=0
        ).astype(jnp.bfloat16)
        together = jnp.concatenate([dq, dkv], axis=1)
        grads.append(exchanged(together.reshape(ways, tokens, q_lanes + 2 * HD)))
    return unpacked(grads, q_lanes)


def solution(mesh):
    rows = P(("seq", "head"), None)
    return jax.shard_map(
        local,
        mesh=mesh,
        in_specs=(rows, rows, rows, rows, P()),
        out_specs=(rows, rows, rows),
        check_vma=False,
    )
```

```python
import functools
import math

import jax
import jax.numpy as jnp
from jax import lax
from jax.experimental import pallas as pl
from jax.experimental.pallas import tpu as pltpu
from jax.sharding import PartitionSpec as P

HD = 128
WINDOW = 1024
TQ = 256
TK = 256
SCALING = HD ** (-0.5)
EXP2_SCALE = SCALING * math.log2(math.e)
MASKED = -1e30


def passed_along(shard, axis, by):
    count = lax.axis_size(axis)
    pairs = [(i, i + by) for i in range(count) if 0 <= i + by < count]
    return lax.ppermute(shard, axis, pairs)


def dot_nt(a, b):
    return lax.dot_general(a, b, (((1,), (1,)), ((), ())), preferred_element_type=jnp.float32)


def dot_nn(a, b):
    return lax.dot_general(a, b, (((1,), (0,)), ((), ())), preferred_element_type=jnp.float32)


def partner_rows(me_ref, k, tokens):
    return pl.ds(pl.multiple_of((me_ref[0] ^ k) * tokens, tokens), tokens)


def gather_rows(me_ref, blocks, out_ref):
    for k, block in enumerate(blocks):
        out_ref[partner_rows(me_ref, k, block.shape[0]), :] = block[...]


def attend_kernel(per_group, ways, me_ref, first_tile, low_ref, halo_k, halo_v, own_k, own_v, *refs):
    blocks, refs = refs[:ways], refs[ways:]
    dq_ref, own_ref, rim_ref, qd_ref, k_ext, v_ext, k_t, dk_ext, dv_ext, s_buf, dp_buf = refs
    gather_rows(me_ref, blocks, qd_ref)
    group = qd_ref.shape[0]
    reach = WINDOW // TK
    k_ext[:WINDOW, :] = halo_k[...]
    k_ext[WINDOW:, :] = own_k[...]
    v_ext[:WINDOW, :] = halo_v[...]
    v_ext[WINDOW:, :] = own_v[...]
    dk_ext[...] = jnp.zeros_like(dk_ext)
    dv_ext[...] = jnp.zeros_like(dv_ext)

    def turn(t, carry):
        rows = pl.ds(pl.multiple_of(t * TK, TK), TK)
        k_t[t] = jnp.transpose(k_ext[rows, :].astype(jnp.float32)).astype(jnp.bfloat16)
        return carry

    lax.fori_loop(0, (group + WINDOW) // TK, turn, 0)
    wide = per_group * TQ
    key_iota = lax.broadcasted_iota(jnp.int32, (TK, wide), 0)

    def q_block(b, carry):
        q_rows = pl.ds(pl.multiple_of(b * TQ, TQ), TQ)
        start = first_tile[b]
        stop = b * (TQ // TK) + (TQ // TK - 1) + reach + 1
        q = jnp.concatenate(
            [qd_ref[q_rows, i * HD : (i + 1) * HD] for i in range(per_group)], axis=0
        )
        d_out = jnp.concatenate(
            [qd_ref[q_rows, i * HD : (i + 1) * HD] for i in range(per_group, 2 * per_group)],
            axis=0,
        )
        low = low_ref[:, q_rows]
        low = jnp.concatenate([low] * per_group, axis=1)
        high = b * TQ + WINDOW + lax.broadcasted_iota(jnp.int32, (1, TQ), 1)
        high = jnp.concatenate([high] * per_group, axis=1)

        def score(t, top):
            rows = pl.ds(pl.multiple_of(t * TK, TK), TK)
            slot = pl.ds(pl.multiple_of((t - start) * TK, TK), TK)
            s = dot_nt(k_ext[rows, :], q)
            j = key_iota + t * TK
            s = jnp.where((j >= low) & (j <= high), s, MASKED)
            s_buf[slot, :] = s
            return jnp.maximum(top, jnp.max(s, axis=0, keepdims=True))

        top = lax.fori_loop(start, stop, score, jnp.full((1, wide), MASKED, jnp.float32))

        def weigh(t, sums):
            total, dotted = sums
            rows = pl.ds(pl.multiple_of(t * TK, TK), TK)
            slot = pl.ds(pl.multiple_of((t - start) * TK, TK), TK)
            p = jnp.exp2((s_buf[slot, :] - top) * EXP2_SCALE)
            dp = dot_nt(v_ext[rows, :], d_out)
            s_buf[slot, :] = p
            dp_buf[slot, :] = dp
            return (
                total + jnp.sum(p, axis=0, keepdims=True),
                dotted + jnp.sum(p * dp, axis=0, keepdims=True),
            )

        zero = jnp.zeros((1, wide), jnp.float32)
        total, dotted = lax.fori_loop(start, stop, weigh, (zero, zero))
        inverse = 1.0 / total
        row_dot = dotted * inverse
        inverse_scaled = inverse * SCALING

        def grads(t, dq_t):
            rows = pl.ds(pl.multiple_of(t * TK, TK), TK)
            slot = pl.ds(pl.multiple_of((t - start) * TK, TK), TK)
            p = s_buf[slot, :]
            ds = ((p * inverse_scaled) * (dp_buf[slot, :] - row_dot)).astype(jnp.bfloat16)
            weights = (p * inverse).astype(jnp.bfloat16)
            dv_ext[rows, :] += dot_nn(weights, d_out)
            dk_ext[rows, :] += dot_nn(ds, q)
            return dq_t + dot_nn(k_t[t], ds)

        dq_t = lax.fori_loop(start, stop, grads, jnp.zeros((HD, wide), jnp.float32))
        dq = jnp.transpose(dq_t).astype(jnp.bfloat16)
        for i in range(per_group):
            dq_ref[q_rows, i * HD : (i + 1) * HD] = dq[i * TQ : (i + 1) * TQ, :]
        return carry

    lax.fori_loop(0, group // TQ, q_block, 0)
    rim_ref[:, :HD] = dk_ext[:WINDOW, :].astype(jnp.bfloat16)
    rim_ref[:, HD:] = dv_ext[:WINDOW, :].astype(jnp.bfloat16)
    own_ref[:, :HD] = dk_ext[WINDOW:, :]
    own_ref[:, HD:] = dv_ext[WINDOW:, :]


def attend(me, qd_blocks, halo, own, chunk, kv_local, low, first_tile):
    group = own.shape[0]
    tokens, qd_lanes = qd_blocks[0].shape
    ways = len(qd_blocks)
    per_group = qd_lanes // (2 * HD)
    ext = group + WINDOW
    wide = per_group * TQ
    span = WINDOW + TQ

    def vmem(shape, lane_block=0):
        return pl.BlockSpec(shape, lambda i: (0, lane_block))

    area = group * (WINDOW + TQ) * per_group
    return pl.pallas_call(
        functools.partial(attend_kernel, per_group, ways),
        grid=(1,),
        out_shape=(
            jax.ShapeDtypeStruct((group, per_group * HD), jnp.bfloat16),
            jax.ShapeDtypeStruct((group, 2 * HD), jnp.float32),
            jax.ShapeDtypeStruct((WINDOW, 2 * HD), jnp.bfloat16),
        ),
        in_specs=[
            pl.BlockSpec(memory_space=pltpu.SMEM),
            pl.BlockSpec(memory_space=pltpu.SMEM),
            vmem((1, group)),
            vmem((WINDOW, HD), chunk),
            vmem((WINDOW, HD), kv_local + chunk),
            vmem((group, HD), chunk),
            vmem((group, HD), kv_local + chunk),
        ]
        + [vmem((tokens, qd_lanes))] * ways,
        out_specs=(
            vmem((group, per_group * HD)),
            vmem((group, 2 * HD)),
            vmem((WINDOW, 2 * HD)),
        ),
        scratch_shapes=[
            pltpu.VMEM((group, qd_lanes), jnp.bfloat16),
            pltpu.VMEM((ext, HD), jnp.bfloat16),
            pltpu.VMEM((ext, HD), jnp.bfloat16),
            pltpu.VMEM((ext // TK, HD, TK), jnp.bfloat16),
            pltpu.VMEM((ext, HD), jnp.float32),
            pltpu.VMEM((ext, HD), jnp.float32),
            pltpu.VMEM((span, wide), jnp.float32),
            pltpu.VMEM((span, wide), jnp.float32),
        ],
        compiler_params=pltpu.CompilerParams(vmem_limit_bytes=40 * 1024 * 1024),
        cost_estimate=pl.CostEstimate(
            flops=area * HD * 2 * 5, bytes_accessed=group * HD * 24, transcendentals=area
        ),
        name="attend",
    )(me, first_tile, low, halo, halo, own, own, *qd_blocks)


SMEM = pl.BlockSpec(memory_space=pltpu.SMEM)
VMEM = pl.BlockSpec(memory_space=pltpu.VMEM)
ANYWHERE = pl.BlockSpec(memory_space=pl.ANY)


def on_chip(kernel, me, arrays, shapes, name, scratch=()):
    moved = sum(a.size * a.dtype.itemsize for a in arrays) + sum(2 * math.prod(s) for s in shapes)
    return pl.pallas_call(
        kernel,
        out_shape=tuple(jax.ShapeDtypeStruct(s, jnp.bfloat16) for s in shapes),
        in_specs=[SMEM] + [VMEM] * len(arrays),
        out_specs=(VMEM,) * len(shapes),
        scratch_shapes=list(scratch),
        compiler_params=pltpu.CompilerParams(vmem_limit_bytes=40 * 1024 * 1024),
        cost_estimate=pl.CostEstimate(flops=0, bytes_accessed=moved, transcendentals=0),
        name=name,
    )(me, *arrays)


def packed(me, arrays, ways, chunks):
    tokens = arrays[0].shape[0]
    lanes = [a.shape[1] // (ways * chunks) for a in arrays]
    total = sum(lanes)

    def kernel(me_ref, *refs):
        ins, outs = refs[: len(arrays)], refs[len(arrays) :]
        for c in range(chunks):
            for k in range(ways):
                first = 0
                for ref, width in zip(ins, lanes):
                    at = pl.multiple_of(((me_ref[0] ^ k) * chunks + c) * width, width)
                    outs[c * ways + k][:, first : first + width] = ref[:, pl.ds(at, width)]
                    first += width

    blocks = on_chip(kernel, me, arrays, [(tokens, total)] * (ways * chunks), "packed")
    return [list(blocks[c * ways : (c + 1) * ways]) for c in range(chunks)]


def unpacked(me, grads, q_lanes):
    chunks, ways = len(grads), len(grads[0])
    tokens = grads[0][0].shape[0]
    lanes = (q_lanes, HD, HD)

    def kernel(me_ref, *refs):
        ins, outs = refs[: chunks * ways], refs[chunks * ways :]
        for c in range(chunks):
            for k in range(ways):
                first = 0
                for out, width in zip(outs, lanes):
                    at = pl.multiple_of(((me_ref[0] ^ k) * chunks + c) * width, width)
                    out[:, pl.ds(at, width)] = ins[c * ways + k][:, first : first + width]
                    first += width

    shapes = [(tokens, ways * chunks * width) for width in lanes]
    return on_chip(kernel, me, [g for blocks in grads for g in blocks], shapes, "unpacked")


def gathered(me, blocks):
    tokens, lanes = blocks[0].shape
    ways = len(blocks)
    group = ways * tokens

    def kernel(me_ref, *refs):
        all_ref, tail_ref = refs[ways:]
        gather_rows(me_ref, refs[:ways], all_ref)
        tail_ref[...] = all_ref[group - WINDOW :, :]

    return on_chip(kernel, me, blocks, [(group, lanes), (WINDOW, lanes)], "gathered")


def settled(me, dq, own, returned, ways):
    group, q_lanes = dq.shape
    tokens = group // ways

    def kernel(me_ref, dq_ref, own_ref, back_ref, *refs):
        outs, total = refs[:ways], refs[ways]
        cut = group - WINDOW
        total[:cut, :] = own_ref[:cut, :].astype(jnp.bfloat16)
        total[cut:, :] = (own_ref[cut:, :] + back_ref[...].astype(jnp.float32)).astype(jnp.bfloat16)
        for k, out in enumerate(outs):
            rows = partner_rows(me_ref, k, tokens)
            out[:, :q_lanes] = dq_ref[rows, :]
            out[:, q_lanes:] = total[rows, :]

    return on_chip(
        kernel, me, (dq, own, returned), [(tokens, q_lanes + 2 * HD)] * ways, "settled",
        [pltpu.VMEM((group, 2 * HD), jnp.bfloat16)],
    )


def after(array, *earlier):
    def kernel(*refs):
        pass

    return pl.pallas_call(
        kernel,
        out_shape=jax.ShapeDtypeStruct(array.shape, array.dtype),
        in_specs=[ANYWHERE] * (1 + len(earlier)),
        out_specs=ANYWHERE,
        input_output_aliases={0: 0},
        name="after",
    )(array, *earlier)


def exchanged(blocks):
    ways = len(blocks)
    came = {0: blocks[0]}
    for k in reversed(range(1, ways)):
        came[k] = lax.ppermute(blocks[k], "head", [(i, i ^ k) for i in range(ways)])
    return [came[k] for k in range(ways)]


def local(queries, keys, values, grad_out, doc_lengths):
    ways = lax.axis_size("head")
    tokens = queries.shape[0]
    group = tokens * ways
    kv_local = keys.shape[1] // (ways * HD)
    per_group = queries.shape[1] // keys.shape[1]
    q_lanes = per_group * HD
    group_first = lax.axis_index("seq") * group
    me = lax.axis_index("head").astype(jnp.int32).reshape(1)

    came = exchanged(packed(me, (keys, values), ways, 1)[0])
    kv, tail = gathered(me, came)
    halo = passed_along(tail, "seq", 1)
    qds = []
    for sent in packed(me, (queries, grad_out), ways, kv_local):
        came = exchanged([sent[0]] + [after(sent[k], came[k]) for k in range(1, ways)])
        qds.append(came)

    position = group_first + jnp.arange(group, dtype=jnp.int32)
    ends = jnp.cumsum(doc_lengths)
    doc_start = jnp.sum(
        jnp.where(position[:, None] >= ends[None, :], doc_lengths[None, :], 0), axis=1
    )
    low = jnp.maximum(doc_start, position - (WINDOW - 1)) - (group_first - WINDOW)
    low = low.astype(jnp.int32)
    first_tile = low[::TQ] // TK

    grads = []
    for c in range(kv_local):
        dq, own, rim = attend(me, qds[c], halo, kv, c, kv_local, low.reshape(1, group), first_tile)
        returned = passed_along(rim, "seq", -1)
        grads.append(exchanged(settled(me, dq, own, returned, ways)))
    return unpacked(me, grads, q_lanes)


def solution(mesh):
    rows = P(("seq", "head"), None)
    return jax.shard_map(
        local,
        mesh=mesh,
        in_specs=(rows, rows, rows, rows, P()),
        out_specs=(rows, rows, rows),
        check_vma=False,
    )
```

```python
import functools
import math

import jax
import jax.numpy as jnp
from jax import lax
from jax.experimental import pallas as pl
from jax.experimental.pallas import tpu as pltpu
from jax.sharding import PartitionSpec as P

HD = 128
WINDOW = 1024
TQ = 256
TK = 256
SCALING = HD ** (-0.5)
EXP2_SCALE = SCALING * math.log2(math.e)
MASKED = -1e30


def passed_along(shard, axis, by):
    count = lax.axis_size(axis)
    pairs = [(i, i + by) for i in range(count) if 0 <= i + by < count]
    return lax.ppermute(shard, axis, pairs)


def dot_nt(a, b):
    return lax.dot_general(a, b, (((1,), (1,)), ((), ())), preferred_element_type=jnp.float32)


def dot_nn(a, b):
    return lax.dot_general(a, b, (((1,), (0,)), ((), ())), preferred_element_type=jnp.float32)


def partner_rows(me_ref, k, tokens):
    return pl.ds(pl.multiple_of((me_ref[0] ^ k) * tokens, tokens), tokens)


def gather_rows(me_ref, blocks, out_ref):
    for k, block in enumerate(blocks):
        out_ref[partner_rows(me_ref, k, block.shape[0]), :] = block[...]


def attend_kernel(per_group, ways, me_ref, first_tile, low_ref, halo_k, halo_v, own_k, own_v, *refs):
    blocks, refs = refs[:ways], refs[ways:]
    dq_ref, own_ref, rim_ref, qd_ref, k_ext, v_ext, k_t, dk_ext, dv_ext, s_buf, dp_buf = refs
    if ways == 1:
        qd_ref = blocks[0]
    else:
        gather_rows(me_ref, blocks, qd_ref)
    group = qd_ref.shape[0]
    reach = WINDOW // TK
    k_ext[:WINDOW, :] = halo_k[...]
    k_ext[WINDOW:, :] = own_k[...]
    v_ext[:WINDOW, :] = halo_v[...]
    v_ext[WINDOW:, :] = own_v[...]
    dk_ext[...] = jnp.zeros_like(dk_ext)
    dv_ext[...] = jnp.zeros_like(dv_ext)

    def turn(t, carry):
        rows = pl.ds(pl.multiple_of(t * TK, TK), TK)
        k_t[t] = jnp.transpose(k_ext[rows, :].astype(jnp.float32)).astype(jnp.bfloat16)
        return carry

    lax.fori_loop(0, (group + WINDOW) // TK, turn, 0)
    wide = per_group * TQ
    key_iota = lax.broadcasted_iota(jnp.int32, (TK, wide), 0)

    def q_block(b, carry):
        q_rows = pl.ds(pl.multiple_of(b * TQ, TQ), TQ)
        start = first_tile[b]
        stop = b * (TQ // TK) + (TQ // TK - 1) + reach + 1
        q = jnp.concatenate(
            [qd_ref[q_rows, i * HD : (i + 1) * HD] for i in range(per_group)], axis=0
        )
        d_out = jnp.concatenate(
            [qd_ref[q_rows, i * HD : (i + 1) * HD] for i in range(per_group, 2 * per_group)],
            axis=0,
        )
        low = low_ref[:, q_rows]
        low = jnp.concatenate([low] * per_group, axis=1)
        high = b * TQ + WINDOW + lax.broadcasted_iota(jnp.int32, (1, TQ), 1)
        high = jnp.concatenate([high] * per_group, axis=1)

        def score(t, top):
            rows = pl.ds(pl.multiple_of(t * TK, TK), TK)
            slot = pl.ds(pl.multiple_of((t - start) * TK, TK), TK)
            s = dot_nt(k_ext[rows, :], q)
            j = key_iota + t * TK
            s = jnp.where((j >= low) & (j <= high), s, MASKED)
            s_buf[slot, :] = s
            return jnp.maximum(top, jnp.max(s, axis=0, keepdims=True))

        top = lax.fori_loop(start, stop, score, jnp.full((1, wide), MASKED, jnp.float32))

        def weigh(t, sums):
            total, dotted = sums
            rows = pl.ds(pl.multiple_of(t * TK, TK), TK)
            slot = pl.ds(pl.multiple_of((t - start) * TK, TK), TK)
            p = jnp.exp2((s_buf[slot, :] - top) * EXP2_SCALE)
            dp = dot_nt(v_ext[rows, :], d_out)
            s_buf[slot, :] = p
            dp_buf[slot, :] = dp
            return (
                total + jnp.sum(p, axis=0, keepdims=True),
                dotted + jnp.sum(p * dp, axis=0, keepdims=True),
            )

        zero = jnp.zeros((1, wide), jnp.float32)
        total, dotted = lax.fori_loop(start, stop, weigh, (zero, zero))
        inverse = 1.0 / total
        row_dot = dotted * inverse
        inverse_scaled = inverse * SCALING

        def grads(t, dq_t):
            rows = pl.ds(pl.multiple_of(t * TK, TK), TK)
            slot = pl.ds(pl.multiple_of((t - start) * TK, TK), TK)
            p = s_buf[slot, :]
            ds = ((p * inverse_scaled) * (dp_buf[slot, :] - row_dot)).astype(jnp.bfloat16)
            weights = (p * inverse).astype(jnp.bfloat16)
            dv_ext[rows, :] += dot_nn(weights, d_out)
            dk_ext[rows, :] += dot_nn(ds, q)
            return dq_t + dot_nn(k_t[t], ds)

        dq_t = lax.fori_loop(start, stop, grads, jnp.zeros((HD, wide), jnp.float32))
        dq = jnp.transpose(dq_t).astype(jnp.bfloat16)
        for i in range(per_group):
            dq_ref[q_rows, i * HD : (i + 1) * HD] = dq[i * TQ : (i + 1) * TQ, :]
        return carry

    lax.fori_loop(0, group // TQ, q_block, 0)
    rim_ref[:, :HD] = dk_ext[:WINDOW, :].astype(jnp.bfloat16)
    rim_ref[:, HD:] = dv_ext[:WINDOW, :].astype(jnp.bfloat16)
    own_ref[:, :HD] = dk_ext[WINDOW:, :]
    own_ref[:, HD:] = dv_ext[WINDOW:, :]


def attend(me, qd_blocks, halo, own, chunk, kv_local, low, first_tile):
    group = own.shape[0]
    tokens, qd_lanes = qd_blocks[0].shape
    ways = len(qd_blocks)
    per_group = qd_lanes // (2 * HD)
    ext = group + WINDOW
    wide = per_group * TQ
    span = WINDOW + TQ

    def vmem(shape, lane_block=0):
        return pl.BlockSpec(shape, lambda i: (0, lane_block))

    area = group * (WINDOW + TQ) * per_group
    return pl.pallas_call(
        functools.partial(attend_kernel, per_group, ways),
        grid=(1,),
        out_shape=(
            jax.ShapeDtypeStruct((group, per_group * HD), jnp.bfloat16),
            jax.ShapeDtypeStruct((group, 2 * HD), jnp.float32),
            jax.ShapeDtypeStruct((WINDOW, 2 * HD), jnp.bfloat16),
        ),
        in_specs=[
            pl.BlockSpec(memory_space=pltpu.SMEM),
            pl.BlockSpec(memory_space=pltpu.SMEM),
            vmem((1, group)),
            vmem((WINDOW, HD), chunk),
            vmem((WINDOW, HD), kv_local + chunk),
            vmem((group, HD), chunk),
            vmem((group, HD), kv_local + chunk),
        ]
        + [vmem((tokens, qd_lanes))] * ways,
        out_specs=(
            vmem((group, per_group * HD)),
            vmem((group, 2 * HD)),
            vmem((WINDOW, 2 * HD)),
        ),
        scratch_shapes=[
            pltpu.VMEM((group, qd_lanes), jnp.bfloat16),
            pltpu.VMEM((ext, HD), jnp.bfloat16),
            pltpu.VMEM((ext, HD), jnp.bfloat16),
            pltpu.VMEM((ext // TK, HD, TK), jnp.bfloat16),
            pltpu.VMEM((ext, HD), jnp.float32),
            pltpu.VMEM((ext, HD), jnp.float32),
            pltpu.VMEM((span, wide), jnp.float32),
            pltpu.VMEM((span, wide), jnp.float32),
        ],
        compiler_params=pltpu.CompilerParams(vmem_limit_bytes=40 * 1024 * 1024),
        cost_estimate=pl.CostEstimate(
            flops=area * HD * 2 * 5, bytes_accessed=group * HD * 24, transcendentals=area
        ),
        name="attend",
    )(me, first_tile, low, halo, halo, own, own, *qd_blocks)


SMEM = pl.BlockSpec(memory_space=pltpu.SMEM)
VMEM = pl.BlockSpec(memory_space=pltpu.VMEM)
ANYWHERE = pl.BlockSpec(memory_space=pl.ANY)


def on_chip(kernel, me, arrays, shapes, name, scratch=(), earlier=()):
    moved = sum(a.size * a.dtype.itemsize for a in arrays) + sum(2 * math.prod(s) for s in shapes)

    def body(me_ref, *refs):
        kernel(me_ref, *refs[len(earlier) :])

    return pl.pallas_call(
        body,
        out_shape=tuple(jax.ShapeDtypeStruct(s, jnp.bfloat16) for s in shapes),
        in_specs=[SMEM] + [ANYWHERE] * len(earlier) + [VMEM] * len(arrays),
        out_specs=(VMEM,) * len(shapes),
        scratch_shapes=list(scratch),
        compiler_params=pltpu.CompilerParams(vmem_limit_bytes=40 * 1024 * 1024),
        cost_estimate=pl.CostEstimate(flops=0, bytes_accessed=moved, transcendentals=0),
        name=name,
    )(me, *earlier, *arrays)


def packed(me, arrays, ways, chunk, chunks, by_partner, earlier=()):
    tokens = arrays[0].shape[0]
    lanes = [a.shape[1] // (ways * chunks) for a in arrays]
    total = sum(lanes)

    def kernel(me_ref, *refs):
        ins, outs = refs[: len(arrays)], refs[len(arrays) :]
        for k in range(ways):
            out = outs[k] if by_partner else outs[0].at[k]
            first = 0
            for ref, width in zip(ins, lanes):
                if by_partner:
                    at = pl.multiple_of(((me_ref[0] ^ k) * chunks + chunk) * width, width)
                else:
                    at = (k * chunks + chunk) * width
                out[:, first : first + width] = ref[:, pl.ds(at, width)]
                first += width

    shapes = [(tokens, total)] * ways if by_partner else [(ways, tokens, total)]
    return on_chip(kernel, me, arrays, shapes, "packed", earlier=earlier)


def unpacked(me, grads, ways, q_lanes):
    chunks = len(grads)
    tokens = grads[0][0].shape[-2]
    lanes = (q_lanes, HD, HD)
    counts = [len(blocks) for blocks in grads]

    def kernel(me_ref, *refs):
        outs = refs[sum(counts) :]
        for c in range(chunks):
            ins = refs[sum(counts[:c]) : sum(counts[: c + 1])]
            for k in range(ways):
                block = ins[k] if len(ins) > 1 else ins[0].at[k]
                first = 0
                for out, width in zip(outs, lanes):
                    if len(ins) > 1:
                        at = pl.multiple_of(((me_ref[0] ^ k) * chunks + c) * width, width)
                    else:
                        at = (k * chunks + c) * width
                    out[:, pl.ds(at, width)] = block[:, first : first + width]
                    first += width

    shapes = [(tokens, ways * chunks * width) for width in lanes]
    return on_chip(kernel, me, [g for blocks in grads for g in blocks], shapes, "unpacked")


def gathered(me, blocks):
    tokens, lanes = blocks[0].shape
    ways = len(blocks)
    group = ways * tokens

    def kernel(me_ref, *refs):
        all_ref, tail_ref = refs[ways:]
        gather_rows(me_ref, refs[:ways], all_ref)
        tail_ref[...] = all_ref[group - WINDOW :, :]

    return on_chip(kernel, me, blocks, [(group, lanes), (WINDOW, lanes)], "gathered")


def settled(me, dq, own, returned, ways, by_partner):
    group, q_lanes = dq.shape
    tokens = group // ways
    total_lanes = q_lanes + 2 * HD

    def kernel(me_ref, dq_ref, own_ref, back_ref, *refs):
        cut = group - WINDOW
        total = refs[-1] if by_partner else refs[0].at[:, q_lanes:]
        total[:cut, :] = own_ref[:cut, :].astype(jnp.bfloat16)
        total[cut:, :] = (own_ref[cut:, :] + back_ref[...].astype(jnp.float32)).astype(jnp.bfloat16)
        if not by_partner:
            refs[0][:, :q_lanes] = dq_ref[...]
            return
        for k, out in enumerate(refs[:ways]):
            rows = partner_rows(me_ref, k, tokens)
            out[:, :q_lanes] = dq_ref[rows, :]
            out[:, q_lanes:] = total[rows, :]

    shapes = [(tokens, total_lanes)] * ways if by_partner else [(group, total_lanes)]
    scratch = [pltpu.VMEM((group, 2 * HD), jnp.bfloat16)] if by_partner else []
    return on_chip(kernel, me, (dq, own, returned), shapes, "settled", scratch)


def exchanged(blocks):
    ways = len(blocks)
    came = {0: blocks[0]}
    for k in reversed(range(1, ways)):
        came[k] = lax.ppermute(blocks[k], "head", [(i, i ^ k) for i in range(ways)])
    return [came[k] for k in range(ways)]


def exchanged_at_once(sent):
    return lax.all_to_all(sent, "head", split_axis=0, concat_axis=0, tiled=True)


def local(queries, keys, values, grad_out, doc_lengths):
    ways = lax.axis_size("head")
    tokens = queries.shape[0]
    group = tokens * ways
    kv_local = keys.shape[1] // (ways * HD)
    per_group = queries.shape[1] // keys.shape[1]
    q_lanes = per_group * HD
    group_first = lax.axis_index("seq") * group
    me = lax.axis_index("head").astype(jnp.int32).reshape(1)

    came = exchanged(packed(me, (keys, values), ways, 0, 1, True))
    kv, tail = gathered(me, came)
    halo = passed_along(tail, "seq", 1)
    qds = [
        exchanged(packed(me, (queries, grad_out), ways, 0, kv_local, True, [came[ways - 2]]))
    ]
    for c in range(1, kv_local):
        earlier = [qds[-1][-2] if c == 1 else qds[-1][0], halo]
        sent = packed(me, (queries, grad_out), ways, c, kv_local, False, earlier)[0]
        qds.append([exchanged_at_once(sent).reshape(group, 2 * q_lanes)])

    position = group_first + jnp.arange(group, dtype=jnp.int32)
    ends = jnp.cumsum(doc_lengths)
    doc_start = jnp.sum(
        jnp.where(position[:, None] >= ends[None, :], doc_lengths[None, :], 0), axis=1
    )
    low = jnp.maximum(doc_start, position - (WINDOW - 1)) - (group_first - WINDOW)
    low = low.astype(jnp.int32)
    first_tile = low[::TQ] // TK

    grads = []
    for c in range(kv_local):
        dq, own, rim = attend(me, qds[c], halo, kv, c, kv_local, low.reshape(1, group), first_tile)
        returned = passed_along(rim, "seq", -1)
        last = c == kv_local - 1
        settled_now = settled(me, dq, own, returned, ways, last)
        if last:
            grads.append(exchanged(settled_now))
        else:
            sent = settled_now[0].reshape(ways, tokens, q_lanes + 2 * HD)
            grads.append([exchanged_at_once(sent)])
    return unpacked(me, grads, ways, q_lanes)


def solution(mesh):
    rows = P(("seq", "head"), None)
    return jax.shard_map(
        local,
        mesh=mesh,
        in_specs=(rows, rows, rows, rows, P()),
        out_specs=(rows, rows, rows),
        check_vma=False,
    )
```

```python
import functools
import math

import jax
import jax.numpy as jnp
from jax import lax
from jax.experimental import pallas as pl
from jax.experimental.pallas import tpu as pltpu
from jax.sharding import PartitionSpec as P

HD = 128
WINDOW = 1024
TQ = 256
TK = 256
SCALING = HD ** (-0.5)
EXP2_SCALE = SCALING * math.log2(math.e)
MASKED = -1e30
SPARE = 4 * 1024 * 1024
SMEM = pl.BlockSpec(memory_space=pltpu.SMEM)
VMEM = pl.BlockSpec(memory_space=pltpu.VMEM)
ANYWHERE = pl.BlockSpec(memory_space=pl.ANY)


def array_bytes(arrays):
    return sum(math.prod(a.shape) * a.dtype.itemsize for a in arrays)


def passed_along(shard, axis, by):
    count = lax.axis_size(axis)
    pairs = [(i, i + by) for i in range(count) if 0 <= i + by < count]
    return lax.ppermute(shard, axis, pairs)


def dot_nt(a, b):
    return lax.dot_general(a, b, (((1,), (1,)), ((), ())), preferred_element_type=jnp.float32)


def dot_nn(a, b):
    return lax.dot_general(a, b, (((1,), (0,)), ((), ())), preferred_element_type=jnp.float32)


def partner_rows(me_ref, k, tokens):
    return pl.ds(pl.multiple_of((me_ref[0] ^ k) * tokens, tokens), tokens)


def gather_rows(me_ref, blocks, out_ref):
    for k, block in enumerate(blocks):
        out_ref[partner_rows(me_ref, k, block.shape[0]), :] = block[...]


def attend_kernel(
    per_group, ways, chunk, kv_local, me_ref, first_tile, low_ref, halo_ref, kv_ref, *refs
):
    blocks, refs = refs[:ways], refs[ways:]
    dq_ref, own_ref, rim_ref, qd_ref, k_ext, v_ext, k_t, dk_ext, dv_ext, s_buf, dp_buf = refs
    if ways == 1:
        qd_ref = blocks[0]
    else:
        gather_rows(me_ref, blocks, qd_ref)
    group = qd_ref.shape[0]
    reach = WINDOW // TK
    for ref, at in ((k_ext, chunk * HD), (v_ext, (kv_local + chunk) * HD)):
        ref[:WINDOW, :] = halo_ref[:, at : at + HD]
        ref[WINDOW:, :] = kv_ref[:, at : at + HD]
    dk_ext[...] = jnp.zeros_like(dk_ext)
    dv_ext[...] = jnp.zeros_like(dv_ext)

    def turn(t, carry):
        rows = pl.ds(pl.multiple_of(t * TK, TK), TK)
        k_t[t] = jnp.transpose(k_ext[rows, :].astype(jnp.float32)).astype(jnp.bfloat16)
        return carry

    lax.fori_loop(0, (group + WINDOW) // TK, turn, 0)
    wide = per_group * TQ
    key_iota = lax.broadcasted_iota(jnp.int32, (TK, wide), 0)

    def q_block(b, carry):
        q_rows = pl.ds(pl.multiple_of(b * TQ, TQ), TQ)
        start = first_tile[b]
        stop = b * (TQ // TK) + (TQ // TK - 1) + reach + 1
        q = jnp.concatenate(
            [qd_ref[q_rows, i * HD : (i + 1) * HD] for i in range(per_group)], axis=0
        )
        d_out = jnp.concatenate(
            [qd_ref[q_rows, i * HD : (i + 1) * HD] for i in range(per_group, 2 * per_group)],
            axis=0,
        )
        low = low_ref[:, q_rows]
        low = jnp.concatenate([low] * per_group, axis=1)
        high = b * TQ + WINDOW + lax.broadcasted_iota(jnp.int32, (1, TQ), 1)
        high = jnp.concatenate([high] * per_group, axis=1)

        def score(t, top):
            rows = pl.ds(pl.multiple_of(t * TK, TK), TK)
            slot = pl.ds(pl.multiple_of((t - start) * TK, TK), TK)
            s = dot_nt(k_ext[rows, :], q)
            j = key_iota + t * TK
            s = jnp.where((j >= low) & (j <= high), s, MASKED)
            s_buf[slot, :] = s
            return jnp.maximum(top, jnp.max(s, axis=0, keepdims=True))

        top = lax.fori_loop(start, stop, score, jnp.full((1, wide), MASKED, jnp.float32))

        def weigh(t, sums):
            total, dotted = sums
            rows = pl.ds(pl.multiple_of(t * TK, TK), TK)
            slot = pl.ds(pl.multiple_of((t - start) * TK, TK), TK)
            p = jnp.exp2((s_buf[slot, :] - top) * EXP2_SCALE)
            dp = dot_nt(v_ext[rows, :], d_out)
            s_buf[slot, :] = p
            dp_buf[slot, :] = dp
            return (
                total + jnp.sum(p, axis=0, keepdims=True),
                dotted + jnp.sum(p * dp, axis=0, keepdims=True),
            )

        zero = jnp.zeros((1, wide), jnp.float32)
        total, dotted = lax.fori_loop(start, stop, weigh, (zero, zero))
        inverse = 1.0 / total
        row_dot = dotted * inverse
        inverse_scaled = inverse * SCALING

        def grads(t, dq_t):
            rows = pl.ds(pl.multiple_of(t * TK, TK), TK)
            slot = pl.ds(pl.multiple_of((t - start) * TK, TK), TK)
            p = s_buf[slot, :]
            ds = ((p * inverse_scaled) * (dp_buf[slot, :] - row_dot)).astype(jnp.bfloat16)
            weights = (p * inverse).astype(jnp.bfloat16)
            dv_ext[rows, :] += dot_nn(weights, d_out)
            dk_ext[rows, :] += dot_nn(ds, q)
            return dq_t + dot_nn(k_t[t], ds)

        dq_t = lax.fori_loop(start, stop, grads, jnp.zeros((HD, wide), jnp.float32))
        dq = jnp.transpose(dq_t).astype(jnp.bfloat16)
        for i in range(per_group):
            dq_ref[q_rows, i * HD : (i + 1) * HD] = dq[i * TQ : (i + 1) * TQ, :]
        return carry

    lax.fori_loop(0, group // TQ, q_block, 0)
    rim_ref[:, :HD] = dk_ext[:WINDOW, :].astype(jnp.bfloat16)
    rim_ref[:, HD:] = dv_ext[:WINDOW, :].astype(jnp.bfloat16)
    own_ref[:, :HD] = dk_ext[WINDOW:, :]
    own_ref[:, HD:] = dv_ext[WINDOW:, :]


def attend(me, qd_blocks, halo, own, chunk, kv_local, low, first_tile):
    group = own.shape[0]
    tokens, qd_lanes = qd_blocks[0].shape
    ways = len(qd_blocks)
    per_group = qd_lanes // (2 * HD)
    ext = group + WINDOW
    wide = per_group * TQ
    span = WINDOW + TQ

    area = group * (WINDOW + TQ) * per_group
    outs = [
        jax.ShapeDtypeStruct((group, per_group * HD), jnp.bfloat16),
        jax.ShapeDtypeStruct((group, 2 * HD), jnp.float32),
        jax.ShapeDtypeStruct((WINDOW, 2 * HD), jnp.bfloat16),
    ]
    scratch = [
        jax.ShapeDtypeStruct((group, qd_lanes) if ways > 1 else (16, 128), jnp.bfloat16),
        jax.ShapeDtypeStruct((ext, HD), jnp.bfloat16),
        jax.ShapeDtypeStruct((ext, HD), jnp.bfloat16),
        jax.ShapeDtypeStruct((ext // TK, HD, TK), jnp.bfloat16),
        jax.ShapeDtypeStruct((ext, HD), jnp.float32),
        jax.ShapeDtypeStruct((ext, HD), jnp.float32),
        jax.ShapeDtypeStruct((span, wide), jnp.float32),
        jax.ShapeDtypeStruct((span, wide), jnp.float32),
    ]
    needed = array_bytes([low, halo, own, *qd_blocks, *outs, *scratch])
    return pl.pallas_call(
        functools.partial(attend_kernel, per_group, ways, chunk, kv_local),
        out_shape=tuple(outs),
        in_specs=[SMEM, SMEM] + [VMEM] * (3 + ways),
        out_specs=(VMEM,) * 3,
        scratch_shapes=[pltpu.VMEM(s.shape, s.dtype) for s in scratch],
        compiler_params=pltpu.CompilerParams(vmem_limit_bytes=needed + SPARE),
        cost_estimate=pl.CostEstimate(
            flops=area * HD * 2 * 5, bytes_accessed=group * HD * 24, transcendentals=area
        ),
        name="attend",
    )(me, first_tile, low, halo, own, *qd_blocks)


def on_chip(kernel, me, arrays, shapes, name, scratch=(), earlier=()):
    outs = tuple(jax.ShapeDtypeStruct(s, jnp.bfloat16) for s in shapes)
    moved = array_bytes([*arrays, *outs])

    def body(me_ref, *refs):
        kernel(me_ref, *refs[len(earlier) :])

    return pl.pallas_call(
        body,
        out_shape=outs,
        in_specs=[SMEM] + [ANYWHERE] * len(earlier) + [VMEM] * len(arrays),
        out_specs=(VMEM,) * len(shapes),
        scratch_shapes=list(scratch),
        compiler_params=pltpu.CompilerParams(vmem_limit_bytes=moved + SPARE),
        cost_estimate=pl.CostEstimate(flops=0, bytes_accessed=moved, transcendentals=0),
        name=name,
    )(me, *earlier, *arrays)


def packed(me, arrays, ways, chunk, chunks, by_partner, earlier=()):
    tokens = arrays[0].shape[0]
    lanes = [a.shape[1] // (ways * chunks) for a in arrays]
    total = sum(lanes)

    def kernel(me_ref, *refs):
        ins, outs = refs[: len(arrays)], refs[len(arrays) :]
        for k in range(ways):
            out = outs[k] if by_partner else outs[0].at[k]
            first = 0
            for ref, width in zip(ins, lanes):
                if by_partner:
                    at = pl.multiple_of(((me_ref[0] ^ k) * chunks + chunk) * width, width)
                else:
                    at = (k * chunks + chunk) * width
                out[:, first : first + width] = ref[:, pl.ds(at, width)]
                first += width

    shapes = [(tokens, total)] * ways if by_partner else [(ways, tokens, total)]
    return on_chip(kernel, me, arrays, shapes, "packed", earlier=earlier)


def unpacked(me, grads, ways, q_lanes):
    chunks = len(grads)
    tokens = grads[0][0].shape[-2]
    lanes = (q_lanes, HD, HD)
    counts = [len(blocks) for blocks in grads]

    def kernel(me_ref, *refs):
        outs = refs[sum(counts) :]
        for c in range(chunks):
            ins = refs[sum(counts[:c]) : sum(counts[: c + 1])]
            for k in range(ways):
                block = ins[k] if len(ins) > 1 else ins[0].at[k]
                first = 0
                for out, width in zip(outs, lanes):
                    if len(ins) > 1:
                        at = pl.multiple_of(((me_ref[0] ^ k) * chunks + c) * width, width)
                    else:
                        at = (k * chunks + c) * width
                    out[:, pl.ds(at, width)] = block[:, first : first + width]
                    first += width

    shapes = [(tokens, ways * chunks * width) for width in lanes]
    return on_chip(kernel, me, [g for blocks in grads for g in blocks], shapes, "unpacked")


def gathered(me, blocks):
    tokens, lanes = blocks[0].shape
    ways = len(blocks)
    group = ways * tokens

    def kernel(me_ref, *refs):
        all_ref, tail_ref = refs[ways:]
        gather_rows(me_ref, refs[:ways], all_ref)
        tail_ref[...] = all_ref[group - WINDOW :, :]

    return on_chip(kernel, me, blocks, [(group, lanes), (WINDOW, lanes)], "gathered")


def settled(me, dq, own, returned, ways, by_partner):
    group, q_lanes = dq.shape
    tokens = group // ways
    total_lanes = q_lanes + 2 * HD

    def kernel(me_ref, dq_ref, own_ref, back_ref, *refs):
        cut = group - WINDOW
        total = refs[-1] if by_partner else refs[0].at[:, q_lanes:]
        total[:cut, :] = own_ref[:cut, :].astype(jnp.bfloat16)
        total[cut:, :] = (own_ref[cut:, :] + back_ref[...].astype(jnp.float32)).astype(jnp.bfloat16)
        if not by_partner:
            refs[0][:, :q_lanes] = dq_ref[...]
            return
        for k, out in enumerate(refs[:ways]):
            rows = partner_rows(me_ref, k, tokens)
            out[:, :q_lanes] = dq_ref[rows, :]
            out[:, q_lanes:] = total[rows, :]

    shapes = [(tokens, total_lanes)] * ways if by_partner else [(group, total_lanes)]
    scratch = [pltpu.VMEM((group, 2 * HD), jnp.bfloat16)] if by_partner else []
    return on_chip(kernel, me, (dq, own, returned), shapes, "settled", scratch)


def exchanged(blocks):
    ways = len(blocks)
    came = {0: blocks[0]}
    for k in reversed(range(1, ways)):
        came[k] = lax.ppermute(blocks[k], "head", [(i, i ^ k) for i in range(ways)])
    return [came[k] for k in range(ways)]


def exchanged_at_once(sent):
    return lax.all_to_all(sent, "head", split_axis=0, concat_axis=0, tiled=True)


def local(queries, keys, values, grad_out, doc_lengths):
    ways = lax.axis_size("head")
    tokens = queries.shape[0]
    group = tokens * ways
    kv_local = keys.shape[1] // (ways * HD)
    per_group = queries.shape[1] // keys.shape[1]
    q_lanes = per_group * HD
    group_first = lax.axis_index("seq") * group
    me = lax.axis_index("head").astype(jnp.int32).reshape(1)

    came = exchanged(packed(me, (keys, values), ways, 0, 1, True))
    kv, tail = gathered(me, came)
    halo = passed_along(tail, "seq", 1)
    qds = [
        exchanged(packed(me, (queries, grad_out), ways, 0, kv_local, True, [came[ways - 2]]))
    ]
    for c in range(1, kv_local):
        earlier = [*qds[-1][min(1, len(qds[-1]) - 1) :], halo]
        sent = packed(me, (queries, grad_out), ways, c, kv_local, False, earlier)[0]
        qds.append([exchanged_at_once(sent).reshape(group, 2 * q_lanes)])

    position = group_first + jnp.arange(group, dtype=jnp.int32)
    ends = jnp.cumsum(doc_lengths)
    doc_start = jnp.sum(
        jnp.where(position[:, None] >= ends[None, :], doc_lengths[None, :], 0), axis=1
    )
    low = jnp.maximum(doc_start, position - (WINDOW - 1)) - (group_first - WINDOW)
    low = low.astype(jnp.int32)
    first_tile = low[::TQ] // TK

    grads = []
    for c in range(kv_local):
        dq, own, rim = attend(me, qds[c], halo, kv, c, kv_local, low.reshape(1, group), first_tile)
        returned = passed_along(rim, "seq", -1)
        last = c == kv_local - 1
        settled_now = settled(me, dq, own, returned, ways, last)
        if last:
            grads.append(exchanged(settled_now))
        else:
            sent = settled_now[0].reshape(ways, tokens, q_lanes + 2 * HD)
            grads.append([exchanged_at_once(sent)])
    return unpacked(me, grads, ways, q_lanes)


def solution(mesh):
    rows = P(("seq", "head"), None)
    return jax.shard_map(
        local,
        mesh=mesh,
        in_specs=(rows, rows, rows, rows, P()),
        out_specs=(rows, rows, rows),
        check_vma=False,
    )
```

```python
import functools
import math

import jax
import jax.numpy as jnp
from jax import lax
from jax.experimental import pallas as pl
from jax.experimental.pallas import tpu as pltpu
from jax.sharding import PartitionSpec as P

HD = 128
WINDOW = 1024
TQ = TK = 256
SCALING = HD ** (-0.5)
EXP2_SCALE = SCALING * math.log2(math.e)
MASKED = -1e30
SPARE = 4 * 1024 * 1024
SMEM = pl.BlockSpec(memory_space=pltpu.SMEM)
VMEM = pl.BlockSpec(memory_space=pltpu.VMEM)


def array_bytes(arrays):
    return sum(math.prod(a.shape) * a.dtype.itemsize for a in arrays)


def passed_along(shard, axis, by):
    count = lax.axis_size(axis)
    pairs = [(i, i + by) for i in range(count) if 0 <= i + by < count]
    return lax.ppermute(shard, axis, pairs)


def dot_nt(a, b):
    return lax.dot_general(a, b, (((1,), (1,)), ((), ())), preferred_element_type=jnp.float32)


def dot_nn(a, b):
    return lax.dot_general(a, b, (((1,), (0,)), ((), ())), preferred_element_type=jnp.float32)


def partner_rows(me_ref, k, tokens):
    return pl.ds(pl.multiple_of((me_ref[0] ^ k) * tokens, tokens), tokens)


def gather_rows(me_ref, blocks, out_ref):
    for k, block in enumerate(blocks):
        out_ref[partner_rows(me_ref, k, block.shape[0]), :] = block[...]


def attend_kernel(
    per_group, ways, chunk, kv_local, me_ref, first_tile, low_ref, halo_ref, kv_ref, *refs
):
    blocks, refs = refs[:ways], refs[ways:]
    dq_ref, own_ref, rim_ref, qd_ref, k_ext, v_ext, k_t, dk_ext, dv_ext, s_buf, dp_buf = refs
    if ways == 1:
        qd_ref = blocks[0]
    else:
        gather_rows(me_ref, blocks, qd_ref)
    group = qd_ref.shape[0]
    reach = WINDOW // TK
    for ref, at in ((k_ext, chunk * HD), (v_ext, (kv_local + chunk) * HD)):
        ref[:WINDOW, :] = halo_ref[:, at : at + HD]
        ref[WINDOW:, :] = kv_ref[:, at : at + HD]
    dk_ext[...] = jnp.zeros_like(dk_ext)
    dv_ext[...] = jnp.zeros_like(dv_ext)

    def turn(t, carry):
        rows = pl.ds(pl.multiple_of(t * TK, TK), TK)
        k_t[t] = jnp.transpose(k_ext[rows, :].astype(jnp.float32)).astype(jnp.bfloat16)
        return carry

    lax.fori_loop(0, (group + WINDOW) // TK, turn, 0)
    wide = per_group * TQ
    key_iota = lax.broadcasted_iota(jnp.int32, (TK, wide), 0)
    query_iota = lax.broadcasted_iota(jnp.int32, (1, TQ), 1)
    diagonal = jnp.concatenate([query_iota] * per_group, axis=1)

    def q_block(b, tiles):
        q_rows = pl.ds(pl.multiple_of(b * TQ, TQ), TQ)
        first = b + reach + 1 - tiles
        q = jnp.concatenate(
            [qd_ref[q_rows, i * HD : (i + 1) * HD] for i in range(per_group)], axis=0
        )
        d_out = jnp.concatenate(
            [qd_ref[q_rows, i * HD : (i + 1) * HD] for i in range(per_group, 2 * per_group)],
            axis=0,
        )
        low = jnp.concatenate([low_ref[:, q_rows]] * per_group, axis=1) - first * TK
        key_rows = [pl.ds(pl.multiple_of((first + t) * TK, TK), TK) for t in range(tiles)]
        slots = [slice(t * TK, (t + 1) * TK) for t in range(tiles)]

        top = jnp.full((1, wide), MASKED, jnp.float32)
        for t in range(tiles):
            s = dot_nt(k_ext[key_rows[t], :], q)
            allowed = key_iota >= low - t * TK
            if t == tiles - 1:
                allowed = allowed & (key_iota <= diagonal)
            s = jnp.where(allowed, s, MASKED)
            s_buf[slots[t], :] = s
            top = jnp.maximum(top, jnp.max(s, axis=0, keepdims=True))

        total = jnp.zeros((1, wide), jnp.float32)
        dotted = jnp.zeros((1, wide), jnp.float32)
        for t in range(tiles):
            p = jnp.exp2((s_buf[slots[t], :] - top) * EXP2_SCALE)
            dp = dot_nt(v_ext[key_rows[t], :], d_out)
            s_buf[slots[t], :] = p
            dp_buf[slots[t], :] = dp
            total += jnp.sum(p, axis=0, keepdims=True)
            dotted += jnp.sum(p * dp, axis=0, keepdims=True)
        inverse = 1.0 / total
        row_dot = dotted * inverse

        dq_t = jnp.zeros((HD, wide), jnp.float32)
        for t in range(tiles):
            weights = s_buf[slots[t], :] * inverse
            ds = (weights * (dp_buf[slots[t], :] - row_dot)).astype(jnp.bfloat16)
            dv_ext[key_rows[t], :] += dot_nn(weights.astype(jnp.bfloat16), d_out)
            dk_ext[key_rows[t], :] += dot_nn(ds, q)
            dq_t += dot_nn(k_t[first + t], ds)

        dq = jnp.transpose(dq_t * SCALING).astype(jnp.bfloat16)
        for i in range(per_group):
            dq_ref[q_rows, i * HD : (i + 1) * HD] = dq[i * TQ : (i + 1) * TQ, :]

    def any_block(b, carry):
        tiles = b + reach + 1 - first_tile[b]
        for count in range(1, reach + 2):
            pl.when(tiles == count)(functools.partial(q_block, b, count))
        return carry

    lax.fori_loop(0, group // TQ, any_block, 0)
    rim_ref[:, :HD] = (dk_ext[:WINDOW, :] * SCALING).astype(jnp.bfloat16)
    rim_ref[:, HD:] = dv_ext[:WINDOW, :].astype(jnp.bfloat16)
    own_ref[:, :HD] = dk_ext[WINDOW:, :] * SCALING
    own_ref[:, HD:] = dv_ext[WINDOW:, :]


def attend(me, qd_blocks, halo, own, chunk, kv_local, low, first_tile):
    group = own.shape[0]
    tokens, qd_lanes = qd_blocks[0].shape
    ways = len(qd_blocks)
    per_group = qd_lanes // (2 * HD)
    ext = group + WINDOW
    wide = per_group * TQ
    span = WINDOW + TQ

    area = group * (WINDOW + TQ) * per_group
    outs = [
        jax.ShapeDtypeStruct((group, per_group * HD), jnp.bfloat16),
        jax.ShapeDtypeStruct((group, 2 * HD), jnp.float32),
        jax.ShapeDtypeStruct((WINDOW, 2 * HD), jnp.bfloat16),
    ]
    scratch = [
        jax.ShapeDtypeStruct((group, qd_lanes) if ways > 1 else (16, 128), jnp.bfloat16),
        jax.ShapeDtypeStruct((ext, HD), jnp.bfloat16),
        jax.ShapeDtypeStruct((ext, HD), jnp.bfloat16),
        jax.ShapeDtypeStruct((ext // TK, HD, TK), jnp.bfloat16),
        jax.ShapeDtypeStruct((ext, HD), jnp.float32),
        jax.ShapeDtypeStruct((ext, HD), jnp.float32),
        jax.ShapeDtypeStruct((span, wide), jnp.float32),
        jax.ShapeDtypeStruct((span, wide), jnp.float32),
    ]
    needed = array_bytes([low, halo, own, *qd_blocks, *outs, *scratch])
    return pl.pallas_call(
        functools.partial(attend_kernel, per_group, ways, chunk, kv_local),
        out_shape=tuple(outs),
        in_specs=[SMEM, SMEM] + [VMEM] * (3 + ways),
        out_specs=(VMEM,) * 3,
        scratch_shapes=[pltpu.VMEM(s.shape, s.dtype) for s in scratch],
        compiler_params=pltpu.CompilerParams(vmem_limit_bytes=needed + SPARE),
        cost_estimate=pl.CostEstimate(
            flops=area * HD * 2 * 5, bytes_accessed=group * HD * 24, transcendentals=area
        ),
        name="attend",
    )(me, first_tile, low, halo, own, *qd_blocks)


def on_chip(kernel, me, arrays, shapes, name, scratch=(), earlier=()):
    outs = tuple(jax.ShapeDtypeStruct(s, jnp.bfloat16) for s in shapes)
    moved = array_bytes([*arrays, *earlier, *outs])

    def body(me_ref, *refs):
        kernel(me_ref, *refs[len(earlier) :])

    return pl.pallas_call(
        body,
        out_shape=outs,
        in_specs=[SMEM] + [VMEM] * (len(earlier) + len(arrays)),
        out_specs=(VMEM,) * len(shapes),
        scratch_shapes=list(scratch),
        compiler_params=pltpu.CompilerParams(vmem_limit_bytes=moved + SPARE),
        cost_estimate=pl.CostEstimate(flops=0, bytes_accessed=moved, transcendentals=0),
        name=name,
    )(me, *earlier, *arrays)


def packed(me, arrays, ways, chunk, chunks, by_partner, earlier=()):
    tokens = arrays[0].shape[0]
    lanes = [a.shape[1] // (ways * chunks) for a in arrays]
    total = sum(lanes)

    def kernel(me_ref, *refs):
        ins, outs = refs[: len(arrays)], refs[len(arrays) :]
        for k in range(ways):
            out = outs[k] if by_partner else outs[0].at[k]
            first = 0
            for ref, width in zip(ins, lanes):
                if by_partner:
                    at = pl.multiple_of(((me_ref[0] ^ k) * chunks + chunk) * width, width)
                else:
                    at = (k * chunks + chunk) * width
                out[:, first : first + width] = ref[:, pl.ds(at, width)]
                first += width

    shapes = [(tokens, total)] * ways if by_partner else [(ways, tokens, total)]
    return on_chip(kernel, me, arrays, shapes, "packed", earlier=earlier)


def unpacked(me, grads, ways, q_lanes):
    chunks = len(grads)
    tokens = grads[0][0].shape[-2]
    lanes = (q_lanes, HD, HD)
    counts = [len(blocks) for blocks in grads]

    def kernel(me_ref, *refs):
        outs = refs[sum(counts) :]
        for c in range(chunks):
            ins = refs[sum(counts[:c]) : sum(counts[: c + 1])]
            for k in range(ways):
                block = ins[k] if len(ins) > 1 else ins[0].at[k]
                first = 0
                for out, width in zip(outs, lanes):
                    if len(ins) > 1:
                        at = pl.multiple_of(((me_ref[0] ^ k) * chunks + c) * width, width)
                    else:
                        at = (k * chunks + c) * width
                    out[:, pl.ds(at, width)] = block[:, first : first + width]
                    first += width

    shapes = [(tokens, ways * chunks * width) for width in lanes]
    return on_chip(kernel, me, [g for blocks in grads for g in blocks], shapes, "unpacked")


def gathered(me, blocks):
    tokens, lanes = blocks[0].shape
    ways = len(blocks)
    group = ways * tokens

    def kernel(me_ref, *refs):
        all_ref, tail_ref = refs[ways:]
        gather_rows(me_ref, refs[:ways], all_ref)
        tail_ref[...] = all_ref[group - WINDOW :, :]

    return on_chip(kernel, me, blocks, [(group, lanes), (WINDOW, lanes)], "gathered")


def settled(me, dq, own, returned, ways, by_partner):
    group, q_lanes = dq.shape
    tokens = group // ways
    total_lanes = q_lanes + 2 * HD

    def kernel(me_ref, dq_ref, own_ref, back_ref, *refs):
        cut = group - WINDOW
        total = refs[-1] if by_partner else refs[0].at[:, q_lanes:]
        total[:cut, :] = own_ref[:cut, :].astype(jnp.bfloat16)
        total[cut:, :] = (own_ref[cut:, :] + back_ref[...].astype(jnp.float32)).astype(jnp.bfloat16)
        if not by_partner:
            refs[0][:, :q_lanes] = dq_ref[...]
            return
        for k, out in enumerate(refs[:ways]):
            rows = partner_rows(me_ref, k, tokens)
            out[:, :q_lanes] = dq_ref[rows, :]
            out[:, q_lanes:] = total[rows, :]

    shapes = [(tokens, total_lanes)] * ways if by_partner else [(group, total_lanes)]
    scratch = [pltpu.VMEM((group, 2 * HD), jnp.bfloat16)] if by_partner else []
    return on_chip(kernel, me, (dq, own, returned), shapes, "settled", scratch)


def exchanged(blocks):
    ways = len(blocks)
    came = {0: blocks[0]}
    for k in reversed(range(1, ways)):
        came[k] = lax.ppermute(blocks[k], "head", [(i, i ^ k) for i in range(ways)])
    return [came[k] for k in range(ways)]


def exchanged_at_once(sent):
    return lax.all_to_all(sent, "head", split_axis=0, concat_axis=0, tiled=True)


def local(queries, keys, values, grad_out, doc_lengths):
    ways = lax.axis_size("head")
    tokens = queries.shape[0]
    group = tokens * ways
    kv_local = keys.shape[1] // (ways * HD)
    per_group = queries.shape[1] // keys.shape[1]
    q_lanes = per_group * HD
    group_first = lax.axis_index("seq") * group
    me = lax.axis_index("head").astype(jnp.int32).reshape(1)

    came = exchanged(packed(me, (keys, values), ways, 0, 1, True))
    kv, tail = gathered(me, came)
    halo = passed_along(tail, "seq", 1)
    qds = [
        exchanged(packed(me, (queries, grad_out), ways, 0, kv_local, True, [came[1]]))
    ]
    for c in range(1, kv_local):
        earlier = [*qds[-1][-2:], halo]
        sent = packed(me, (queries, grad_out), ways, c, kv_local, False, earlier)[0]
        qds.append([exchanged_at_once(sent).reshape(group, 2 * q_lanes)])

    position = group_first + jnp.arange(group, dtype=jnp.int32)
    ends = jnp.cumsum(doc_lengths)
    doc_start = jnp.sum(
        jnp.where(position[:, None] >= ends[None, :], doc_lengths[None, :], 0), axis=1
    )
    low = jnp.maximum(doc_start, position - (WINDOW - 1)) - (group_first - WINDOW)
    low = low.astype(jnp.int32)
    first_tile = low[::TQ] // TK

    grads = []
    for c in range(kv_local):
        dq, own, rim = attend(me, qds[c], halo, kv, c, kv_local, low.reshape(1, group), first_tile)
        returned = passed_along(rim, "seq", -1)
        last = c == kv_local - 1
        settled_now = settled(me, dq, own, returned, ways, last)
        if last:
            grads.append(exchanged(settled_now))
        else:
            sent = settled_now[0].reshape(ways, tokens, q_lanes + 2 * HD)
            grads.append([exchanged_at_once(sent)])
    return unpacked(me, grads, ways, q_lanes)


def solution(mesh):
    rows = P(("seq", "head"), None)
    return jax.shard_map(
        local,
        mesh=mesh,
        in_specs=(rows, rows, rows, rows, P()),
        out_specs=(rows, rows, rows),
        check_vma=False,
    )
```

```python
import functools
import math

import jax
import jax.numpy as jnp
from jax import lax
from jax.experimental import pallas as pl
from jax.experimental.pallas import tpu as pltpu
from jax.sharding import PartitionSpec as P

HD = 128
WINDOW = 1024
TQ = TK = 256
SCALING = HD ** (-0.5)
EXP2_SCALE = SCALING * math.log2(math.e)
MASKED = -1e30
SPARE = 4 * 1024 * 1024
SMEM = pl.BlockSpec(memory_space=pltpu.SMEM)
VMEM = pl.BlockSpec(memory_space=pltpu.VMEM)


def array_bytes(arrays):
    return sum(math.prod(a.shape) * a.dtype.itemsize for a in arrays)


def passed_along(shard, axis, by):
    count = lax.axis_size(axis)
    pairs = [(i, i + by) for i in range(count) if 0 <= i + by < count]
    return lax.ppermute(shard, axis, pairs)


def dot_nt(a, b):
    return lax.dot_general(a, b, (((1,), (1,)), ((), ())), preferred_element_type=jnp.float32)


def dot_nn(a, b):
    return lax.dot_general(a, b, (((1,), (0,)), ((), ())), preferred_element_type=jnp.float32)


def partner_rows(me_ref, k, tokens):
    return pl.ds(pl.multiple_of((me_ref[0] ^ k) * tokens, tokens), tokens)


def gather_rows(me_ref, blocks, out_ref):
    for k, block in enumerate(blocks):
        out_ref[partner_rows(me_ref, k, block.shape[0]), :] = block[...]


def attend_kernel(
    per_group, ways, chunk, kv_local, me_ref, first_tile, low_ref, halo_ref, kv_ref, *refs
):
    blocks, refs = refs[:ways], refs[ways:]
    dq_ref, own_ref, rim_ref, qd_ref, k_ext, v_ext, k_t, dk_ext, dv_ext, s_buf, dp_buf = refs
    if ways == 1:
        qd_ref = blocks[0]
    else:
        gather_rows(me_ref, blocks, qd_ref)
    group = qd_ref.shape[0]
    reach = WINDOW // TK
    for ref, at in ((k_ext, chunk * HD), (v_ext, (kv_local + chunk) * HD)):
        ref[:WINDOW, :] = halo_ref[:, at : at + HD]
        ref[WINDOW:, :] = kv_ref[:, at : at + HD]
    dk_ext[...] = jnp.zeros_like(dk_ext)
    dv_ext[...] = jnp.zeros_like(dv_ext)

    def turn(t, carry):
        rows = pl.ds(pl.multiple_of(t * TK, TK), TK)
        k_t[t] = jnp.transpose(k_ext[rows, :].astype(jnp.float32)).astype(jnp.bfloat16)
        return carry

    lax.fori_loop(0, (group + WINDOW) // TK, turn, 0)
    wide = per_group * TQ
    key_iota = lax.broadcasted_iota(jnp.int32, (TK, wide), 0)
    query_iota = lax.broadcasted_iota(jnp.int32, (1, TQ), 1)
    diagonal = jnp.concatenate([query_iota] * per_group, axis=1)

    def q_block(b, tiles):
        q_rows = pl.ds(pl.multiple_of(b * TQ, TQ), TQ)
        first = b + reach + 1 - tiles
        q = jnp.concatenate(
            [qd_ref[q_rows, i * HD : (i + 1) * HD] for i in range(per_group)], axis=0
        )
        d_out = jnp.concatenate(
            [qd_ref[q_rows, i * HD : (i + 1) * HD] for i in range(per_group, 2 * per_group)],
            axis=0,
        )
        low = jnp.concatenate([low_ref[:, q_rows]] * per_group, axis=1) - first * TK
        key_rows = [pl.ds(pl.multiple_of((first + t) * TK, TK), TK) for t in range(tiles)]
        slots = [slice(t * TK, (t + 1) * TK) for t in range(tiles)]

        top = jnp.full((1, wide), MASKED, jnp.float32)
        for t in range(tiles):
            s = dot_nt(k_ext[key_rows[t], :], q)
            allowed = key_iota >= low - t * TK
            if t == tiles - 1:
                allowed = allowed & (key_iota <= diagonal)
            s = jnp.where(allowed, s, MASKED)
            s_buf[slots[t], :] = s
            top = jnp.maximum(top, jnp.max(s, axis=0, keepdims=True))

        total = jnp.zeros((1, wide), jnp.float32)
        dotted = jnp.zeros((1, wide), jnp.float32)
        for t in range(tiles):
            p = jnp.exp2((s_buf[slots[t], :] - top) * EXP2_SCALE)
            dp = dot_nt(v_ext[key_rows[t], :], d_out)
            s_buf[slots[t], :] = p
            dp_buf[slots[t], :] = dp
            total += jnp.sum(p, axis=0, keepdims=True)
            dotted += jnp.sum(p * dp, axis=0, keepdims=True)
        inverse = 1.0 / total
        row_dot = dotted * inverse

        dq_t = jnp.zeros((HD, wide), jnp.float32)
        for t in range(tiles):
            weights = s_buf[slots[t], :] * inverse
            ds = (weights * (dp_buf[slots[t], :] - row_dot)).astype(jnp.bfloat16)
            dv_ext[key_rows[t], :] += dot_nn(weights.astype(jnp.bfloat16), d_out)
            dk_ext[key_rows[t], :] += dot_nn(ds, q)
            dq_t += dot_nn(k_t[first + t], ds)

        dq = jnp.transpose(dq_t * SCALING).astype(jnp.bfloat16)
        for i in range(per_group):
            dq_ref[q_rows, i * HD : (i + 1) * HD] = dq[i * TQ : (i + 1) * TQ, :]

    def any_block(b, carry):
        tiles = b + reach + 1 - first_tile[b]
        for count in range(1, reach + 2):
            pl.when(tiles == count)(functools.partial(q_block, b, count))
        return carry

    lax.fori_loop(0, group // TQ, any_block, 0)
    rim_ref[:, :HD] = (dk_ext[:WINDOW, :] * SCALING).astype(jnp.bfloat16)
    rim_ref[:, HD:] = dv_ext[:WINDOW, :].astype(jnp.bfloat16)
    own_ref[:, :HD] = dk_ext[WINDOW:, :] * SCALING
    own_ref[:, HD:] = dv_ext[WINDOW:, :]


def attend(me, qd_blocks, halo, own, chunk, kv_local, low, first_tile):
    group = own.shape[0]
    tokens, qd_lanes = qd_blocks[0].shape
    ways = len(qd_blocks)
    per_group = qd_lanes // (2 * HD)
    ext = group + WINDOW
    wide = per_group * TQ
    span = WINDOW + TQ

    area = group * (WINDOW + TQ) * per_group
    outs = [
        jax.ShapeDtypeStruct((group, per_group * HD), jnp.bfloat16),
        jax.ShapeDtypeStruct((group, 2 * HD), jnp.float32),
        jax.ShapeDtypeStruct((WINDOW, 2 * HD), jnp.bfloat16),
    ]
    scratch = [
        jax.ShapeDtypeStruct((group, qd_lanes) if ways > 1 else (16, 128), jnp.bfloat16),
        jax.ShapeDtypeStruct((ext, HD), jnp.bfloat16),
        jax.ShapeDtypeStruct((ext, HD), jnp.bfloat16),
        jax.ShapeDtypeStruct((ext // TK, HD, TK), jnp.bfloat16),
        jax.ShapeDtypeStruct((ext, HD), jnp.float32),
        jax.ShapeDtypeStruct((ext, HD), jnp.float32),
        jax.ShapeDtypeStruct((span, wide), jnp.float32),
        jax.ShapeDtypeStruct((span, wide), jnp.float32),
    ]
    needed = array_bytes([low, halo, own, *qd_blocks, *outs, *scratch])
    return pl.pallas_call(
        functools.partial(attend_kernel, per_group, ways, chunk, kv_local),
        out_shape=tuple(outs),
        in_specs=[SMEM, SMEM] + [VMEM] * (3 + ways),
        out_specs=(VMEM,) * 3,
        scratch_shapes=[pltpu.VMEM(s.shape, s.dtype) for s in scratch],
        compiler_params=pltpu.CompilerParams(vmem_limit_bytes=needed + SPARE),
        cost_estimate=pl.CostEstimate(
            flops=area * HD * 2 * 5, bytes_accessed=group * HD * 24, transcendentals=area
        ),
        name="attend",
    )(me, first_tile, low, halo, own, *qd_blocks)


def on_chip(kernel, me, arrays, shapes, name, scratch=(), earlier=()):
    outs = tuple(jax.ShapeDtypeStruct(s, jnp.bfloat16) for s in shapes)
    moved = array_bytes([*arrays, *earlier, *outs])

    def body(me_ref, *refs):
        kernel(me_ref, *refs[len(earlier) :])

    return pl.pallas_call(
        body,
        out_shape=outs,
        in_specs=[SMEM] + [VMEM] * (len(earlier) + len(arrays)),
        out_specs=(VMEM,) * len(shapes),
        scratch_shapes=list(scratch),
        compiler_params=pltpu.CompilerParams(vmem_limit_bytes=moved + SPARE),
        cost_estimate=pl.CostEstimate(flops=0, bytes_accessed=moved, transcendentals=0),
        name=name,
    )(me, *earlier, *arrays)


def packed(me, arrays, ways, chunk, chunks, by_partner, earlier=()):
    tokens = arrays[0].shape[0]
    lanes = [a.shape[1] // (ways * chunks) for a in arrays]
    total = sum(lanes)

    def kernel(me_ref, *refs):
        ins, outs = refs[: len(arrays)], refs[len(arrays) :]
        for k in range(ways):
            out = outs[k] if by_partner else outs[0].at[k]
            first = 0
            for ref, width in zip(ins, lanes):
                if by_partner:
                    at = pl.multiple_of(((me_ref[0] ^ k) * chunks + chunk) * width, width)
                else:
                    at = (k * chunks + chunk) * width
                out[:, first : first + width] = ref[:, pl.ds(at, width)]
                first += width

    shapes = [(tokens, total)] * ways if by_partner else [(ways, tokens, total)]
    return on_chip(kernel, me, arrays, shapes, "packed", earlier=earlier)


def unpacked(me, grads, ways, q_lanes):
    chunks = len(grads)
    tokens = grads[0][0].shape[-2]
    lanes = (q_lanes, HD, HD)
    counts = [len(blocks) for blocks in grads]

    def kernel(me_ref, *refs):
        outs = refs[sum(counts) :]
        for c in range(chunks):
            ins = refs[sum(counts[:c]) : sum(counts[: c + 1])]
            for k in range(ways):
                block = ins[k] if len(ins) > 1 else ins[0].at[k]
                first = 0
                for out, width in zip(outs, lanes):
                    if len(ins) > 1:
                        at = pl.multiple_of(((me_ref[0] ^ k) * chunks + c) * width, width)
                    else:
                        at = (k * chunks + c) * width
                    out[:, pl.ds(at, width)] = block[:, first : first + width]
                    first += width

    shapes = [(tokens, ways * chunks * width) for width in lanes]
    return on_chip(kernel, me, [g for blocks in grads for g in blocks], shapes, "unpacked")


def gathered(me, blocks):
    tokens, lanes = blocks[0].shape
    ways = len(blocks)
    group = ways * tokens

    def kernel(me_ref, *refs):
        all_ref, tail_ref = refs[ways:]
        gather_rows(me_ref, refs[:ways], all_ref)
        tail_ref[...] = all_ref[group - WINDOW :, :]

    return on_chip(kernel, me, blocks, [(group, lanes), (WINDOW, lanes)], "gathered")


def settled(me, dq, own, returned, ways, by_partner):
    group, q_lanes = dq.shape
    tokens = group // ways
    total_lanes = q_lanes + 2 * HD

    def kernel(me_ref, dq_ref, own_ref, back_ref, *refs):
        cut = group - WINDOW
        total = refs[-1] if by_partner else refs[0].at[:, q_lanes:]
        total[:cut, :] = own_ref[:cut, :].astype(jnp.bfloat16)
        total[cut:, :] = (own_ref[cut:, :] + back_ref[...].astype(jnp.float32)).astype(jnp.bfloat16)
        if not by_partner:
            refs[0][:, :q_lanes] = dq_ref[...]
            return
        for k, out in enumerate(refs[:ways]):
            rows = partner_rows(me_ref, k, tokens)
            out[:, :q_lanes] = dq_ref[rows, :]
            out[:, q_lanes:] = total[rows, :]

    shapes = [(tokens, total_lanes)] * ways if by_partner else [(group, total_lanes)]
    scratch = [pltpu.VMEM((group, 2 * HD), jnp.bfloat16)] if by_partner else []
    return on_chip(kernel, me, (dq, own, returned), shapes, "settled", scratch)


def exchanged(blocks):
    ways = len(blocks)
    came = {0: blocks[0]}
    for k in reversed(range(1, ways)):
        came[k] = lax.ppermute(blocks[k], "head", [(i, i ^ k) for i in range(ways)])
    return [came[k] for k in range(ways)]


def exchanged_at_once(sent):
    return lax.all_to_all(sent, "head", split_axis=0, concat_axis=0, tiled=True)


def local(queries, keys, values, grad_out, doc_lengths):
    ways = lax.axis_size("head")
    tokens = queries.shape[0]
    group = tokens * ways
    kv_local = keys.shape[1] // (ways * HD)
    per_group = queries.shape[1] // keys.shape[1]
    q_lanes = per_group * HD
    group_first = lax.axis_index("seq") * group
    me = lax.axis_index("head").astype(jnp.int32).reshape(1)

    came = exchanged(packed(me, (keys, values), ways, 0, 1, True))
    kv, tail = gathered(me, came)
    halo = passed_along(tail, "seq", 1)
    qds = [
        exchanged(packed(me, (queries, grad_out), ways, 0, kv_local, True, [came[1]]))
    ]
    for c in range(1, kv_local):
        earlier = [*qds[-1][-(ways - 1) :], halo]
        sent = packed(me, (queries, grad_out), ways, c, kv_local, False, earlier)[0]
        qds.append([exchanged_at_once(sent).reshape(group, 2 * q_lanes)])

    position = group_first + jnp.arange(group, dtype=jnp.int32)
    ends = jnp.cumsum(doc_lengths)
    doc_start = jnp.sum(
        jnp.where(position[:, None] >= ends[None, :], doc_lengths[None, :], 0), axis=1
    )
    low = jnp.maximum(doc_start, position - (WINDOW - 1)) - (group_first - WINDOW)
    low = low.astype(jnp.int32)
    first_tile = low[::TQ] // TK

    grads = []
    for c in range(kv_local):
        dq, own, rim = attend(me, qds[c], halo, kv, c, kv_local, low.reshape(1, group), first_tile)
        returned = passed_along(rim, "seq", -1)
        last = c == kv_local - 1
        settled_now = settled(me, dq, own, returned, ways, last)
        if last:
            grads.append(exchanged(settled_now))
        else:
            sent = settled_now[0].reshape(ways, tokens, q_lanes + 2 * HD)
            grads.append([exchanged_at_once(sent)])
    return unpacked(me, grads, ways, q_lanes)


def solution(mesh):
    rows = P(("seq", "head"), None)
    return jax.shard_map(
        local,
        mesh=mesh,
        in_specs=(rows, rows, rows, rows, P()),
        out_specs=(rows, rows, rows),
        check_vma=False,
    )
```

```python
import functools
import math

import jax
import jax.numpy as jnp
from jax import lax
from jax.experimental import pallas as pl
from jax.experimental.pallas import tpu as pltpu
from jax.sharding import PartitionSpec as P

HD = 128
WINDOW = 1024
TQ = TK = 256
SCALING = HD ** (-0.5)
EXP2_SCALE = SCALING * math.log2(math.e)
MASKED = -1e30
SPARE = 4 * 1024 * 1024
SMEM = pl.BlockSpec(memory_space=pltpu.SMEM)
VMEM = pl.BlockSpec(memory_space=pltpu.VMEM)


def array_bytes(arrays):
    return sum(math.prod(a.shape) * a.dtype.itemsize for a in arrays)


def passed_along(shard, axis, by):
    count = lax.axis_size(axis)
    pairs = [(i, i + by) for i in range(count) if 0 <= i + by < count]
    return lax.ppermute(shard, axis, pairs)


def dot_nt(a, b):
    return lax.dot_general(a, b, (((1,), (1,)), ((), ())), preferred_element_type=jnp.float32)


def dot_nn(a, b):
    return lax.dot_general(a, b, (((1,), (0,)), ((), ())), preferred_element_type=jnp.float32)


def partner_rows(me_ref, k, tokens):
    return pl.ds(pl.multiple_of((me_ref[0] ^ k) * tokens, tokens), tokens)


def gather_rows(me_ref, blocks, out_ref):
    for k, block in enumerate(blocks):
        out_ref[partner_rows(me_ref, k, block.shape[0]), :] = block[...]


def attend_kernel(
    per_group, ways, chunk, kv_local, me_ref, first_tile, low_ref, halo_ref, kv_ref, *refs
):
    blocks, refs = refs[:ways], refs[ways:]
    dq_ref, own_ref, rim_ref, qd_ref, k_ext, v_ext, k_t, dk_ext, dv_ext, s_buf, dp_buf = refs
    gather_rows(me_ref, blocks, qd_ref)
    group = qd_ref.shape[0]
    reach = WINDOW // TK
    for ref, at in ((k_ext, chunk * HD), (v_ext, (kv_local + chunk) * HD)):
        ref[:WINDOW, :] = halo_ref[:, at : at + HD]
        ref[WINDOW:, :] = kv_ref[:, at : at + HD]
    dk_ext[...] = jnp.zeros_like(dk_ext)
    dv_ext[...] = jnp.zeros_like(dv_ext)

    def turn(t, carry):
        rows = pl.ds(pl.multiple_of(t * TK, TK), TK)
        k_t[t] = jnp.transpose(k_ext[rows, :].astype(jnp.float32)).astype(jnp.bfloat16)
        return carry

    lax.fori_loop(0, (group + WINDOW) // TK, turn, 0)
    wide = per_group * TQ
    key_iota = lax.broadcasted_iota(jnp.int32, (TK, wide), 0)
    query_iota = lax.broadcasted_iota(jnp.int32, (1, TQ), 1)
    diagonal = jnp.concatenate([query_iota] * per_group, axis=1)

    def q_block(b, tiles):
        q_rows = pl.ds(pl.multiple_of(b * TQ, TQ), TQ)
        first = b + reach + 1 - tiles
        q = jnp.concatenate(
            [qd_ref[q_rows, i * HD : (i + 1) * HD] for i in range(per_group)], axis=0
        )
        d_out = jnp.concatenate(
            [qd_ref[q_rows, i * HD : (i + 1) * HD] for i in range(per_group, 2 * per_group)],
            axis=0,
        )
        low = jnp.concatenate([low_ref[:, q_rows]] * per_group, axis=1) - first * TK
        key_rows = [pl.ds(pl.multiple_of((first + t) * TK, TK), TK) for t in range(tiles)]
        slots = [slice(t * TK, (t + 1) * TK) for t in range(tiles)]

        top = jnp.full((1, wide), MASKED, jnp.float32)
        for t in range(tiles):
            s = dot_nt(k_ext[key_rows[t], :], q)
            allowed = key_iota >= low - t * TK
            if t == tiles - 1:
                allowed = allowed & (key_iota <= diagonal)
            s = jnp.where(allowed, s, MASKED)
            s_buf[slots[t], :] = s
            top = jnp.maximum(top, jnp.max(s, axis=0, keepdims=True))

        total = jnp.zeros((1, wide), jnp.float32)
        dotted = jnp.zeros((1, wide), jnp.float32)
        for t in range(tiles):
            p = jnp.exp2((s_buf[slots[t], :] - top) * EXP2_SCALE)
            dp = dot_nt(v_ext[key_rows[t], :], d_out)
            s_buf[slots[t], :] = p
            dp_buf[slots[t], :] = dp
            total += jnp.sum(p, axis=0, keepdims=True)
            dotted += jnp.sum(p * dp, axis=0, keepdims=True)
        inverse = 1.0 / total
        row_dot = dotted * inverse

        dq_t = jnp.zeros((HD, wide), jnp.float32)
        for t in range(tiles):
            weights = s_buf[slots[t], :] * inverse
            ds = (weights * (dp_buf[slots[t], :] - row_dot)).astype(jnp.bfloat16)
            dv_ext[key_rows[t], :] += dot_nn(weights.astype(jnp.bfloat16), d_out)
            dk_ext[key_rows[t], :] += dot_nn(ds, q)
            dq_t += dot_nn(k_t[first + t], ds)

        dq = jnp.transpose(dq_t * SCALING).astype(jnp.bfloat16)
        for i in range(per_group):
            dq_ref[q_rows, i * HD : (i + 1) * HD] = dq[i * TQ : (i + 1) * TQ, :]

    def any_block(b, carry):
        tiles = b + reach + 1 - first_tile[b]
        for count in range(1, reach + 2):
            pl.when(tiles == count)(functools.partial(q_block, b, count))
        return carry

    lax.fori_loop(0, group // TQ, any_block, 0)
    rim_ref[:, :HD] = (dk_ext[:WINDOW, :] * SCALING).astype(jnp.bfloat16)
    rim_ref[:, HD:] = dv_ext[:WINDOW, :].astype(jnp.bfloat16)
    own_ref[:, :HD] = dk_ext[WINDOW:, :] * SCALING
    own_ref[:, HD:] = dv_ext[WINDOW:, :]


def attend(me, qd_blocks, halo, own, chunk, kv_local, low, first_tile):
    group = own.shape[0]
    tokens, qd_lanes = qd_blocks[0].shape
    ways = len(qd_blocks)
    per_group = qd_lanes // (2 * HD)
    ext = group + WINDOW
    wide = per_group * TQ
    span = WINDOW + TQ

    area = group * (WINDOW + TQ) * per_group
    outs = [
        jax.ShapeDtypeStruct((group, per_group * HD), jnp.bfloat16),
        jax.ShapeDtypeStruct((group, 2 * HD), jnp.float32),
        jax.ShapeDtypeStruct((WINDOW, 2 * HD), jnp.bfloat16),
    ]
    scratch = [
        jax.ShapeDtypeStruct((group, qd_lanes), jnp.bfloat16),
        jax.ShapeDtypeStruct((ext, HD), jnp.bfloat16),
        jax.ShapeDtypeStruct((ext, HD), jnp.bfloat16),
        jax.ShapeDtypeStruct((ext // TK, HD, TK), jnp.bfloat16),
        jax.ShapeDtypeStruct((ext, HD), jnp.float32),
        jax.ShapeDtypeStruct((ext, HD), jnp.float32),
        jax.ShapeDtypeStruct((span, wide), jnp.float32),
        jax.ShapeDtypeStruct((span, wide), jnp.float32),
    ]
    needed = array_bytes([low, halo, own, *qd_blocks, *outs, *scratch])
    return pl.pallas_call(
        functools.partial(attend_kernel, per_group, ways, chunk, kv_local),
        out_shape=tuple(outs),
        in_specs=[SMEM, SMEM] + [VMEM] * (3 + ways),
        out_specs=(VMEM,) * 3,
        scratch_shapes=[pltpu.VMEM(s.shape, s.dtype) for s in scratch],
        compiler_params=pltpu.CompilerParams(vmem_limit_bytes=needed + SPARE),
        cost_estimate=pl.CostEstimate(
            flops=area * HD * 2 * 5, bytes_accessed=group * HD * 24, transcendentals=area
        ),
        name="attend",
    )(me, first_tile, low, halo, own, *qd_blocks)


def on_chip(kernel, me, arrays, shapes, name, scratch=(), earlier=()):
    outs = tuple(jax.ShapeDtypeStruct(s, jnp.bfloat16) for s in shapes)
    moved = array_bytes([*arrays, *earlier, *outs])

    def body(me_ref, *refs):
        kernel(me_ref, *refs[len(earlier) :])

    return pl.pallas_call(
        body,
        out_shape=outs,
        in_specs=[SMEM] + [VMEM] * (len(earlier) + len(arrays)),
        out_specs=(VMEM,) * len(shapes),
        scratch_shapes=list(scratch),
        compiler_params=pltpu.CompilerParams(vmem_limit_bytes=moved + SPARE),
        cost_estimate=pl.CostEstimate(flops=0, bytes_accessed=moved, transcendentals=0),
        name=name,
    )(me, *earlier, *arrays)


def packed(me, arrays, ways, places, chunk=0, chunks=1, earlier=()):
    tokens = arrays[0].shape[0]
    lanes = [a.shape[1] // (ways * chunks) for a in arrays]

    def kernel(me_ref, *refs):
        ins, outs = refs[: len(arrays)], refs[len(arrays) :]
        for k, out in zip(places, outs):
            first = 0
            for ref, width in zip(ins, lanes):
                at = pl.multiple_of(((me_ref[0] ^ k) * chunks + chunk) * width, width)
                out[:, first : first + width] = ref[:, pl.ds(at, width)]
                first += width

    shapes = [(tokens, sum(lanes))] * len(places)
    return on_chip(kernel, me, arrays, shapes, "packed", earlier=earlier)


def unpacked(me, grads, q_lanes):
    chunks, ways = len(grads), len(grads[0])
    tokens = grads[0][0].shape[0]
    lanes = (q_lanes, HD, HD)

    def kernel(me_ref, *refs):
        ins, outs = refs[: chunks * ways], refs[chunks * ways :]
        for c in range(chunks):
            for k in range(ways):
                first = 0
                for out, width in zip(outs, lanes):
                    at = pl.multiple_of(((me_ref[0] ^ k) * chunks + c) * width, width)
                    out[:, pl.ds(at, width)] = ins[c * ways + k][:, first : first + width]
                    first += width

    shapes = [(tokens, ways * chunks * width) for width in lanes]
    return on_chip(kernel, me, [g for blocks in grads for g in blocks], shapes, "unpacked")


def gathered(me, blocks):
    tokens, lanes = blocks[0].shape
    ways = len(blocks)
    group = ways * tokens

    def kernel(me_ref, *refs):
        all_ref, tail_ref = refs[ways:]
        gather_rows(me_ref, refs[:ways], all_ref)
        tail_ref[...] = all_ref[group - WINDOW :, :]

    return on_chip(kernel, me, blocks, [(group, lanes), (WINDOW, lanes)], "gathered")


def settled(me, dq, own, returned, ways, places, earlier=()):
    group, q_lanes = dq.shape
    tokens = group // ways

    def kernel(me_ref, dq_ref, own_ref, back_ref, *refs):
        outs, total = refs[:-1], refs[-1]
        cut = group - WINDOW
        total[:cut, :] = own_ref[:cut, :].astype(jnp.bfloat16)
        total[cut:, :] = (own_ref[cut:, :] + back_ref[...].astype(jnp.float32)).astype(jnp.bfloat16)
        for k, out in zip(places, outs):
            rows = partner_rows(me_ref, k, tokens)
            out[:, :q_lanes] = dq_ref[rows, :]
            out[:, q_lanes:] = total[rows, :]

    shapes = [(tokens, q_lanes + 2 * HD)] * len(places)
    scratch = [pltpu.VMEM((group, 2 * HD), jnp.bfloat16)]
    return on_chip(kernel, me, (dq, own, returned), shapes, "settled", scratch, earlier)


def exchanged(blocks):
    ways = len(blocks)
    return [blocks[0]] + [
        lax.ppermute(blocks[k], "head", [(i, i ^ k) for i in range(ways)]) for k in range(1, ways)
    ]


def local(queries, keys, values, grad_out, doc_lengths):
    ways = lax.axis_size("head")
    tokens = queries.shape[0]
    group = tokens * ways
    kv_local = keys.shape[1] // (ways * HD)
    per_group = queries.shape[1] // keys.shape[1]
    q_lanes = per_group * HD
    group_first = lax.axis_index("seq") * group
    me = lax.axis_index("head").astype(jnp.int32).reshape(1)
    places = list(range(ways))
    early = places[: ways - ways // 4]
    late = places[ways - ways // 4 :]

    position = group_first + jnp.arange(group, dtype=jnp.int32)
    ends = jnp.cumsum(doc_lengths)
    doc_start = jnp.sum(
        jnp.where(position[:, None] >= ends[None, :], doc_lengths[None, :], 0), axis=1
    )
    low = jnp.maximum(doc_start, position - (WINDOW - 1)) - (group_first - WINDOW)
    low = low.astype(jnp.int32)
    first_tile = low[::TQ] // TK

    came = exchanged(packed(me, (keys, values), ways, places))
    kv, tail = gathered(me, came)
    halo = passed_along(tail, "seq", 1)

    parts, returned = [], []
    for c in range(kv_local):
        sent = []
        for k in places:
            earlier = [parts[-1][0]] if parts and k in late else [came[k]] if k else []
            sent += packed(me, (queries, grad_out), ways, [k], c, kv_local, earlier)
        came = exchanged(sent)
        parts.append(attend(me, came, halo, kv, c, kv_local, low.reshape(1, group), first_tile))
        returned.append(passed_along(parts[-1][2], "seq", -1))

    grads = []
    for c, (dq, own, _) in enumerate(parts):
        if c < kv_local - 1:
            sent = [
                *settled(me, dq, own, returned[c], ways, early),
                *settled(me, dq, own, returned[c], ways, late, [parts[c + 1][0]]),
            ]
        else:
            sent = settled(me, dq, own, returned[c], ways, places)
        grads.append(exchanged(sent))
    return unpacked(me, grads, q_lanes)


def solution(mesh):
    rows = P(("seq", "head"), None)
    return jax.shard_map(
        local,
        mesh=mesh,
        in_specs=(rows, rows, rows, rows, P()),
        out_specs=(rows, rows, rows),
        check_vma=False,
    )
```

```python
import functools
import math

import jax
import jax.numpy as jnp
from jax import lax
from jax.experimental import pallas as pl
from jax.experimental.pallas import tpu as pltpu
from jax.sharding import PartitionSpec as P

HD = 128
WINDOW = 1024
TQ = TK = 256
SCALING = HD ** (-0.5)
EXP2_SCALE = SCALING * math.log2(math.e)
MASKED = -1e30
SPARE = 4 * 1024 * 1024
SMEM = pl.BlockSpec(memory_space=pltpu.SMEM)
VMEM = pl.BlockSpec(memory_space=pltpu.VMEM)


def array_bytes(arrays):
    return sum(math.prod(a.shape) * a.dtype.itemsize for a in arrays)


def passed_along(shard, axis, by):
    count = lax.axis_size(axis)
    pairs = [(i, i + by) for i in range(count) if 0 <= i + by < count]
    return lax.ppermute(shard, axis, pairs)


def dot_nt(a, b):
    return lax.dot_general(a, b, (((1,), (1,)), ((), ())), preferred_element_type=jnp.float32)


def dot_nn(a, b):
    return lax.dot_general(a, b, (((1,), (0,)), ((), ())), preferred_element_type=jnp.float32)


def partner_rows(me_ref, k, tokens):
    return pl.ds(pl.multiple_of((me_ref[0] ^ k) * tokens, tokens), tokens)


def gather_rows(me_ref, blocks, places, out_ref):
    for k, block in zip(places, blocks):
        out_ref[partner_rows(me_ref, k, block.shape[0]), :] = block[...]


def attend_kernel(
    per_group, places, chunk, kv_local, me_ref, docs_ref, halo_ref, kv_ref, *refs
):
    blocks, refs = refs[: len(places)], refs[-11:]
    dq_ref, own_ref, rim_ref, qd_ref, k_ext, v_ext, k_t, dk_ext, dv_ext, s_buf, dp_buf = refs
    gather_rows(me_ref, blocks, places, qd_ref)
    group = qd_ref.shape[0]
    reach = WINDOW // TK
    for ref, at in ((k_ext, chunk * HD), (v_ext, (kv_local + chunk) * HD)):
        ref[:WINDOW, :] = halo_ref[:, at : at + HD]
        ref[WINDOW:, :] = kv_ref[:, at : at + HD]
    dk_ext[...] = jnp.zeros_like(dk_ext)
    dv_ext[...] = jnp.zeros_like(dv_ext)

    def turn(t, carry):
        rows = pl.ds(pl.multiple_of(t * TK, TK), TK)
        k_t[t] = jnp.transpose(k_ext[rows, :].astype(jnp.float32)).astype(jnp.bfloat16)
        return carry

    lax.fori_loop(0, (group + WINDOW) // TK, turn, 0)
    wide = per_group * TQ
    key_iota = lax.broadcasted_iota(jnp.int32, (TK, wide), 0)
    query_iota = lax.broadcasted_iota(jnp.int32, (1, TQ), 1)
    diagonal = jnp.concatenate([query_iota] * per_group, axis=1)

    def q_block(b, low, tiles):
        q_rows = pl.ds(pl.multiple_of(b * TQ, TQ), TQ)
        first = b + reach + 1 - tiles
        q = jnp.concatenate(
            [qd_ref[q_rows, i * HD : (i + 1) * HD] for i in range(per_group)], axis=0
        )
        d_out = jnp.concatenate(
            [qd_ref[q_rows, i * HD : (i + 1) * HD] for i in range(per_group, 2 * per_group)],
            axis=0,
        )
        low = jnp.concatenate([low] * per_group, axis=1) - first * TK
        key_rows = [pl.ds(pl.multiple_of((first + t) * TK, TK), TK) for t in range(tiles)]
        slots = [slice(t * TK, (t + 1) * TK) for t in range(tiles)]

        top = jnp.full((1, wide), MASKED, jnp.float32)
        for t in range(tiles):
            s = dot_nt(k_ext[key_rows[t], :], q)
            allowed = key_iota >= low - t * TK
            if t == tiles - 1:
                allowed = allowed & (key_iota <= diagonal)
            s = jnp.where(allowed, s, MASKED)
            s_buf[slots[t], :] = s
            top = jnp.maximum(top, jnp.max(s, axis=0, keepdims=True))

        total = jnp.zeros((1, wide), jnp.float32)
        dotted = jnp.zeros((1, wide), jnp.float32)
        for t in range(tiles):
            p = jnp.exp2((s_buf[slots[t], :] - top) * EXP2_SCALE)
            dp = dot_nt(v_ext[key_rows[t], :], d_out)
            s_buf[slots[t], :] = p
            dp_buf[slots[t], :] = dp
            total += jnp.sum(p, axis=0, keepdims=True)
            dotted += jnp.sum(p * dp, axis=0, keepdims=True)
        inverse = 1.0 / total
        row_dot = dotted * inverse

        dq_t = jnp.zeros((HD, wide), jnp.float32)
        for t in range(tiles):
            weights = s_buf[slots[t], :] * inverse
            ds = (weights * (dp_buf[slots[t], :] - row_dot)).astype(jnp.bfloat16)
            dv_ext[key_rows[t], :] += dot_nn(weights.astype(jnp.bfloat16), d_out)
            dk_ext[key_rows[t], :] += dot_nn(ds, q)
            dq_t += dot_nn(k_t[first + t], ds)

        dq = jnp.transpose(dq_t * SCALING).astype(jnp.bfloat16)
        for i in range(per_group):
            dq_ref[q_rows, i * HD : (i + 1) * HD] = dq[i * TQ : (i + 1) * TQ, :]

    def first_allowed(position):
        start, end = 0, 0
        for d in range(docs_ref.shape[0]):
            end = end + docs_ref[d]
            start = jnp.where(position >= end, end, start)
        return jnp.maximum(start, position - (WINDOW - 1)) - (me_ref[1] - WINDOW)

    def any_block(b, carry):
        position = me_ref[1] + b * TQ
        tiles = b + reach + 1 - lax.div(first_allowed(position), TK)
        low = first_allowed(position + query_iota)
        for count in range(1, reach + 2):
            pl.when(tiles == count)(functools.partial(q_block, b, low, count))
        return carry

    lax.fori_loop(0, group // TQ, any_block, 0)
    rim_ref[:, :HD] = (dk_ext[:WINDOW, :] * SCALING).astype(jnp.bfloat16)
    rim_ref[:, HD:] = dv_ext[:WINDOW, :].astype(jnp.bfloat16)
    own_ref[:, :HD] = dk_ext[WINDOW:, :] * SCALING
    own_ref[:, HD:] = dv_ext[WINDOW:, :]


def attend(me, docs, qd_blocks, places, halo, own, chunk, kv_local, earlier):
    group = own.shape[0]
    qd_lanes = qd_blocks[0].shape[1]
    per_group = qd_lanes // (2 * HD)
    ext = group + WINDOW
    wide = per_group * TQ
    span = WINDOW + TQ

    area = group * (WINDOW + TQ) * per_group
    outs = [
        jax.ShapeDtypeStruct((group, per_group * HD), jnp.bfloat16),
        jax.ShapeDtypeStruct((group, 2 * HD), jnp.float32),
        jax.ShapeDtypeStruct((WINDOW, 2 * HD), jnp.bfloat16),
    ]
    scratch = [
        jax.ShapeDtypeStruct((group, qd_lanes), jnp.bfloat16),
        jax.ShapeDtypeStruct((ext, HD), jnp.bfloat16),
        jax.ShapeDtypeStruct((ext, HD), jnp.bfloat16),
        jax.ShapeDtypeStruct((ext // TK, HD, TK), jnp.bfloat16),
        jax.ShapeDtypeStruct((ext, HD), jnp.float32),
        jax.ShapeDtypeStruct((ext, HD), jnp.float32),
        jax.ShapeDtypeStruct((span, wide), jnp.float32),
        jax.ShapeDtypeStruct((span, wide), jnp.float32),
    ]
    needed = array_bytes([halo, own, *qd_blocks, *earlier, *outs, *scratch])
    return pl.pallas_call(
        functools.partial(attend_kernel, per_group, places, chunk, kv_local),
        out_shape=tuple(outs),
        in_specs=[SMEM, SMEM] + [VMEM] * (2 + len(qd_blocks) + len(earlier)),
        out_specs=(VMEM,) * 3,
        scratch_shapes=[pltpu.VMEM(s.shape, s.dtype) for s in scratch],
        compiler_params=pltpu.CompilerParams(vmem_limit_bytes=needed + SPARE),
        cost_estimate=pl.CostEstimate(
            flops=area * HD * 2 * 5, bytes_accessed=group * HD * 24, transcendentals=area
        ),
        name="attend",
    )(me, docs, halo, own, *qd_blocks, *earlier)


def on_chip(kernel, me, arrays, shapes, name, scratch=(), earlier=()):
    outs = tuple(jax.ShapeDtypeStruct(s, jnp.bfloat16) for s in shapes)
    moved = array_bytes([*arrays, *earlier, *outs])

    def body(me_ref, *refs):
        kernel(me_ref, *refs[len(earlier) :])

    return pl.pallas_call(
        body,
        out_shape=outs,
        in_specs=[SMEM] + [VMEM] * (len(earlier) + len(arrays)),
        out_specs=(VMEM,) * len(shapes),
        scratch_shapes=list(scratch),
        compiler_params=pltpu.CompilerParams(vmem_limit_bytes=moved + SPARE),
        cost_estimate=pl.CostEstimate(flops=0, bytes_accessed=moved, transcendentals=0),
        name=name,
    )(me, *earlier, *arrays)


def packed(me, arrays, ways, places, chunk=0, chunks=1, earlier=()):
    tokens = arrays[0].shape[0]
    lanes = [a.shape[1] // (ways * chunks) for a in arrays]

    def kernel(me_ref, *refs):
        ins, outs = refs[: len(arrays)], refs[len(arrays) :]
        for k, out in zip(places, outs):
            first = 0
            for ref, width in zip(ins, lanes):
                at = pl.multiple_of(((me_ref[0] ^ k) * chunks + chunk) * width, width)
                out[:, first : first + width] = ref[:, pl.ds(at, width)]
                first += width

    shapes = [(tokens, sum(lanes))] * len(places)
    return on_chip(kernel, me, arrays, shapes, "packed", earlier=earlier)


def unpacked(me, grads, places, q_lanes):
    chunks, ways = len(grads), len(places)
    tokens = grads[0][0].shape[0]
    lanes = (q_lanes, HD, HD)

    def kernel(me_ref, *refs):
        ins, outs = refs[: chunks * ways], refs[chunks * ways :]
        for c in range(chunks):
            for k, block in zip(places, ins[c * ways : (c + 1) * ways]):
                first = 0
                for out, width in zip(outs, lanes):
                    at = pl.multiple_of(((me_ref[0] ^ k) * chunks + c) * width, width)
                    out[:, pl.ds(at, width)] = block[:, first : first + width]
                    first += width

    shapes = [(tokens, ways * chunks * width) for width in lanes]
    return on_chip(kernel, me, [g for blocks in grads for g in blocks], shapes, "unpacked")


def gathered(me, blocks, places):
    tokens, lanes = blocks[0].shape
    group = len(places) * tokens

    def kernel(me_ref, *refs):
        all_ref, tail_ref = refs[len(places) :]
        gather_rows(me_ref, refs[: len(places)], places, all_ref)
        tail_ref[...] = all_ref[group - WINDOW :, :]

    return on_chip(kernel, me, blocks, [(group, lanes), (WINDOW, lanes)], "gathered")


def settled(me, dq, own, returned, ways, places, earlier=()):
    group, q_lanes = dq.shape
    tokens = group // ways

    def kernel(me_ref, dq_ref, own_ref, back_ref, *refs):
        outs, total = refs[:-1], refs[-1]
        cut = group - WINDOW
        total[:cut, :] = own_ref[:cut, :].astype(jnp.bfloat16)
        total[cut:, :] = (own_ref[cut:, :] + back_ref[...].astype(jnp.float32)).astype(jnp.bfloat16)
        for k, out in zip(places, outs):
            rows = partner_rows(me_ref, k, tokens)
            out[:, :q_lanes] = dq_ref[rows, :]
            out[:, q_lanes:] = total[rows, :]

    shapes = [(tokens, q_lanes + 2 * HD)] * len(places)
    scratch = [pltpu.VMEM((group, 2 * HD), jnp.bfloat16)]
    return on_chip(kernel, me, (dq, own, returned), shapes, "settled", scratch, earlier)


def exchanged(blocks, places):
    ways = lax.axis_size("head")
    return [
        lax.ppermute(block, "head", [(i, i ^ k) for i in range(ways)]) if k else block
        for k, block in zip(places, blocks)
    ]


def local(queries, keys, values, grad_out, doc_lengths):
    ways = lax.axis_size("head")
    tokens = queries.shape[0]
    group = tokens * ways
    kv_local = keys.shape[1] // (ways * HD)
    per_group = queries.shape[1] // keys.shape[1]
    q_lanes = per_group * HD
    group_first = lax.axis_index("seq") * group
    me = jnp.stack([lax.axis_index("head"), group_first]).astype(jnp.int32)
    half, quarter = ways // 2, ways // 4
    early = [*range(half, half + quarter), *range(quarter, half, 2)]
    late = [k for k in [*range(ways - 1, 0, -1), 0] if k not in early]
    places = early + late

    came = exchanged(packed(me, (keys, values), ways, places), places)
    kv, tail = gathered(me, came, places)
    halo = passed_along(tail, "seq", 1)

    parts, returned, firsts = [], [], []
    for c in range(kv_local):
        sent = []
        for k, before in zip(places, came):
            earlier = [parts[-1][0]] if parts and k in late else [before] if k else []
            sent += packed(me, (queries, grad_out), ways, [k], c, kv_local, earlier)
        came = exchanged(sent, places)
        if parts:
            dq, own, _ = parts[-1]
            firsts.append(settled(me, dq, own, returned[-1], ways, early))
        earlier = [firsts[-1][0]] if firsts else []
        parts.append(attend(me, doc_lengths, came, places, halo, kv, c, kv_local, earlier))
        returned.append(passed_along(parts[-1][2], "seq", -1))

    grads = []
    for c, (dq, own, _) in enumerate(parts):
        if c < kv_local - 1:
            rest = settled(me, dq, own, returned[c], ways, late, [parts[c + 1][0]])
            sent = [*firsts[c], *rest]
        else:
            sent = settled(me, dq, own, returned[c], ways, places)
        grads.append(exchanged(sent, places))
    return unpacked(me, grads, places, q_lanes)


def solution(mesh):
    rows = P(("seq", "head"), None)
    return jax.shard_map(
        local,
        mesh=mesh,
        in_specs=(rows, rows, rows, rows, P()),
        out_specs=(rows, rows, rows),
        check_vma=False,
    )
```

```python
import functools
import math

import jax
import jax.numpy as jnp
from jax import lax
from jax.experimental import pallas as pl
from jax.experimental.pallas import tpu as pltpu
from jax.sharding import PartitionSpec as P

HD = 128
WINDOW = 1024
TQ = TK = 256
SCALING = HD ** (-0.5)
EXP2_SCALE = SCALING * math.log2(math.e)
MASKED = -1e30
SPARE = 4 * 1024 * 1024
SMEM = pl.BlockSpec(memory_space=pltpu.SMEM)
VMEM = pl.BlockSpec(memory_space=pltpu.VMEM)


def array_bytes(arrays):
    return sum(math.prod(a.shape) * a.dtype.itemsize for a in arrays)


def passed_along(shard, axis, by):
    count = lax.axis_size(axis)
    pairs = [(i, i + by) for i in range(count) if 0 <= i + by < count]
    return lax.ppermute(shard, axis, pairs)


def dot_nt(a, b):
    return lax.dot_general(a, b, (((1,), (1,)), ((), ())), preferred_element_type=jnp.float32)


def dot_nn(a, b):
    return lax.dot_general(a, b, (((1,), (0,)), ((), ())), preferred_element_type=jnp.float32)


def partner_rows(me_ref, k, tokens):
    return pl.ds(pl.multiple_of((me_ref[0] ^ k) * tokens, tokens), tokens)


def gather_rows(me_ref, blocks, places, out_ref):
    for k, block in zip(places, blocks):
        out_ref[partner_rows(me_ref, k, block.shape[0]), :] = block[...]


def attend_kernel(
    per_group, places, chunk, kv_local, me_ref, docs_ref, halo_ref, kv_ref, *refs
):
    blocks, refs = refs[: len(places)], refs[-11:]
    dq_ref, own_ref, rim_ref, qd_ref, k_ext, v_ext, k_t, dk_ext, dv_ext, s_buf, dp_buf = refs
    gather_rows(me_ref, blocks, places, qd_ref)
    group = qd_ref.shape[0]
    reach = WINDOW // TK
    for ref, at in ((k_ext, chunk * HD), (v_ext, (kv_local + chunk) * HD)):
        ref[:WINDOW, :] = halo_ref[:, at : at + HD]
        ref[WINDOW:, :] = kv_ref[:, at : at + HD]
    dk_ext[...] = jnp.zeros_like(dk_ext)
    dv_ext[...] = jnp.zeros_like(dv_ext)

    def turn(t, carry):
        rows = pl.ds(pl.multiple_of(t * TK, TK), TK)
        k_t[t] = jnp.transpose(k_ext[rows, :].astype(jnp.float32)).astype(jnp.bfloat16)
        return carry

    lax.fori_loop(0, (group + WINDOW) // TK, turn, 0)
    wide = per_group * TQ
    key_iota = lax.broadcasted_iota(jnp.int32, (TK, wide), 0)
    query_iota = lax.broadcasted_iota(jnp.int32, (1, TQ), 1)
    diagonal = jnp.concatenate([query_iota] * per_group, axis=1)

    def q_block(b, low, tiles):
        q_rows = pl.ds(pl.multiple_of(b * TQ, TQ), TQ)
        first = b + reach + 1 - tiles
        q = jnp.concatenate(
            [qd_ref[q_rows, i * HD : (i + 1) * HD] for i in range(per_group)], axis=0
        )
        d_out = jnp.concatenate(
            [qd_ref[q_rows, i * HD : (i + 1) * HD] for i in range(per_group, 2 * per_group)],
            axis=0,
        )
        low = jnp.concatenate([low] * per_group, axis=1) - first * TK
        key_rows = [pl.ds(pl.multiple_of((first + t) * TK, TK), TK) for t in range(tiles)]
        slots = [slice(t * TK, (t + 1) * TK) for t in range(tiles)]

        top = jnp.full((1, wide), MASKED, jnp.float32)
        for t in range(tiles):
            s = dot_nt(k_ext[key_rows[t], :], q)
            allowed = key_iota >= low - t * TK
            if t == tiles - 1:
                allowed = allowed & (key_iota <= diagonal)
            s = jnp.where(allowed, s, MASKED)
            s_buf[slots[t], :] = s
            top = jnp.maximum(top, jnp.max(s, axis=0, keepdims=True))

        total = jnp.zeros((1, wide), jnp.float32)
        dotted = jnp.zeros((1, wide), jnp.float32)
        for t in range(tiles):
            p = jnp.exp2((s_buf[slots[t], :] - top) * EXP2_SCALE)
            dp = dot_nt(v_ext[key_rows[t], :], d_out)
            s_buf[slots[t], :] = p
            dp_buf[slots[t], :] = dp
            total += jnp.sum(p, axis=0, keepdims=True)
            dotted += jnp.sum(p * dp, axis=0, keepdims=True)
        inverse = 1.0 / total
        row_dot = dotted * inverse

        dq_t = jnp.zeros((HD, wide), jnp.float32)
        for t in range(tiles):
            weights = s_buf[slots[t], :] * inverse
            ds = (weights * (dp_buf[slots[t], :] - row_dot)).astype(jnp.bfloat16)
            dv_ext[key_rows[t], :] += dot_nn(weights.astype(jnp.bfloat16), d_out)
            dk_ext[key_rows[t], :] += dot_nn(ds, q)
            dq_t += dot_nn(k_t[first + t], ds)

        dq = jnp.transpose(dq_t * SCALING).astype(jnp.bfloat16)
        for i in range(per_group):
            dq_ref[q_rows, i * HD : (i + 1) * HD] = dq[i * TQ : (i + 1) * TQ, :]

    def first_allowed(position):
        start, end = 0, 0
        for d in range(docs_ref.shape[0]):
            end = end + docs_ref[d]
            start = jnp.where(position >= end, end, start)
        return jnp.maximum(start, position - (WINDOW - 1)) - (me_ref[1] - WINDOW)

    def any_block(b, carry):
        position = me_ref[1] + b * TQ
        tiles = b + reach + 1 - lax.div(first_allowed(position), TK)
        low = first_allowed(position + query_iota)
        for count in range(1, reach + 2):
            pl.when(tiles == count)(functools.partial(q_block, b, low, count))
        return carry

    lax.fori_loop(0, group // TQ, any_block, 0)
    rim_ref[:, :HD] = (dk_ext[:WINDOW, :] * SCALING).astype(jnp.bfloat16)
    rim_ref[:, HD:] = dv_ext[:WINDOW, :].astype(jnp.bfloat16)
    own_ref[:, :HD] = dk_ext[WINDOW:, :] * SCALING
    own_ref[:, HD:] = dv_ext[WINDOW:, :]


def attend(me, docs, qd_blocks, places, halo, own, chunk, kv_local, earlier):
    group = own.shape[0]
    qd_lanes = qd_blocks[0].shape[1]
    per_group = qd_lanes // (2 * HD)
    ext = group + WINDOW
    wide = per_group * TQ
    span = WINDOW + TQ

    area = group * (WINDOW + TQ) * per_group
    outs = [
        jax.ShapeDtypeStruct((group, per_group * HD), jnp.bfloat16),
        jax.ShapeDtypeStruct((group, 2 * HD), jnp.float32),
        jax.ShapeDtypeStruct((WINDOW, 2 * HD), jnp.bfloat16),
    ]
    scratch = [
        jax.ShapeDtypeStruct((group, qd_lanes), jnp.bfloat16),
        jax.ShapeDtypeStruct((ext, HD), jnp.bfloat16),
        jax.ShapeDtypeStruct((ext, HD), jnp.bfloat16),
        jax.ShapeDtypeStruct((ext // TK, HD, TK), jnp.bfloat16),
        jax.ShapeDtypeStruct((ext, HD), jnp.float32),
        jax.ShapeDtypeStruct((ext, HD), jnp.float32),
        jax.ShapeDtypeStruct((span, wide), jnp.float32),
        jax.ShapeDtypeStruct((span, wide), jnp.float32),
    ]
    needed = array_bytes([halo, own, *qd_blocks, *earlier, *outs, *scratch])
    return pl.pallas_call(
        functools.partial(attend_kernel, per_group, places, chunk, kv_local),
        out_shape=tuple(outs),
        in_specs=[SMEM, SMEM] + [VMEM] * (2 + len(qd_blocks) + len(earlier)),
        out_specs=(VMEM,) * 3,
        scratch_shapes=[pltpu.VMEM(s.shape, s.dtype) for s in scratch],
        compiler_params=pltpu.CompilerParams(vmem_limit_bytes=needed + SPARE),
        cost_estimate=pl.CostEstimate(
            flops=area * HD * 2 * 5, bytes_accessed=group * HD * 24, transcendentals=area
        ),
        name="attend",
    )(me, docs, halo, own, *qd_blocks, *earlier)


def on_chip(kernel, me, arrays, shapes, name, scratch=(), earlier=()):
    outs = tuple(jax.ShapeDtypeStruct(s, jnp.bfloat16) for s in shapes)
    moved = array_bytes([*arrays, *earlier, *outs])

    def body(me_ref, *refs):
        kernel(me_ref, *refs[len(earlier) :])

    return pl.pallas_call(
        body,
        out_shape=outs,
        in_specs=[SMEM] + [VMEM] * (len(earlier) + len(arrays)),
        out_specs=(VMEM,) * len(shapes),
        scratch_shapes=list(scratch),
        compiler_params=pltpu.CompilerParams(vmem_limit_bytes=moved + SPARE),
        cost_estimate=pl.CostEstimate(flops=0, bytes_accessed=moved, transcendentals=0),
        name=name,
    )(me, *earlier, *arrays)


def packed(me, arrays, ways, places, chunk=0, chunks=1, earlier=()):
    tokens = arrays[0].shape[0]
    lanes = [a.shape[1] // (ways * chunks) for a in arrays]

    def kernel(me_ref, *refs):
        ins, outs = refs[: len(arrays)], refs[len(arrays) :]
        for k, out in zip(places, outs):
            first = 0
            for ref, width in zip(ins, lanes):
                at = pl.multiple_of(((me_ref[0] ^ k) * chunks + chunk) * width, width)
                out[:, first : first + width] = ref[:, pl.ds(at, width)]
                first += width

    shapes = [(tokens, sum(lanes))] * len(places)
    return on_chip(kernel, me, arrays, shapes, "packed", earlier=earlier)


def unpacked(me, grads, places, q_lanes):
    chunks, ways = len(grads), len(places)
    tokens = grads[0][0].shape[-2]
    lanes = (q_lanes, HD, HD)
    counts = [len(blocks) for blocks in grads]

    def kernel(me_ref, *refs):
        outs = refs[sum(counts) :]
        for c in range(chunks):
            ins = refs[sum(counts[:c]) : sum(counts[: c + 1])]
            for n in range(ways):
                block = ins[n] if len(ins) > 1 else ins[0].at[n]
                place = me_ref[0] ^ places[n] if len(ins) > 1 else n
                first = 0
                for out, width in zip(outs, lanes):
                    at = (place * chunks + c) * width
                    at = at if isinstance(at, int) else pl.multiple_of(at, width)
                    out[:, pl.ds(at, width)] = block[:, first : first + width]
                    first += width

    shapes = [(tokens, ways * chunks * width) for width in lanes]
    return on_chip(kernel, me, [g for blocks in grads for g in blocks], shapes, "unpacked")


def gathered(me, blocks, places):
    tokens, lanes = blocks[0].shape
    group = len(places) * tokens

    def kernel(me_ref, *refs):
        all_ref, tail_ref = refs[len(places) :]
        gather_rows(me_ref, refs[: len(places)], places, all_ref)
        tail_ref[...] = all_ref[group - WINDOW :, :]

    return on_chip(kernel, me, blocks, [(group, lanes), (WINDOW, lanes)], "gathered")


def settled(me, dq, own, returned, ways, places=None):
    group, q_lanes = dq.shape
    tokens = group // ways
    total_lanes = q_lanes + 2 * HD

    def kernel(me_ref, dq_ref, own_ref, back_ref, *refs):
        cut = group - WINDOW
        total = refs[-1] if places else refs[0].at[:, q_lanes:]
        total[:cut, :] = own_ref[:cut, :].astype(jnp.bfloat16)
        total[cut:, :] = (own_ref[cut:, :] + back_ref[...].astype(jnp.float32)).astype(jnp.bfloat16)
        if not places:
            refs[0][:, :q_lanes] = dq_ref[...]
            return
        for k, out in zip(places, refs):
            rows = partner_rows(me_ref, k, tokens)
            out[:, :q_lanes] = dq_ref[rows, :]
            out[:, q_lanes:] = total[rows, :]

    shapes = [(tokens, total_lanes)] * ways if places else [(group, total_lanes)]
    scratch = [pltpu.VMEM((group, 2 * HD), jnp.bfloat16)] if places else []
    return on_chip(kernel, me, (dq, own, returned), shapes, "settled", scratch)


def exchanged(blocks, places):
    ways = lax.axis_size("head")
    return [
        lax.ppermute(block, "head", [(i, i ^ k) for i in range(ways)]) if k else block
        for k, block in zip(places, blocks)
    ]


def local(queries, keys, values, grad_out, doc_lengths):
    ways = lax.axis_size("head")
    tokens = queries.shape[0]
    group = tokens * ways
    kv_local = keys.shape[1] // (ways * HD)
    per_group = queries.shape[1] // keys.shape[1]
    q_lanes = per_group * HD
    group_first = lax.axis_index("seq") * group
    me = jnp.stack([lax.axis_index("head"), group_first]).astype(jnp.int32)
    places = list(range(ways))
    late = places[ways - ways // 4 :]

    came = exchanged(packed(me, (keys, values), ways, places), places)
    kv, tail = gathered(me, came, places)
    halo = passed_along(tail, "seq", 1)

    parts, returned, firsts = [], [], []
    for c in range(kv_local):
        sent = []
        for k, before in zip(places, came):
            earlier = [parts[-1][0]] if parts and k in late else [before] if k else []
            sent += packed(me, (queries, grad_out), ways, [k], c, kv_local, earlier)
        came = exchanged(sent, places)
        if parts:
            dq, own, _ = parts[-1]
            firsts += settled(me, dq, own, returned[-1], ways)
        earlier = firsts[-1:]
        parts.append(attend(me, doc_lengths, came, places, halo, kv, c, kv_local, earlier))
        returned.append(passed_along(parts[-1][2], "seq", -1))

    grads = []
    for rows in firsts:
        sent = rows.reshape(ways, tokens, rows.shape[1])
        grads.append([lax.all_to_all(sent, "head", split_axis=0, concat_axis=0, tiled=True)])
    dq, own, _ = parts[-1]
    grads.append(exchanged(settled(me, dq, own, returned[-1], ways, places), places))
    return unpacked(me, grads, places, q_lanes)


def solution(mesh):
    rows = P(("seq", "head"), None)
    return jax.shard_map(
        local,
        mesh=mesh,
        in_specs=(rows, rows, rows, rows, P()),
        out_specs=(rows, rows, rows),
        check_vma=False,
    )
```

```python
import functools
import math

import jax
import jax.numpy as jnp
from jax import lax
from jax.experimental import pallas as pl
from jax.experimental.pallas import tpu as pltpu
from jax.sharding import PartitionSpec as P

HD = 128
WINDOW = 1024
TQ = TK = 256
SCALING = HD ** (-0.5)
EXP2_SCALE = SCALING * math.log2(math.e)
MASKED = -1e30
SPARE = 4 * 1024 * 1024
SMEM = pl.BlockSpec(memory_space=pltpu.SMEM)
VMEM = pl.BlockSpec(memory_space=pltpu.VMEM)


def array_bytes(arrays):
    return sum(math.prod(a.shape) * a.dtype.itemsize for a in arrays)


def passed_along(shard, axis, by):
    count = lax.axis_size(axis)
    pairs = [(i, i + by) for i in range(count) if 0 <= i + by < count]
    return lax.ppermute(shard, axis, pairs)


def dot_nt(a, b):
    return lax.dot_general(a, b, (((1,), (1,)), ((), ())), preferred_element_type=jnp.float32)


def dot_nn(a, b):
    return lax.dot_general(a, b, (((1,), (0,)), ((), ())), preferred_element_type=jnp.float32)


def partner_rows(me_ref, k, tokens):
    return pl.ds(pl.multiple_of((me_ref[0] ^ k) * tokens, tokens), tokens)


def gather_rows(me_ref, blocks, places, out_ref):
    for k, block in zip(places, blocks):
        out_ref[partner_rows(me_ref, k, block.shape[0]), :] = block[...]


def attend_kernel(
    per_group, chunk, kv_local, me_ref, docs_ref, halo_ref, kv_ref, qd_ref,
    dq_ref, own_ref, rim_ref, k_ext, v_ext, k_t, dk_ext, dv_ext, s_buf, dp_buf,
):
    group = qd_ref.shape[0]
    reach = WINDOW // TK
    for ref, at in ((k_ext, chunk * HD), (v_ext, (kv_local + chunk) * HD)):
        ref[:WINDOW, :] = halo_ref[:, at : at + HD]
        ref[WINDOW:, :] = kv_ref[:, at : at + HD]
    dk_ext[...] = jnp.zeros_like(dk_ext)
    dv_ext[...] = jnp.zeros_like(dv_ext)

    def turn(t, carry):
        rows = pl.ds(pl.multiple_of(t * TK, TK), TK)
        k_t[t] = jnp.transpose(k_ext[rows, :].astype(jnp.float32)).astype(jnp.bfloat16)
        return carry

    lax.fori_loop(0, (group + WINDOW) // TK, turn, 0)
    wide = per_group * TQ
    key_iota = lax.broadcasted_iota(jnp.int32, (TK, wide), 0)
    query_iota = lax.broadcasted_iota(jnp.int32, (1, TQ), 1)
    diagonal = jnp.concatenate([query_iota] * per_group, axis=1)

    def q_block(b, low, tiles):
        q_rows = pl.ds(pl.multiple_of(b * TQ, TQ), TQ)
        first = b + reach + 1 - tiles
        q = jnp.concatenate(
            [qd_ref[q_rows, i * HD : (i + 1) * HD] for i in range(per_group)], axis=0
        )
        d_out = jnp.concatenate(
            [qd_ref[q_rows, i * HD : (i + 1) * HD] for i in range(per_group, 2 * per_group)],
            axis=0,
        )
        low = jnp.concatenate([low] * per_group, axis=1) - first * TK
        key_rows = [pl.ds(pl.multiple_of((first + t) * TK, TK), TK) for t in range(tiles)]
        slots = [slice(t * TK, (t + 1) * TK) for t in range(tiles)]

        top = jnp.full((1, wide), MASKED, jnp.float32)
        for t in range(tiles):
            s = dot_nt(k_ext[key_rows[t], :], q)
            allowed = key_iota >= low - t * TK
            if t == tiles - 1:
                allowed = allowed & (key_iota <= diagonal)
            s = jnp.where(allowed, s, MASKED)
            s_buf[slots[t], :] = s
            top = jnp.maximum(top, jnp.max(s, axis=0, keepdims=True))

        total = jnp.zeros((1, wide), jnp.float32)
        dotted = jnp.zeros((1, wide), jnp.float32)
        for t in range(tiles):
            p = jnp.exp2((s_buf[slots[t], :] - top) * EXP2_SCALE)
            dp = dot_nt(v_ext[key_rows[t], :], d_out)
            s_buf[slots[t], :] = p
            dp_buf[slots[t], :] = dp
            total += jnp.sum(p, axis=0, keepdims=True)
            dotted += jnp.sum(p * dp, axis=0, keepdims=True)
        inverse = 1.0 / total
        row_dot = dotted * inverse

        dq_t = jnp.zeros((HD, wide), jnp.float32)
        for t in range(tiles):
            weights = s_buf[slots[t], :] * inverse
            ds = (weights * (dp_buf[slots[t], :] - row_dot)).astype(jnp.bfloat16)
            dv_ext[key_rows[t], :] += dot_nn(weights.astype(jnp.bfloat16), d_out)
            dk_ext[key_rows[t], :] += dot_nn(ds, q)
            dq_t += dot_nn(k_t[first + t], ds)

        dq = jnp.transpose(dq_t * SCALING).astype(jnp.bfloat16)
        for i in range(per_group):
            dq_ref[q_rows, i * HD : (i + 1) * HD] = dq[i * TQ : (i + 1) * TQ, :]

    def first_allowed(position):
        start, end = 0, 0
        for d in range(docs_ref.shape[0]):
            end = end + docs_ref[d]
            start = jnp.where(position >= end, end, start)
        return jnp.maximum(start, position - (WINDOW - 1)) - (me_ref[1] - WINDOW)

    def any_block(b, carry):
        position = me_ref[1] + b * TQ
        tiles = b + reach + 1 - lax.div(first_allowed(position), TK)
        low = first_allowed(position + query_iota)
        for count in range(1, reach + 2):
            pl.when(tiles == count)(functools.partial(q_block, b, low, count))
        return carry

    lax.fori_loop(0, group // TQ, any_block, 0)
    rim_ref[:, :HD] = (dk_ext[:WINDOW, :] * SCALING).astype(jnp.bfloat16)
    rim_ref[:, HD:] = dv_ext[:WINDOW, :].astype(jnp.bfloat16)
    own_ref[:, :HD] = dk_ext[WINDOW:, :] * SCALING
    own_ref[:, HD:] = dv_ext[WINDOW:, :]


def attend(me, docs, qd, halo, own, chunk, kv_local):
    group = own.shape[0]
    per_group = qd.shape[1] // (2 * HD)
    ext = group + WINDOW
    wide = per_group * TQ
    span = WINDOW + TQ

    area = group * (WINDOW + TQ) * per_group
    outs = [
        jax.ShapeDtypeStruct((group, per_group * HD), jnp.bfloat16),
        jax.ShapeDtypeStruct((group, 2 * HD), jnp.float32),
        jax.ShapeDtypeStruct((WINDOW, 2 * HD), jnp.bfloat16),
    ]
    scratch = [
        jax.ShapeDtypeStruct((ext, HD), jnp.bfloat16),
        jax.ShapeDtypeStruct((ext, HD), jnp.bfloat16),
        jax.ShapeDtypeStruct((ext // TK, HD, TK), jnp.bfloat16),
        jax.ShapeDtypeStruct((ext, HD), jnp.float32),
        jax.ShapeDtypeStruct((ext, HD), jnp.float32),
        jax.ShapeDtypeStruct((span, wide), jnp.float32),
        jax.ShapeDtypeStruct((span, wide), jnp.float32),
    ]
    needed = array_bytes([halo, own, qd, *outs, *scratch])
    return pl.pallas_call(
        functools.partial(attend_kernel, per_group, chunk, kv_local),
        out_shape=tuple(outs),
        in_specs=[SMEM, SMEM] + [VMEM] * 3,
        out_specs=(VMEM,) * 3,
        scratch_shapes=[pltpu.VMEM(s.shape, s.dtype) for s in scratch],
        compiler_params=pltpu.CompilerParams(vmem_limit_bytes=needed + SPARE),
        cost_estimate=pl.CostEstimate(
            flops=area * HD * 2 * 5, bytes_accessed=group * HD * 24, transcendentals=area
        ),
        name="attend",
    )(me, docs, halo, own, qd)


def on_chip(kernel, me, arrays, shapes, name, scratch=(), earlier=()):
    outs = tuple(jax.ShapeDtypeStruct(s, jnp.bfloat16) for s in shapes)
    moved = array_bytes([*arrays, *earlier, *outs])

    def body(me_ref, *refs):
        kernel(me_ref, *refs[len(earlier) :])

    return pl.pallas_call(
        body,
        out_shape=outs,
        in_specs=[SMEM] + [VMEM] * (len(earlier) + len(arrays)),
        out_specs=(VMEM,) * len(shapes),
        scratch_shapes=list(scratch),
        compiler_params=pltpu.CompilerParams(vmem_limit_bytes=moved + SPARE),
        cost_estimate=pl.CostEstimate(flops=0, bytes_accessed=moved, transcendentals=0),
        name=name,
    )(me, *earlier, *arrays)


def packed(me, arrays, ways, chunk=0, chunks=1, places=None, earlier=()):
    tokens = arrays[0].shape[0]
    lanes = [a.shape[1] // (ways * chunks) for a in arrays]
    total = sum(lanes)

    def kernel(me_ref, *refs):
        ins, outs = refs[: len(arrays)], refs[len(arrays) :]
        for n in range(ways):
            out = outs[n] if places else outs[0].at[n]
            place = me_ref[0] ^ places[n] if places else n
            first = 0
            for ref, width in zip(ins, lanes):
                at = (place * chunks + chunk) * width
                at = pl.multiple_of(at, width) if places else at
                out[:, first : first + width] = ref[:, pl.ds(at, width)]
                first += width

    shapes = [(tokens, total)] * ways if places else [(ways, tokens, total)]
    return on_chip(kernel, me, arrays, shapes, "packed", earlier=earlier)


def unpacked(me, grads, places, q_lanes):
    chunks, ways = len(grads), len(places)
    tokens = grads[0][0].shape[-2]
    lanes = (q_lanes, HD, HD)
    counts = [len(blocks) for blocks in grads]

    def kernel(me_ref, *refs):
        outs = refs[sum(counts) :]
        for c in range(chunks):
            ins = refs[sum(counts[:c]) : sum(counts[: c + 1])]
            for n in range(ways):
                block = ins[n] if len(ins) > 1 else ins[0].at[n]
                place = me_ref[0] ^ places[n] if len(ins) > 1 else n
                first = 0
                for out, width in zip(outs, lanes):
                    at = (place * chunks + c) * width
                    at = at if isinstance(at, int) else pl.multiple_of(at, width)
                    out[:, pl.ds(at, width)] = block[:, first : first + width]
                    first += width

    shapes = [(tokens, ways * chunks * width) for width in lanes]
    return on_chip(kernel, me, [g for blocks in grads for g in blocks], shapes, "unpacked")


def gathered(me, blocks, places, tail):
    tokens, lanes = blocks[0].shape
    group = len(places) * tokens

    def kernel(me_ref, *refs):
        ins, outs = refs[: len(places)], refs[len(places) :]
        gather_rows(me_ref, ins, places, outs[0])
        if tail:
            outs[1][...] = outs[0][group - tail :, :]

    shapes = [(group, lanes)] + ([(tail, lanes)] if tail else [])
    return on_chip(kernel, me, blocks, shapes, "gathered")


def settled(me, dq, own, returned, ways, places=None):
    group, q_lanes = dq.shape
    tokens = group // ways
    total_lanes = q_lanes + 2 * HD

    def kernel(me_ref, dq_ref, own_ref, back_ref, *refs):
        cut = group - WINDOW
        total = refs[-1] if places else refs[0].at[:, q_lanes:]
        total[:cut, :] = own_ref[:cut, :].astype(jnp.bfloat16)
        total[cut:, :] = (own_ref[cut:, :] + back_ref[...].astype(jnp.float32)).astype(jnp.bfloat16)
        if not places:
            refs[0][:, :q_lanes] = dq_ref[...]
            return
        for k, out in zip(places, refs):
            rows = partner_rows(me_ref, k, tokens)
            out[:, :q_lanes] = dq_ref[rows, :]
            out[:, q_lanes:] = total[rows, :]

    shapes = [(tokens, total_lanes)] * ways if places else [(group, total_lanes)]
    scratch = [pltpu.VMEM((group, 2 * HD), jnp.bfloat16)] if places else []
    return on_chip(kernel, me, (dq, own, returned), shapes, "settled", scratch)


def exchanged(blocks, places):
    ways = lax.axis_size("head")
    return [
        lax.ppermute(block, "head", [(i, i ^ k) for i in range(ways)]) if k else block
        for k, block in zip(places, blocks)
    ]


def exchanged_at_once(sent):
    return lax.all_to_all(sent, "head", split_axis=0, concat_axis=0, tiled=True)


def local(queries, keys, values, grad_out, doc_lengths):
    ways = lax.axis_size("head")
    tokens = queries.shape[0]
    group = tokens * ways
    kv_local = keys.shape[1] // (ways * HD)
    per_group = queries.shape[1] // keys.shape[1]
    q_lanes = per_group * HD
    group_first = lax.axis_index("seq") * group
    me = jnp.stack([lax.axis_index("head"), group_first]).astype(jnp.int32)
    places = list(range(ways))

    came = exchanged(packed(me, (keys, values), ways, places=places), places)
    kv, tail = gathered(me, came, places, WINDOW)
    halo = passed_along(tail, "seq", 1)
    sent = packed(me, (queries, grad_out), ways, 0, kv_local, places, [came[-1]])
    qds = list(gathered(me, exchanged(sent, places), places, 0))
    for c in range(1, kv_local):
        sent = packed(me, (queries, grad_out), ways, c, kv_local, None, [qds[-1], halo])[0]
        qds.append(exchanged_at_once(sent).reshape(group, 2 * q_lanes))

    grads = []
    for c, qd in enumerate(qds):
        dq, own, rim = attend(me, doc_lengths, qd, halo, kv, c, kv_local)
        returned = passed_along(rim, "seq", -1)
        if c < kv_local - 1:
            rows = settled(me, dq, own, returned, ways)[0]
            grads.append([exchanged_at_once(rows.reshape(ways, tokens, rows.shape[1]))])
        else:
            grads.append(exchanged(settled(me, dq, own, returned, ways, places), places))
    return unpacked(me, grads, places, q_lanes)


def solution(mesh):
    rows = P(("seq", "head"), None)
    return jax.shard_map(
        local,
        mesh=mesh,
        in_specs=(rows, rows, rows, rows, P()),
        out_specs=(rows, rows, rows),
        check_vma=False,
    )
```

```python
import functools
import math

import jax
import jax.numpy as jnp
from jax import lax
from jax.experimental import pallas as pl
from jax.experimental.pallas import tpu as pltpu
from jax.sharding import PartitionSpec as P

HD = 128
WINDOW = 1024
TQ = TK = 256
SCALING = HD ** (-0.5)
EXP2_SCALE = SCALING * math.log2(math.e)
MASKED = -1e30
SPARE = 4 * 1024 * 1024
SMEM = pl.BlockSpec(memory_space=pltpu.SMEM)
VMEM = pl.BlockSpec(memory_space=pltpu.VMEM)


def array_bytes(arrays):
    return sum(math.prod(a.shape) * a.dtype.itemsize for a in arrays)


def passed_along(shard, axis, by):
    count = lax.axis_size(axis)
    pairs = [(i, i + by) for i in range(count) if 0 <= i + by < count]
    return lax.ppermute(shard, axis, pairs)


def dot_nt(a, b):
    return lax.dot_general(a, b, (((1,), (1,)), ((), ())), preferred_element_type=jnp.float32)


def dot_nn(a, b):
    return lax.dot_general(a, b, (((1,), (0,)), ((), ())), preferred_element_type=jnp.float32)


def partner_rows(me_ref, k, tokens):
    return pl.ds(pl.multiple_of((me_ref[0] ^ k) * tokens, tokens), tokens)


def gather_rows(me_ref, blocks, places, out_ref):
    for k, block in zip(places, blocks):
        out_ref[partner_rows(me_ref, k, block.shape[0]), :] = block[...]


def attend_kernel(
    per_group, chunk, kv_local, me_ref, docs_ref, halo_ref, kv_ref, qd_ref,
    dq_ref, own_ref, rim_ref, k_ext, v_ext, k_t, dk_ext, dv_ext, s_buf, dp_buf,
):
    group = qd_ref.shape[0]
    reach = WINDOW // TK
    for ref, at in ((k_ext, chunk * HD), (v_ext, (kv_local + chunk) * HD)):
        ref[:WINDOW, :] = halo_ref[:, at : at + HD]
        ref[WINDOW:, :] = kv_ref[:, at : at + HD]
    dk_ext[...] = jnp.zeros_like(dk_ext)
    dv_ext[...] = jnp.zeros_like(dv_ext)

    def turn(t, carry):
        rows = pl.ds(pl.multiple_of(t * TK, TK), TK)
        k_t[t] = jnp.transpose(k_ext[rows, :].astype(jnp.float32)).astype(jnp.bfloat16)
        return carry

    lax.fori_loop(0, (group + WINDOW) // TK, turn, 0)
    wide = per_group * TQ
    key_iota = lax.broadcasted_iota(jnp.int32, (TK, wide), 0)
    query_iota = lax.broadcasted_iota(jnp.int32, (1, TQ), 1)
    diagonal = jnp.concatenate([query_iota] * per_group, axis=1)

    def q_block(b, low, tiles):
        q_rows = pl.ds(pl.multiple_of(b * TQ, TQ), TQ)
        first = b + reach + 1 - tiles
        q = jnp.concatenate(
            [qd_ref[q_rows, i * HD : (i + 1) * HD] for i in range(per_group)], axis=0
        )
        d_out = jnp.concatenate(
            [qd_ref[q_rows, i * HD : (i + 1) * HD] for i in range(per_group, 2 * per_group)],
            axis=0,
        )
        low = jnp.concatenate([low] * per_group, axis=1) - first * TK
        key_rows = [pl.ds(pl.multiple_of((first + t) * TK, TK), TK) for t in range(tiles)]
        slots = [slice(t * TK, (t + 1) * TK) for t in range(tiles)]

        top = jnp.full((1, wide), MASKED, jnp.float32)
        for t in range(tiles):
            s = dot_nt(k_ext[key_rows[t], :], q)
            allowed = key_iota >= low - t * TK
            if t == tiles - 1:
                allowed = allowed & (key_iota <= diagonal)
            s = jnp.where(allowed, s, MASKED)
            s_buf[slots[t], :] = s
            top = jnp.maximum(top, jnp.max(s, axis=0, keepdims=True))

        total = jnp.zeros((1, wide), jnp.float32)
        dotted = jnp.zeros((1, wide), jnp.float32)
        for t in range(tiles):
            p = jnp.exp2((s_buf[slots[t], :] - top) * EXP2_SCALE)
            dp = dot_nt(v_ext[key_rows[t], :], d_out)
            s_buf[slots[t], :] = p
            dp_buf[slots[t], :] = dp
            total += jnp.sum(p, axis=0, keepdims=True)
            dotted += jnp.sum(p * dp, axis=0, keepdims=True)
        inverse = 1.0 / total
        row_dot = dotted * inverse

        dq_t = jnp.zeros((HD, wide), jnp.float32)
        for t in range(tiles):
            weights = s_buf[slots[t], :] * inverse
            ds = (weights * (dp_buf[slots[t], :] - row_dot)).astype(jnp.bfloat16)
            dv_ext[key_rows[t], :] += dot_nn(weights.astype(jnp.bfloat16), d_out)
            dk_ext[key_rows[t], :] += dot_nn(ds, q)
            dq_t += dot_nn(k_t[first + t], ds)

        dq = jnp.transpose(dq_t * SCALING).astype(jnp.bfloat16)
        for i in range(per_group):
            dq_ref[q_rows, i * HD : (i + 1) * HD] = dq[i * TQ : (i + 1) * TQ, :]

    def first_allowed(position):
        start, end = 0, 0
        for d in range(docs_ref.shape[0]):
            end = end + docs_ref[d]
            start = jnp.where(position >= end, end, start)
        return jnp.maximum(start, position - (WINDOW - 1)) - (me_ref[1] - WINDOW)

    def any_block(b, carry):
        position = me_ref[1] + b * TQ
        tiles = b + reach + 1 - lax.div(first_allowed(position), TK)
        low = first_allowed(position + query_iota)
        for count in range(1, reach + 2):
            pl.when(tiles == count)(functools.partial(q_block, b, low, count))
        return carry

    lax.fori_loop(0, group // TQ, any_block, 0)
    rim_ref[:, :HD] = (dk_ext[:WINDOW, :] * SCALING).astype(jnp.bfloat16)
    rim_ref[:, HD:] = dv_ext[:WINDOW, :].astype(jnp.bfloat16)
    own_ref[:, :HD] = dk_ext[WINDOW:, :] * SCALING
    own_ref[:, HD:] = dv_ext[WINDOW:, :]


def attend(me, docs, qd, halo, own, chunk, kv_local):
    group = own.shape[0]
    per_group = qd.shape[1] // (2 * HD)
    ext = group + WINDOW
    wide = per_group * TQ
    span = WINDOW + TQ

    area = group * (WINDOW + TQ) * per_group
    outs = [
        jax.ShapeDtypeStruct((group, per_group * HD), jnp.bfloat16),
        jax.ShapeDtypeStruct((group, 2 * HD), jnp.float32),
        jax.ShapeDtypeStruct((WINDOW, 2 * HD), jnp.bfloat16),
    ]
    scratch = [
        jax.ShapeDtypeStruct((ext, HD), jnp.bfloat16),
        jax.ShapeDtypeStruct((ext, HD), jnp.bfloat16),
        jax.ShapeDtypeStruct((ext // TK, HD, TK), jnp.bfloat16),
        jax.ShapeDtypeStruct((ext, HD), jnp.float32),
        jax.ShapeDtypeStruct((ext, HD), jnp.float32),
        jax.ShapeDtypeStruct((span, wide), jnp.float32),
        jax.ShapeDtypeStruct((span, wide), jnp.float32),
    ]
    needed = array_bytes([halo, own, qd, *outs, *scratch])
    return pl.pallas_call(
        functools.partial(attend_kernel, per_group, chunk, kv_local),
        out_shape=tuple(outs),
        in_specs=[SMEM, SMEM] + [VMEM] * 3,
        out_specs=(VMEM,) * 3,
        scratch_shapes=[pltpu.VMEM(s.shape, s.dtype) for s in scratch],
        compiler_params=pltpu.CompilerParams(vmem_limit_bytes=needed + SPARE),
        cost_estimate=pl.CostEstimate(
            flops=area * HD * 2 * 5, bytes_accessed=group * HD * 24, transcendentals=area
        ),
        name="attend",
    )(me, docs, halo, own, qd)


def on_chip(kernel, me, arrays, shapes, name, scratch=(), earlier=()):
    outs = tuple(jax.ShapeDtypeStruct(s, jnp.bfloat16) for s in shapes)
    moved = array_bytes([*arrays, *earlier, *outs])

    def body(me_ref, *refs):
        kernel(me_ref, *refs[len(earlier) :])

    return pl.pallas_call(
        body,
        out_shape=outs,
        in_specs=[SMEM] + [VMEM] * (len(earlier) + len(arrays)),
        out_specs=(VMEM,) * len(shapes),
        scratch_shapes=list(scratch),
        compiler_params=pltpu.CompilerParams(vmem_limit_bytes=moved + SPARE),
        cost_estimate=pl.CostEstimate(flops=0, bytes_accessed=moved, transcendentals=0),
        name=name,
    )(me, *earlier, *arrays)


def packed(me, arrays, ways, places, chunk=0, chunks=1, earlier=()):
    tokens = arrays[0].shape[0]
    lanes = [a.shape[1] // (ways * chunks) for a in arrays]

    def kernel(me_ref, *refs):
        ins, outs = refs[: len(arrays)], refs[len(arrays) :]
        for k, out in zip(places, outs):
            first = 0
            for ref, width in zip(ins, lanes):
                at = pl.multiple_of(((me_ref[0] ^ k) * chunks + chunk) * width, width)
                out[:, first : first + width] = ref[:, pl.ds(at, width)]
                first += width

    shapes = [(tokens, sum(lanes))] * len(places)
    return on_chip(kernel, me, arrays, shapes, "packed", earlier=earlier)


def unpacked(me, grads, places, q_lanes):
    chunks, ways = len(grads), len(places)
    tokens = grads[0][0].shape[-2]
    lanes = (q_lanes, HD, HD)
    counts = [len(blocks) for blocks in grads]

    def kernel(me_ref, *refs):
        outs = refs[sum(counts) :]
        for c in range(chunks):
            ins = refs[sum(counts[:c]) : sum(counts[: c + 1])]
            for n in range(ways):
                block = ins[n] if len(ins) > 1 else ins[0].at[n]
                place = me_ref[0] ^ places[n] if len(ins) > 1 else n
                first = 0
                for out, width in zip(outs, lanes):
                    at = (place * chunks + c) * width
                    at = at if isinstance(at, int) else pl.multiple_of(at, width)
                    out[:, pl.ds(at, width)] = block[:, first : first + width]
                    first += width

    shapes = [(tokens, ways * chunks * width) for width in lanes]
    return on_chip(kernel, me, [g for blocks in grads for g in blocks], shapes, "unpacked")


def gathered(me, blocks, places, tail):
    tokens, lanes = blocks[0].shape
    group = len(places) * tokens

    def kernel(me_ref, *refs):
        ins, outs = refs[: len(places)], refs[len(places) :]
        gather_rows(me_ref, ins, places, outs[0])
        if tail:
            outs[1][...] = outs[0][group - tail :, :]

    shapes = [(group, lanes)] + ([(tail, lanes)] if tail else [])
    return on_chip(kernel, me, blocks, shapes, "gathered")


def settled(me, dq, own, returned, ways, places=None, earlier=()):
    group, q_lanes = dq.shape
    tokens = group // ways
    total_lanes = q_lanes + 2 * HD

    def kernel(me_ref, dq_ref, own_ref, back_ref, *refs):
        cut = group - WINDOW
        total = refs[-1] if places else refs[0].at[:, q_lanes:]
        total[:cut, :] = own_ref[:cut, :].astype(jnp.bfloat16)
        total[cut:, :] = (own_ref[cut:, :] + back_ref[...].astype(jnp.float32)).astype(jnp.bfloat16)
        if not places:
            refs[0][:, :q_lanes] = dq_ref[...]
            return
        for k, out in zip(places, refs):
            rows = partner_rows(me_ref, k, tokens)
            out[:, :q_lanes] = dq_ref[rows, :]
            out[:, q_lanes:] = total[rows, :]

    shapes = [(tokens, total_lanes)] * ways if places else [(group, total_lanes)]
    scratch = [pltpu.VMEM((group, 2 * HD), jnp.bfloat16)] if places else []
    return on_chip(kernel, me, (dq, own, returned), shapes, "settled", scratch, earlier)


def exchanged(blocks, places):
    ways = lax.axis_size("head")
    return [
        lax.ppermute(block, "head", [(i, i ^ k) for i in range(ways)]) if k else block
        for k, block in zip(places, blocks)
    ]


def exchanged_at_once(sent):
    return lax.all_to_all(sent, "head", split_axis=0, concat_axis=0, tiled=True)


def local(queries, keys, values, grad_out, doc_lengths):
    ways = lax.axis_size("head")
    tokens = queries.shape[0]
    group = tokens * ways
    kv_local = keys.shape[1] // (ways * HD)
    per_group = queries.shape[1] // keys.shape[1]
    q_lanes = per_group * HD
    group_first = lax.axis_index("seq") * group
    me = jnp.stack([lax.axis_index("head"), group_first]).astype(jnp.int32)
    places = list(range(ways))

    late = places[ways - ways // 4 :]
    came = exchanged(packed(me, (keys, values), ways, places), places)
    kv, tail = gathered(me, came, places, WINDOW)
    halo = passed_along(tail, "seq", 1)

    parts, returned, grads = [], [], []
    for c in range(kv_local):
        sent = []
        for k, before in zip(places, came):
            earlier = [parts[-1][0]] if parts and k in late else [before] if k else []
            sent += packed(me, (queries, grad_out), ways, [k], c, kv_local, earlier)
        came = exchanged(sent, places)
        qd = gathered(me, came, places, 0)[0]
        if parts:
            dq, own, _ = parts[-1]
            rows = settled(me, dq, own, returned[-1], ways, None, [qd])[0]
            grads.append([exchanged_at_once(rows.reshape(ways, tokens, rows.shape[1]))])
        parts.append(attend(me, doc_lengths, qd, halo, kv, c, kv_local))
        returned.append(passed_along(parts[-1][2], "seq", -1))

    dq, own, _ = parts[-1]
    grads.append(exchanged(settled(me, dq, own, returned[-1], ways, places), places))
    return unpacked(me, grads, places, q_lanes)


def solution(mesh):
    rows = P(("seq", "head"), None)
    return jax.shard_map(
        local,
        mesh=mesh,
        in_specs=(rows, rows, rows, rows, P()),
        out_specs=(rows, rows, rows),
        check_vma=False,
    )
```

```python
import functools
import math

import jax
import jax.numpy as jnp
from jax import lax
from jax.experimental import pallas as pl
from jax.experimental.pallas import tpu as pltpu
from jax.sharding import PartitionSpec as P

HD = 128
WINDOW = 1024
TQ = TK = 256
SCALING = HD ** (-0.5)
EXP2_SCALE = SCALING * math.log2(math.e)
MASKED = -1e30
SPARE = 4 * 1024 * 1024
SMEM = pl.BlockSpec(memory_space=pltpu.SMEM)
VMEM = pl.BlockSpec(memory_space=pltpu.VMEM)


def array_bytes(arrays):
    return sum(math.prod(a.shape) * a.dtype.itemsize for a in arrays)


def passed_along(shard, axis, by):
    count = lax.axis_size(axis)
    pairs = [(i, i + by) for i in range(count) if 0 <= i + by < count]
    return lax.ppermute(shard, axis, pairs)


def dot_nt(a, b):
    return lax.dot_general(a, b, (((1,), (1,)), ((), ())), preferred_element_type=jnp.float32)


def dot_nn(a, b):
    return lax.dot_general(a, b, (((1,), (0,)), ((), ())), preferred_element_type=jnp.float32)


def partner_rows(me_ref, k, tokens):
    return pl.ds(pl.multiple_of((me_ref[0] ^ k) * tokens, tokens), tokens)


def gather_rows(me_ref, blocks, places, out_ref):
    for k, block in zip(places, blocks):
        out_ref[partner_rows(me_ref, k, block.shape[0]), :] = block[...]


def attend_kernel(
    per_group, chunk, kv_local, me_ref, docs_ref, halo_ref, kv_ref, qd_ref,
    dq_ref, own_ref, rim_ref, k_ext, v_ext, k_t, dk_ext, dv_ext, s_buf, dp_buf,
):
    group = qd_ref.shape[0]
    reach = WINDOW // TK
    for ref, at in ((k_ext, chunk * HD), (v_ext, (kv_local + chunk) * HD)):
        ref[:WINDOW, :] = halo_ref[:, at : at + HD]
        ref[WINDOW:, :] = kv_ref[:, at : at + HD]
    dk_ext[...] = jnp.zeros_like(dk_ext)
    dv_ext[...] = jnp.zeros_like(dv_ext)

    def turn(t, carry):
        rows = pl.ds(pl.multiple_of(t * TK, TK), TK)
        k_t[t] = jnp.transpose(k_ext[rows, :].astype(jnp.float32)).astype(jnp.bfloat16)
        return carry

    lax.fori_loop(0, (group + WINDOW) // TK, turn, 0)
    wide = per_group * TQ
    key_iota = lax.broadcasted_iota(jnp.int32, (TK, wide), 0)
    query_iota = lax.broadcasted_iota(jnp.int32, (1, TQ), 1)
    diagonal = jnp.concatenate([query_iota] * per_group, axis=1)

    def q_block(b, low, tiles):
        q_rows = pl.ds(pl.multiple_of(b * TQ, TQ), TQ)
        first = b + reach + 1 - tiles
        q = jnp.concatenate(
            [qd_ref[q_rows, i * HD : (i + 1) * HD] for i in range(per_group)], axis=0
        )
        d_out = jnp.concatenate(
            [qd_ref[q_rows, i * HD : (i + 1) * HD] for i in range(per_group, 2 * per_group)],
            axis=0,
        )
        low = jnp.concatenate([low] * per_group, axis=1) - first * TK
        key_rows = [pl.ds(pl.multiple_of((first + t) * TK, TK), TK) for t in range(tiles)]
        slots = [slice(t * TK, (t + 1) * TK) for t in range(tiles)]

        top = jnp.full((1, wide), MASKED, jnp.float32)
        for t in range(tiles):
            s = dot_nt(k_ext[key_rows[t], :], q)
            allowed = key_iota >= low - t * TK
            if t == tiles - 1:
                allowed = allowed & (key_iota <= diagonal)
            s = jnp.where(allowed, s, MASKED)
            s_buf[slots[t], :] = s
            top = jnp.maximum(top, jnp.max(s, axis=0, keepdims=True))

        total = jnp.zeros((1, wide), jnp.float32)
        dotted = jnp.zeros((1, wide), jnp.float32)
        for t in range(tiles):
            p = jnp.exp2((s_buf[slots[t], :] - top) * EXP2_SCALE)
            dp = dot_nt(v_ext[key_rows[t], :], d_out)
            s_buf[slots[t], :] = p
            dp_buf[slots[t], :] = dp
            total += jnp.sum(p, axis=0, keepdims=True)
            dotted += jnp.sum(p * dp, axis=0, keepdims=True)
        inverse = 1.0 / total
        row_dot = dotted * inverse

        dq_t = jnp.zeros((HD, wide), jnp.float32)
        for t in range(tiles):
            weights = s_buf[slots[t], :] * inverse
            ds = (weights * (dp_buf[slots[t], :] - row_dot)).astype(jnp.bfloat16)
            dv_ext[key_rows[t], :] += dot_nn(weights.astype(jnp.bfloat16), d_out)
            dk_ext[key_rows[t], :] += dot_nn(ds, q)
            dq_t += dot_nn(k_t[first + t], ds)

        dq = jnp.transpose(dq_t * SCALING).astype(jnp.bfloat16)
        for i in range(per_group):
            dq_ref[q_rows, i * HD : (i + 1) * HD] = dq[i * TQ : (i + 1) * TQ, :]

    def first_allowed(position):
        start, end = 0, 0
        for d in range(docs_ref.shape[0]):
            end = end + docs_ref[d]
            start = jnp.where(position >= end, end, start)
        return jnp.maximum(start, position - (WINDOW - 1)) - (me_ref[1] - WINDOW)

    def any_block(b, carry):
        position = me_ref[1] + b * TQ
        tiles = b + reach + 1 - lax.div(first_allowed(position), TK)
        low = first_allowed(position + query_iota)
        for count in range(1, reach + 2):
            pl.when(tiles == count)(functools.partial(q_block, b, low, count))
        return carry

    lax.fori_loop(0, group // TQ, any_block, 0)
    rim_ref[:, :HD] = (dk_ext[:WINDOW, :] * SCALING).astype(jnp.bfloat16)
    rim_ref[:, HD:] = dv_ext[:WINDOW, :].astype(jnp.bfloat16)
    own_ref[:, :HD] = dk_ext[WINDOW:, :] * SCALING
    own_ref[:, HD:] = dv_ext[WINDOW:, :]


def attend(me, docs, qd, halo, own, chunk, kv_local):
    group = own.shape[0]
    per_group = qd.shape[1] // (2 * HD)
    ext = group + WINDOW
    wide = per_group * TQ
    span = WINDOW + TQ

    area = group * (WINDOW + TQ) * per_group
    outs = [
        jax.ShapeDtypeStruct((group, per_group * HD), jnp.bfloat16),
        jax.ShapeDtypeStruct((group, 2 * HD), jnp.float32),
        jax.ShapeDtypeStruct((WINDOW, 2 * HD), jnp.bfloat16),
    ]
    scratch = [
        jax.ShapeDtypeStruct((ext, HD), jnp.bfloat16),
        jax.ShapeDtypeStruct((ext, HD), jnp.bfloat16),
        jax.ShapeDtypeStruct((ext // TK, HD, TK), jnp.bfloat16),
        jax.ShapeDtypeStruct((ext, HD), jnp.float32),
        jax.ShapeDtypeStruct((ext, HD), jnp.float32),
        jax.ShapeDtypeStruct((span, wide), jnp.float32),
        jax.ShapeDtypeStruct((span, wide), jnp.float32),
    ]
    needed = array_bytes([halo, own, qd, *outs, *scratch])
    return pl.pallas_call(
        functools.partial(attend_kernel, per_group, chunk, kv_local),
        out_shape=tuple(outs),
        in_specs=[SMEM, SMEM] + [VMEM] * 3,
        out_specs=(VMEM,) * 3,
        scratch_shapes=[pltpu.VMEM(s.shape, s.dtype) for s in scratch],
        compiler_params=pltpu.CompilerParams(vmem_limit_bytes=needed + SPARE),
        cost_estimate=pl.CostEstimate(
            flops=area * HD * 2 * 5, bytes_accessed=group * HD * 24, transcendentals=area
        ),
        name="attend",
    )(me, docs, halo, own, qd)


def on_chip(kernel, me, arrays, shapes, name, scratch=(), earlier=()):
    outs = tuple(jax.ShapeDtypeStruct(s, jnp.bfloat16) for s in shapes)
    moved = array_bytes([*arrays, *earlier, *outs])

    def body(me_ref, *refs):
        kernel(me_ref, *refs[len(earlier) :])

    return pl.pallas_call(
        body,
        out_shape=outs,
        in_specs=[SMEM] + [VMEM] * (len(earlier) + len(arrays)),
        out_specs=(VMEM,) * len(shapes),
        scratch_shapes=list(scratch),
        compiler_params=pltpu.CompilerParams(vmem_limit_bytes=moved + SPARE),
        cost_estimate=pl.CostEstimate(flops=0, bytes_accessed=moved, transcendentals=0),
        name=name,
    )(me, *earlier, *arrays)


def packed(me, arrays, ways, chunk=0, chunks=1, places=None, earlier=()):
    tokens = arrays[0].shape[0]
    lanes = [a.shape[1] // (ways * chunks) for a in arrays]
    total = sum(lanes)

    def kernel(me_ref, *refs):
        ins, outs = refs[: len(arrays)], refs[len(arrays) :]
        for n in range(ways):
            out = outs[n] if places else outs[0].at[n]
            place = me_ref[0] ^ places[n] if places else n
            first = 0
            for ref, width in zip(ins, lanes):
                at = (place * chunks + chunk) * width
                at = pl.multiple_of(at, width) if places else at
                out[:, first : first + width] = ref[:, pl.ds(at, width)]
                first += width

    shapes = [(tokens, total)] * ways if places else [(ways, tokens, total)]
    return on_chip(kernel, me, arrays, shapes, "packed", earlier=earlier)


def unpacked(me, grads, places, q_lanes):
    chunks, ways = len(grads), len(places)
    tokens = grads[0][0].shape[-2]
    lanes = (q_lanes, HD, HD)
    counts = [len(blocks) for blocks in grads]

    def kernel(me_ref, *refs):
        outs = refs[sum(counts) :]
        for c in range(chunks):
            ins = refs[sum(counts[:c]) : sum(counts[: c + 1])]
            for n in range(ways):
                block = ins[n] if len(ins) > 1 else ins[0].at[n]
                place = me_ref[0] ^ places[n] if len(ins) > 1 else n
                first = 0
                for out, width in zip(outs, lanes):
                    at = (place * chunks + c) * width
                    at = at if isinstance(at, int) else pl.multiple_of(at, width)
                    out[:, pl.ds(at, width)] = block[:, first : first + width]
                    first += width

    shapes = [(tokens, ways * chunks * width) for width in lanes]
    return on_chip(kernel, me, [g for blocks in grads for g in blocks], shapes, "unpacked")


def gathered(me, blocks, places, tail):
    tokens, lanes = blocks[0].shape
    group = len(places) * tokens

    def kernel(me_ref, *refs):
        ins, outs = refs[: len(places)], refs[len(places) :]
        gather_rows(me_ref, ins, places, outs[0])
        if tail:
            outs[1][...] = outs[0][group - tail :, :]

    shapes = [(group, lanes)] + ([(tail, lanes)] if tail else [])
    return on_chip(kernel, me, blocks, shapes, "gathered")


def settled(me, dq, own, returned, ways, places=None):
    group, q_lanes = dq.shape
    tokens = group // ways
    total_lanes = q_lanes + 2 * HD

    def kernel(me_ref, dq_ref, own_ref, back_ref, *refs):
        cut = group - WINDOW
        total = refs[-1] if places else refs[0].at[:, q_lanes:]
        total[:cut, :] = own_ref[:cut, :].astype(jnp.bfloat16)
        total[cut:, :] = (own_ref[cut:, :] + back_ref[...].astype(jnp.float32)).astype(jnp.bfloat16)
        if not places:
            refs[0][:, :q_lanes] = dq_ref[...]
            return
        for k, out in zip(places, refs):
            rows = partner_rows(me_ref, k, tokens)
            out[:, :q_lanes] = dq_ref[rows, :]
            out[:, q_lanes:] = total[rows, :]

    shapes = [(tokens, total_lanes)] * ways if places else [(group, total_lanes)]
    scratch = [pltpu.VMEM((group, 2 * HD), jnp.bfloat16)] if places else []
    return on_chip(kernel, me, (dq, own, returned), shapes, "settled", scratch)


def exchanged(blocks, places):
    ways = lax.axis_size("head")
    return [
        lax.ppermute(block, "head", [(i, i ^ k) for i in range(ways)]) if k else block
        for k, block in zip(places, blocks)
    ]


def exchanged_at_once(sent):
    return lax.all_to_all(sent, "head", split_axis=0, concat_axis=0, tiled=True)


def local(queries, keys, values, grad_out, doc_lengths):
    ways = lax.axis_size("head")
    tokens = queries.shape[0]
    group = tokens * ways
    kv_local = keys.shape[1] // (ways * HD)
    per_group = queries.shape[1] // keys.shape[1]
    q_lanes = per_group * HD
    group_first = lax.axis_index("seq") * group
    me = jnp.stack([lax.axis_index("head"), group_first]).astype(jnp.int32)
    places = list(range(ways))

    came = exchanged(packed(me, (keys, values), ways, places=places), places)
    kv, tail = gathered(me, came, places, WINDOW)
    halo = passed_along(tail, "seq", 1)
    sent = packed(me, (queries, grad_out), ways, 0, kv_local, places, [came[1]])
    qds = list(gathered(me, exchanged(sent, places), places, 0))
    for c in range(1, kv_local):
        sent = packed(me, (queries, grad_out), ways, c, kv_local, None, [qds[-1], halo])[0]
        qds.append(exchanged_at_once(sent).reshape(group, 2 * q_lanes))

    grads = []
    for c, qd in enumerate(qds):
        dq, own, rim = attend(me, doc_lengths, qd, halo, kv, c, kv_local)
        returned = passed_along(rim, "seq", -1)
        if c < kv_local - 1:
            rows = settled(me, dq, own, returned, ways)[0]
            grads.append([exchanged_at_once(rows.reshape(ways, tokens, rows.shape[1]))])
        else:
            grads.append(exchanged(settled(me, dq, own, returned, ways, places), places))
    return unpacked(me, grads, places, q_lanes)


def solution(mesh):
    rows = P(("seq", "head"), None)
    return jax.shard_map(
        local,
        mesh=mesh,
        in_specs=(rows, rows, rows, rows, P()),
        out_specs=(rows, rows, rows),
        check_vma=False,
    )
```

```python
import functools
import math

import jax
import jax.numpy as jnp
from jax import lax
from jax.experimental import pallas as pl
from jax.experimental.pallas import tpu as pltpu
from jax.sharding import PartitionSpec as P

HD = 128
WINDOW = 1024
TQ = TK = 256
SCALING = HD ** (-0.5)
EXP2_SCALE = SCALING * math.log2(math.e)
MASKED = -1e30
SPARE = 4 * 1024 * 1024
SMEM = pl.BlockSpec(memory_space=pltpu.SMEM)
VMEM = pl.BlockSpec(memory_space=pltpu.VMEM)


def array_bytes(arrays):
    return sum(math.prod(a.shape) * a.dtype.itemsize for a in arrays)


def passed_along(shard, axis, by):
    count = lax.axis_size(axis)
    pairs = [(i, i + by) for i in range(count) if 0 <= i + by < count]
    return lax.ppermute(shard, axis, pairs)


def dot_nt(a, b):
    return lax.dot_general(a, b, (((1,), (1,)), ((), ())), preferred_element_type=jnp.float32)


def dot_nn(a, b):
    return lax.dot_general(a, b, (((1,), (0,)), ((), ())), preferred_element_type=jnp.float32)


def partner_rows(me_ref, k, tokens):
    return pl.ds(pl.multiple_of((me_ref[0] ^ k) * tokens, tokens), tokens)


def gather_rows(me_ref, blocks, places, out_ref):
    for k, block in zip(places, blocks):
        out_ref[partner_rows(me_ref, k, block.shape[0]), :] = block[...]


def attend_kernel(
    per_group, chunk, kv_local, me_ref, docs_ref, halo_ref, kv_ref, qd_ref,
    dq_ref, own_ref, rim_ref, k_ext, v_ext, k_t, dk_ext, dv_ext, s_buf, dp_buf,
):
    group = qd_ref.shape[0]
    reach = WINDOW // TK
    for ref, at in ((k_ext, chunk * HD), (v_ext, (kv_local + chunk) * HD)):
        ref[:WINDOW, :] = halo_ref[:, at : at + HD]
        ref[WINDOW:, :] = kv_ref[:, at : at + HD]
    dk_ext[...] = jnp.zeros_like(dk_ext)
    dv_ext[...] = jnp.zeros_like(dv_ext)

    def turn(t, carry):
        rows = pl.ds(pl.multiple_of(t * TK, TK), TK)
        k_t[t] = jnp.transpose(k_ext[rows, :].astype(jnp.float32)).astype(jnp.bfloat16)
        return carry

    lax.fori_loop(0, (group + WINDOW) // TK, turn, 0)
    wide = per_group * TQ
    key_iota = lax.broadcasted_iota(jnp.int32, (TK, wide), 0)
    query_iota = lax.broadcasted_iota(jnp.int32, (1, TQ), 1)
    diagonal = jnp.concatenate([query_iota] * per_group, axis=1)

    def q_block(b, low, tiles):
        q_rows = pl.ds(pl.multiple_of(b * TQ, TQ), TQ)
        first = b + reach + 1 - tiles
        q = jnp.concatenate(
            [qd_ref[q_rows, i * HD : (i + 1) * HD] for i in range(per_group)], axis=0
        )
        d_out = jnp.concatenate(
            [qd_ref[q_rows, i * HD : (i + 1) * HD] for i in range(per_group, 2 * per_group)],
            axis=0,
        )
        low = jnp.concatenate([low] * per_group, axis=1) - first * TK
        key_rows = [pl.ds(pl.multiple_of((first + t) * TK, TK), TK) for t in range(tiles)]
        slots = [slice(t * TK, (t + 1) * TK) for t in range(tiles)]

        top = jnp.full((1, wide), MASKED, jnp.float32)
        for t in range(tiles):
            s = dot_nt(k_ext[key_rows[t], :], q)
            allowed = key_iota >= low - t * TK
            if t == tiles - 1:
                allowed = allowed & (key_iota <= diagonal)
            s = jnp.where(allowed, s, MASKED)
            s_buf[slots[t], :] = s
            top = jnp.maximum(top, jnp.max(s, axis=0, keepdims=True))

        total = jnp.zeros((1, wide), jnp.float32)
        dotted = jnp.zeros((1, wide), jnp.float32)
        for t in range(tiles):
            p = jnp.exp2((s_buf[slots[t], :] - top) * EXP2_SCALE)
            dp = dot_nt(v_ext[key_rows[t], :], d_out)
            s_buf[slots[t], :] = p
            dp_buf[slots[t], :] = dp
            total += jnp.sum(p, axis=0, keepdims=True)
            dotted += jnp.sum(p * dp, axis=0, keepdims=True)
        inverse = 1.0 / total
        row_dot = dotted * inverse

        dq_t = jnp.zeros((HD, wide), jnp.float32)
        for t in range(tiles):
            weights = s_buf[slots[t], :] * inverse
            ds = (weights * (dp_buf[slots[t], :] - row_dot)).astype(jnp.bfloat16)
            dv_ext[key_rows[t], :] += dot_nn(weights.astype(jnp.bfloat16), d_out)
            dk_ext[key_rows[t], :] += dot_nn(ds, q)
            dq_t += dot_nn(k_t[first + t], ds)

        dq = jnp.transpose(dq_t * SCALING).astype(jnp.bfloat16)
        for i in range(per_group):
            dq_ref[q_rows, i * HD : (i + 1) * HD] = dq[i * TQ : (i + 1) * TQ, :]

    def first_allowed(position):
        start, end = 0, 0
        for d in range(docs_ref.shape[0]):
            end = end + docs_ref[d]
            start = jnp.where(position >= end, end, start)
        return jnp.maximum(start, position - (WINDOW - 1)) - (me_ref[1] - WINDOW)

    def any_block(b, carry):
        position = me_ref[1] + b * TQ
        tiles = b + reach + 1 - lax.div(first_allowed(position), TK)
        low = first_allowed(position + query_iota)
        for count in range(1, reach + 2):
            pl.when(tiles == count)(functools.partial(q_block, b, low, count))
        return carry

    lax.fori_loop(0, group // TQ, any_block, 0)
    rim_ref[:, :HD] = (dk_ext[:WINDOW, :] * SCALING).astype(jnp.bfloat16)
    rim_ref[:, HD:] = dv_ext[:WINDOW, :].astype(jnp.bfloat16)
    own_ref[:, :HD] = dk_ext[WINDOW:, :] * SCALING
    own_ref[:, HD:] = dv_ext[WINDOW:, :]


def attend(me, docs, qd, halo, own, chunk, kv_local):
    group = own.shape[0]
    per_group = qd.shape[1] // (2 * HD)
    ext = group + WINDOW
    wide = per_group * TQ
    span = WINDOW + TQ

    area = group * (WINDOW + TQ) * per_group
    outs = [
        jax.ShapeDtypeStruct((group, per_group * HD), jnp.bfloat16),
        jax.ShapeDtypeStruct((group, 2 * HD), jnp.float32),
        jax.ShapeDtypeStruct((WINDOW, 2 * HD), jnp.bfloat16),
    ]
    scratch = [
        jax.ShapeDtypeStruct((ext, HD), jnp.bfloat16),
        jax.ShapeDtypeStruct((ext, HD), jnp.bfloat16),
        jax.ShapeDtypeStruct((ext // TK, HD, TK), jnp.bfloat16),
        jax.ShapeDtypeStruct((ext, HD), jnp.float32),
        jax.ShapeDtypeStruct((ext, HD), jnp.float32),
        jax.ShapeDtypeStruct((span, wide), jnp.float32),
        jax.ShapeDtypeStruct((span, wide), jnp.float32),
    ]
    needed = array_bytes([halo, own, qd, *outs, *scratch])
    return pl.pallas_call(
        functools.partial(attend_kernel, per_group, chunk, kv_local),
        out_shape=tuple(outs),
        in_specs=[SMEM, SMEM] + [VMEM] * 3,
        out_specs=(VMEM,) * 3,
        scratch_shapes=[pltpu.VMEM(s.shape, s.dtype) for s in scratch],
        compiler_params=pltpu.CompilerParams(vmem_limit_bytes=needed + SPARE),
        cost_estimate=pl.CostEstimate(
            flops=area * HD * 2 * 5, bytes_accessed=group * HD * 24, transcendentals=area
        ),
        name="attend",
    )(me, docs, halo, own, qd)


def on_chip(kernel, me, arrays, shapes, name, scratch=(), earlier=()):
    outs = tuple(jax.ShapeDtypeStruct(s, jnp.bfloat16) for s in shapes)
    moved = array_bytes([*arrays, *earlier, *outs])

    def body(me_ref, *refs):
        kernel(me_ref, *refs[len(earlier) :])

    return pl.pallas_call(
        body,
        out_shape=outs,
        in_specs=[SMEM] + [VMEM] * (len(earlier) + len(arrays)),
        out_specs=(VMEM,) * len(shapes),
        scratch_shapes=list(scratch),
        compiler_params=pltpu.CompilerParams(vmem_limit_bytes=moved + SPARE),
        cost_estimate=pl.CostEstimate(flops=0, bytes_accessed=moved, transcendentals=0),
        name=name,
    )(me, *earlier, *arrays)


def packed(me, arrays, ways, chunk=0, chunks=1, places=None, earlier=()):
    tokens = arrays[0].shape[0]
    lanes = [a.shape[1] // (ways * chunks) for a in arrays]
    total = sum(lanes)

    def kernel(me_ref, *refs):
        ins, outs = refs[: len(arrays)], refs[len(arrays) :]
        for n in range(ways):
            out = outs[n] if places else outs[0].at[n]
            place = me_ref[0] ^ places[n] if places else n
            first = 0
            for ref, width in zip(ins, lanes):
                at = (place * chunks + chunk) * width
                at = pl.multiple_of(at, width) if places else at
                out[:, first : first + width] = ref[:, pl.ds(at, width)]
                first += width

    shapes = [(tokens, total)] * ways if places else [(ways, tokens, total)]
    return on_chip(kernel, me, arrays, shapes, "packed", earlier=earlier)


def unpacked(me, grads, places, q_lanes):
    chunks, ways = len(grads), len(places)
    tokens = grads[0][0].shape[-2]
    lanes = (q_lanes, HD, HD)
    counts = [len(blocks) for blocks in grads]

    def kernel(me_ref, *refs):
        outs = refs[sum(counts) :]
        for c in range(chunks):
            ins = refs[sum(counts[:c]) : sum(counts[: c + 1])]
            for n in range(ways):
                block = ins[n] if len(ins) > 1 else ins[0].at[n]
                place = me_ref[0] ^ places[n] if len(ins) > 1 else n
                first = 0
                for out, width in zip(outs, lanes):
                    at = (place * chunks + c) * width
                    at = at if isinstance(at, int) else pl.multiple_of(at, width)
                    out[:, pl.ds(at, width)] = block[:, first : first + width]
                    first += width

    shapes = [(tokens, ways * chunks * width) for width in lanes]
    return on_chip(kernel, me, [g for blocks in grads for g in blocks], shapes, "unpacked")


def gathered(me, blocks, places, tail):
    tokens, lanes = blocks[0].shape
    group = len(places) * tokens

    def kernel(me_ref, *refs):
        ins, outs = refs[: len(places)], refs[len(places) :]
        gather_rows(me_ref, ins, places, outs[0])
        if tail:
            outs[1][...] = outs[0][group - tail :, :]

    shapes = [(group, lanes)] + ([(tail, lanes)] if tail else [])
    return on_chip(kernel, me, blocks, shapes, "gathered")


def settled(me, dq, own, returned, ways, places=None):
    group, q_lanes = dq.shape
    tokens = group // ways
    total_lanes = q_lanes + 2 * HD

    def kernel(me_ref, dq_ref, own_ref, back_ref, *refs):
        cut = group - WINDOW
        total = refs[-1] if places else refs[0].at[:, q_lanes:]
        total[:cut, :] = own_ref[:cut, :].astype(jnp.bfloat16)
        total[cut:, :] = (own_ref[cut:, :] + back_ref[...].astype(jnp.float32)).astype(jnp.bfloat16)
        if not places:
            refs[0][:, :q_lanes] = dq_ref[...]
            return
        for k, out in zip(places, refs):
            rows = partner_rows(me_ref, k, tokens)
            out[:, :q_lanes] = dq_ref[rows, :]
            out[:, q_lanes:] = total[rows, :]

    shapes = [(tokens, total_lanes)] * ways if places else [(group, total_lanes)]
    scratch = [pltpu.VMEM((group, 2 * HD), jnp.bfloat16)] if places else []
    return on_chip(kernel, me, (dq, own, returned), shapes, "settled", scratch)


def exchanged(blocks, places):
    ways = lax.axis_size("head")
    return [
        lax.ppermute(block, "head", [(i, i ^ k) for i in range(ways)]) if k else block
        for k, block in zip(places, blocks)
    ]


def exchanged_at_once(sent):
    return lax.all_to_all(sent, "head", split_axis=0, concat_axis=0, tiled=True)


def local(queries, keys, values, grad_out, doc_lengths):
    ways = lax.axis_size("head")
    tokens = queries.shape[0]
    group = tokens * ways
    kv_local = keys.shape[1] // (ways * HD)
    per_group = queries.shape[1] // keys.shape[1]
    q_lanes = per_group * HD
    group_first = lax.axis_index("seq") * group
    me = jnp.stack([lax.axis_index("head"), group_first]).astype(jnp.int32)
    places = list(range(ways))

    came = exchanged(packed(me, (keys, values), ways, places=places), places)
    kv, tail = gathered(me, came, places, WINDOW)
    halo = passed_along(tail, "seq", 1)
    sent = packed(me, (queries, grad_out), ways, 0, kv_local, places, [came[1]])
    first = exchanged(sent, places)
    qds = list(gathered(me, first, places, 0))
    for c in range(1, kv_local):
        sent = packed(me, (queries, grad_out), ways, c, kv_local, None, [*(first[1:] if c == 1 else qds[-1:]), halo])[0]
        qds.append(exchanged_at_once(sent).reshape(group, 2 * q_lanes))

    grads = []
    for c, qd in enumerate(qds):
        dq, own, rim = attend(me, doc_lengths, qd, halo, kv, c, kv_local)
        returned = passed_along(rim, "seq", -1)
        if c < kv_local - 1:
            rows = settled(me, dq, own, returned, ways)[0]
            grads.append([exchanged_at_once(rows.reshape(ways, tokens, rows.shape[1]))])
        else:
            grads.append(exchanged(settled(me, dq, own, returned, ways, places), places))
    return unpacked(me, grads, places, q_lanes)


def solution(mesh):
    rows = P(("seq", "head"), None)
    return jax.shard_map(
        local,
        mesh=mesh,
        in_specs=(rows, rows, rows, rows, P()),
        out_specs=(rows, rows, rows),
        check_vma=False,
    )
```
